256 devices in a mesh: solver: 2 (over y_lo), gy: 16 (over y_hi, x, core), gz: 8 (over z).
Axes of the slice: x: 4, y: 4 (y_hi: 2, y_lo: 2; y = y_hi * 2 + y_lo), z: 8, core: 2. Of those that a mesh axis runs over, the one named last changes fastest.
Arguments:
- coupled_state: float32 [2, 190, 16, 8, 2048], P('solver', None, 'gy', 'gz'), may hold values from -0.5 to 2.5, as said below
- solid_mask: int32 [5, 16, 8, 2048], P(None, 'gy', 'gz'), may hold values 0 or 1
- inlet_source: int32 [8, 256], P('gz'), may hold values from 0 to 255, as said below
Outputs:
- new_state: float32 [2, 190, 16, 8, 2048], P('solver', None, 'gy', 'gz')
The draws below stay inside these ranges and needn't reach their ends.
Inputs may be any that keep to these rules, and one draw needn't show every extreme that they name: Block 0 of coupled_state is positive. For every k, inlet_source[k] is a permutation of the 256 rows. Within one k, each outlet tile of 16 rows sends 2 rows to exactly one inlet tile, none to exactly one other, and 1 to each of the rest.
All inputs are finite; a program needn't handle non-finite values. No bound on the sum of `solid_mask` on one device may be relied on, other than what follows from the above.
Results may differ from the reference program's by a relative error of at most 0.0003.
Values sent between devices are 32-bit elements; how exact they have to be, the bound alone decides.
A program may use at most 128 MiB of HBM per device.

```python
import math
import jax
import jax.numpy as jnp
from jax import lax

CY = 16
CZ = 128
LX = 5
FX = 38
WORDS = 190
TILE = 2048
NY = 256
NZ = 1024
N_GY = 16
N_GZ = 8


VELOCITY_TABLE = [(0, 0, 0), (1, 0, 0), (-1, 0, 0), (0, 1, 0), (0, -1, 0), (0, 0, 1), (0, 0, -1), (1, 1, 0), (-1, -1, 0), (1, -1, 0), (-1, 1, 0), (1, 0, 1), (-1, 0, -1), (1, 0, -1), (-1, 0, 1), (0, 1, 1), (0, -1, -1), (0, 1, -1), (0, -1, 1)]


def draw_coupled_state(key, part):
    key = jax.random.fold_in(key, 11)
    key_list = jax.random.split(key, 10)
    cell_shape = (LX, N_GY, N_GZ, TILE)
    pipe_shape = (FX, N_GY, N_GZ, TILE)
    first_phase_density = jax.random.uniform(key_list[0], cell_shape, jnp.float32, 0.05, 1.0)
    second_phase_density = jax.random.uniform(key_list[1], cell_shape, jnp.float32, 0.05, 1.0)
    fraction = jax.random.uniform(key_list[2], pipe_shape, jnp.float32, 0.0, 1.0)
    pressure = jax.random.uniform(key_list[3], pipe_shape, jnp.float32, -0.5, 0.5)
    stream_vel = jax.random.uniform(key_list[4], pipe_shape, jnp.float32, 0.2, 0.6)
    vel_x = 0.05 + jax.random.uniform(key_list[5], cell_shape, jnp.float32, -0.05, 0.05)
    vel_y = jax.random.uniform(key_list[6], cell_shape, jnp.float32, -0.05, 0.05)
    vel_z = jax.random.uniform(key_list[7], cell_shape, jnp.float32, -0.05, 0.05)
    col_shape = (19, 1, 1, 1, 1)
    dir_x = jnp.array([float(velocity[0]) for velocity in VELOCITY_TABLE], dtype=jnp.float32).reshape(col_shape)
    dir_y = jnp.array([float(velocity[1]) for velocity in VELOCITY_TABLE], dtype=jnp.float32).reshape(col_shape)
    dir_z = jnp.array([float(velocity[2]) for velocity in VELOCITY_TABLE], dtype=jnp.float32).reshape(col_shape)
    proj_vel = dir_x * vel_x + dir_y * vel_y + dir_z * vel_z
    speed_sq = vel_x * vel_x + vel_y * vel_y + vel_z * vel_z
    shape_factor = 1.0 + 3.0 * proj_vel + 4.5 * proj_vel * proj_vel - 1.5 * speed_sq
    noise = jax.random.uniform(key_list[8], (2, 19) + cell_shape, jnp.float32, -0.2, 0.2)
    nozzle = jnp.stack([first_phase_density, second_phase_density])[:, None] * shape_factor[None] * (1.0 + noise)
    nozzle_words = nozzle.reshape((WORDS,) + cell_shape[1:])
    cross_key = jax.random.split(key_list[9], 2)
    cross_y = jax.random.uniform(cross_key[0], pipe_shape, jnp.float32, -0.2, 0.2)
    cross_z = jax.random.uniform(cross_key[1], pipe_shape, jnp.float32, -0.2, 0.2)
    pipe_words = jnp.stack([fraction, stream_vel, cross_y, cross_z, pressure]).reshape((WORDS,) + pipe_shape[1:])
    return jnp.stack([nozzle_words, pipe_words])


def draw_inlet_source(key, part):
    key = jax.random.fold_in(key, 23)

    def one_column(column_key):
        key_list = jax.random.split(column_key, 3)
        tile_ids = jnp.arange(N_GY, dtype=jnp.int32)
        tile_order = jax.random.permutation(key_list[0], tile_ids)
        half_cap = CY // N_GY
        counts = half_cap + half_cap * (tile_ids[None, :] == tile_order[:, None]).astype(jnp.int32) - half_cap * (tile_ids[None, :] == jnp.roll(tile_order, -1)[:, None]).astype(jnp.int32)
        count_ends = jnp.cumsum(counts, axis=1)
        position = jnp.arange(CY, dtype=jnp.int32)
        source_perm = jax.vmap(lambda sub_key: jax.random.permutation(sub_key, position))(jax.random.split(key_list[1], N_GY))
        dest_tile = jnp.sum((count_ends[:, None, :] <= position[None, :, None]).astype(jnp.int32), axis=2)
        sort_key = dest_tile * NY + tile_ids[:, None] * CY + position[None, :]
        order_rows = jnp.argsort(sort_key.reshape(NY), stable=True)
        source_rows = (tile_ids[:, None] * CY + source_perm).reshape(NY)[order_rows]
        dest_perm = jax.vmap(lambda sub_key: jax.random.permutation(sub_key, position))(jax.random.split(key_list[2], N_GY))
        dest_rows = (tile_ids[:, None] * CY + dest_perm).reshape(NY)
        return jnp.zeros(NY, jnp.int32).at[dest_rows].set(source_rows)
    return jax.vmap(one_column)(jax.random.split(key, N_GZ))


def place_ends(values, rng, least, largest):
    place = [jax.random.randint(jax.random.fold_in(rng, axis), (), 0, length) for axis, length in enumerate(values.shape)]
    longest = values.shape.index(max(values.shape))
    neighbour = place[:longest] + [(place[longest] + 1) % values.shape[longest]] + place[longest + 1:]
    return values.at[tuple(place)].set(least).at[tuple(neighbour)].set(largest)


def setup_inputs(seed: int = 0) -> dict:
    arg_keys = jax.random.split(jax.random.key(seed), 4)
    return {
        "coupled_state": draw_coupled_state(jax.random.fold_in(arg_keys[3], 71), 0),
        "solid_mask": place_ends((jax.random.randint(arg_keys[1], (LX, N_GY, N_GZ, TILE), 0, 5) < 1).astype(jnp.int32), jax.random.fold_in(arg_keys[1], 1), 0, 1),
        "inlet_source": draw_inlet_source(jax.random.fold_in(arg_keys[3], 71), 0),
    }


VELOCITY_TABLE = [(0, 0, 0), (1, 0, 0), (-1, 0, 0), (0, 1, 0), (0, -1, 0), (0, 0, 1), (0, 0, -1), (1, 1, 0), (-1, -1, 0), (1, -1, 0), (-1, 1, 0), (1, 0, 1), (-1, 0, -1), (1, 0, -1), (-1, 0, 1), (0, 1, 1), (0, -1, -1), (0, 1, -1), (0, -1, 1)]
OPPOSITE_TABLE = [0, 2, 1, 4, 3, 6, 5, 8, 7, 10, 9, 12, 11, 14, 13, 16, 15, 18, 17]
WEIGHT_TABLE = [1.0 / 3.0] + [1.0 / 18.0] * 6 + [1.0 / 36.0] * 12
RELAX_TIME = 0.8
SURF_TENSION = 0.02
SEGREGATION_BETA = 0.7
GRAD_FLOOR = 0.1
TIME_STEP = 0.2
VISCOSITY = 0.05
DIFFUSION = 0.05
SOUND_SPEED = 1.0
DENSITY_LOG = math.log(2.0)

def lattice_columns():
    shape_col = (19, 1, 1, 1)
    dir_x = jnp.array([float(velocity[0]) for velocity in VELOCITY_TABLE], dtype=jnp.float32).reshape(shape_col)
    dir_y = jnp.array([float(velocity[1]) for velocity in VELOCITY_TABLE], dtype=jnp.float32).reshape(shape_col)
    dir_z = jnp.array([float(velocity[2]) for velocity in VELOCITY_TABLE], dtype=jnp.float32).reshape(shape_col)
    weights = jnp.array(WEIGHT_TABLE, dtype=jnp.float32).reshape(shape_col)
    return (dir_x, dir_y, dir_z, weights)

def equilibrium(density, vel_x, vel_y, vel_z, lattice):
    dir_x, dir_y, dir_z, weights = lattice
    proj_vel = dir_x * vel_x + dir_y * vel_y + dir_z * vel_z
    speed_sq = vel_x * vel_x + vel_y * vel_y + vel_z * vel_z
    return density * (1.0 + 3.0 * proj_vel + 4.5 * proj_vel * proj_vel - 1.5 * speed_sq)

def colour_masses(pops, lattice):
    weights = lattice[3]
    return (lax.optimization_barrier(jnp.sum(weights * pops[0], axis=0)), lax.optimization_barrier(jnp.sum(weights * pops[1], axis=0)))

def flow_moments(pops, summed_density, lattice):
    dir_x, dir_y, dir_z, weights = lattice
    mixed_pops = pops[0] + pops[1]
    mom_x = lax.optimization_barrier(jnp.sum(weights * dir_x * mixed_pops, axis=0)) / summed_density
    mom_y = lax.optimization_barrier(jnp.sum(weights * dir_y * mixed_pops, axis=0)) / summed_density
    mom_z = lax.optimization_barrier(jnp.sum(weights * dir_z * mixed_pops, axis=0)) / summed_density
    return (mixed_pops, mom_x, mom_y, mom_z)

def nozzle_profile(cell_words, lattice):
    pops = cell_words.reshape((2, 19, -1) + cell_words.shape[1:])
    last_row = pops[:, :, -1:]
    first_phase_density, second_phase_density = colour_masses(last_row, lattice)
    summed_density = first_phase_density + second_phase_density
    mixed_pops, mom_x, mom_y, mom_z = flow_moments(last_row, summed_density, lattice)
    phase_field = (first_phase_density - second_phase_density) / summed_density
    return jnp.stack([mom_x[0], mom_y[0], mom_z[0], phase_field[0]])

def pipe_profile(cell_words):
    fields = cell_words.reshape((5, -1) + cell_words.shape[1:])
    return jnp.stack([fields[4, 0], fields[1, 0], fields[2, 0], fields[3, 0]])

def nozzle_step(pops, inflow, solid_part, lattice):
    dir_x, dir_y, dir_z, weights = lattice
    row_count = pops.shape[2]
    wide = pops.shape[3]
    deep = pops.shape[4]
    last_red, last_blue = colour_masses(pops[:, :, row_count - 1:row_count], lattice)
    phi_last = (last_red - last_blue) / (last_red + last_blue)
    outflow = equilibrium(jnp.exp(inflow[0]), inflow[1], inflow[2], inflow[3], lattice)
    upper_ghost = jnp.stack([0.5 * (1.0 + phi_last) * outflow, 0.5 * (1.0 - phi_last) * outflow])
    lower_ghost = pops[:, :, 0:1]
    extended = jnp.concatenate([lower_ghost, lower_ghost, pops, upper_ghost, upper_ghost], axis=2)
    moved_list = []
    for direction in range(19):
        shift_x, shift_y, shift_z = VELOCITY_TABLE[direction]
        moved_list.append(extended[:, direction, 1 - shift_x:3 - shift_x + row_count, 1 - shift_y:wide - 1 - shift_y, 1 - shift_z:deep - 1 - shift_z])
    read = jnp.stack(moved_list, axis=1)
    red_all, blue_all = colour_masses(read, lattice)
    phase_field = (red_all - blue_all) / (red_all + blue_all)
    grad_x = 0.5 * (phase_field[2:, 1:-1, 1:-1] - phase_field[:-2, 1:-1, 1:-1])
    grad_y = 0.5 * (phase_field[1:-1, 2:, 1:-1] - phase_field[1:-1, :-2, 1:-1])
    grad_z = 0.5 * (phase_field[1:-1, 1:-1, 2:] - phase_field[1:-1, 1:-1, :-2])
    inner_pops = read[:, :, 1:-1, 1:-1, 1:-1]
    first_phase_density = red_all[1:-1, 1:-1, 1:-1]
    second_phase_density = blue_all[1:-1, 1:-1, 1:-1]
    summed_density = first_phase_density + second_phase_density
    mixed_pops, mom_x, mom_y, mom_z = flow_moments(inner_pops, summed_density, lattice)
    balance = equilibrium(summed_density, mom_x, mom_y, mom_z, lattice)
    relaxed = mixed_pops - (mixed_pops - balance) / RELAX_TIME
    grad_sq = grad_x * grad_x + grad_y * grad_y + grad_z * grad_z
    slope_norm = jnp.sqrt(grad_sq + GRAD_FLOOR * GRAD_FLOOR)
    slope_cosine_term = dir_x * grad_x + dir_y * grad_y + dir_z * grad_z
    perturbed_entries = relaxed + SURF_TENSION * (slope_cosine_term * slope_cosine_term - grad_sq / 3.0) / slope_norm
    revised_first_phase = first_phase_density / summed_density * perturbed_entries + SEGREGATION_BETA * (first_phase_density * second_phase_density / summed_density) * slope_cosine_term / slope_norm
    fluid_pops = jnp.stack([revised_first_phase, perturbed_entries - revised_first_phase])
    reversed_pops = jnp.stack([inner_pops[:, opposite] for opposite in OPPOSITE_TABLE], axis=1)
    return solid_part * reversed_pops + (1.0 - solid_part) * fluid_pops

def pipe_segment(fields, inflow, start_state):
    row_count = fields.shape[1]
    inlet_ghost = jnp.stack([0.5 * (1.0 + inflow[3]), inflow[0], inflow[1], inflow[2], fields[4, 0]])[:, None]
    outlet_ghost = fields[:, row_count - 1:row_count]
    extended = jnp.concatenate([inlet_ghost, inlet_ghost, fields, outlet_ghost, outlet_ghost], axis=1)
    wide = extended.shape[2]
    deep = extended.shape[3]

    def window(shift_x, shift_y, shift_z):
        return extended[:, 2 + shift_x:2 + shift_x + row_count, 2 + shift_y:wide - 2 + shift_y, 2 + shift_z:deep - 2 + shift_z]
    centre = window(0, 0, 0)
    deriv_x = (window(-2, 0, 0) - 8.0 * window(-1, 0, 0) + 8.0 * window(1, 0, 0) - window(2, 0, 0)) / 12.0
    deriv_y = (window(0, -2, 0) - 8.0 * window(0, -1, 0) + 8.0 * window(0, 1, 0) - window(0, 2, 0)) / 12.0
    deriv_z = (window(0, 0, -2) - 8.0 * window(0, 0, -1) + 8.0 * window(0, 0, 1) - window(0, 0, 2)) / 12.0
    smooth = window(1, 0, 0) + window(-1, 0, 0) + window(0, 1, 0) + window(0, -1, 0) + window(0, 0, 1) + window(0, 0, -1) - 6.0 * centre
    fraction = centre[0]
    vel_x = centre[1]
    vel_y = centre[2]
    vel_z = centre[3]
    advect = vel_x * deriv_x + vel_y * deriv_y + vel_z * deriv_z
    inv_density = jnp.exp((1.0 - fraction) * DENSITY_LOG)
    rate_all = jnp.stack([-advect[0] + DIFFUSION * smooth[0], -advect[1] - inv_density * deriv_x[4] + VISCOSITY * smooth[1], -advect[2] - inv_density * deriv_y[4] + VISCOSITY * smooth[2], -advect[3] - inv_density * deriv_z[4] + VISCOSITY * smooth[3], -SOUND_SPEED * (deriv_x[1] + deriv_y[2] + deriv_z[3]) + DIFFUSION * smooth[4]])
    moved_state = centre + TIME_STEP * rate_all
    if start_state is None:
        return moved_state
    return 0.5 * (start_state + moved_state)

def to_grid(tiled):
    depth_count = tiled.shape[0]
    return tiled.reshape(depth_count, N_GY, N_GZ, CY, CZ).transpose(0, 1, 3, 2, 4).reshape(depth_count, NY, NZ)

def to_tiles(grid):
    depth_count = grid.shape[0]
    return grid.reshape(depth_count, N_GY, CY, N_GZ, CZ).transpose(0, 1, 3, 2, 4).reshape(depth_count, N_GY, N_GZ, CY * CZ)

def wrap_pad(cells):
    return jnp.pad(cells, ((0, 0), (2, 2), (2, 2)), mode='wrap')

def route_rows(profile, index_map):
    blocks = profile.reshape(4, NY, N_GZ, CZ)
    pick_rows = jnp.broadcast_to(index_map.T[None, :, :, None], blocks.shape)
    return jnp.take_along_axis(blocks, pick_rows, axis=1).reshape(4, NY, NZ)

def by_blocks(step_fn, padded):

    def one_block(block_index):
        offset_rows = (block_index * CY).astype(jnp.int32)
        piece_cells = lax.dynamic_slice_in_dim(padded, offset_rows, CY + 4, 1)
        return step_fn(piece_cells, offset_rows)
    stacked = lax.map(one_block, jnp.arange(N_GY, dtype=jnp.int32))
    return stacked.transpose(1, 0, 2, 3).reshape(stacked.shape[1], NY, NZ)

def reference(coupled_state, solid_mask, inlet_source):
    lattice = lattice_columns()
    nozzle_words = to_grid(coupled_state[0])
    pipe_words = to_grid(coupled_state[1])
    solid_grid = to_grid(solid_mask).astype(jnp.float32)
    nozzle_rows = nozzle_profile(nozzle_words, lattice)
    pipe_rows = pipe_profile(pipe_words)
    row_ids = jnp.arange(NY, dtype=jnp.int32)
    inverse = jax.vmap(lambda column: jnp.zeros(NY, jnp.int32).at[column].set(row_ids))(inlet_source)
    pipe_inflow = route_rows(nozzle_rows, inlet_source)
    nozzle_inflow = route_rows(pipe_rows, inverse)

    def nozzle_piece(piece_cells, offset_rows):
        solid_piece = lax.dynamic_slice_in_dim(solid_grid, offset_rows, CY, 1)
        pops = piece_cells[:WORDS].reshape(2, 19, LX, CY + 4, NZ + 4)
        return nozzle_step(pops, piece_cells[WORDS:], solid_piece, lattice).reshape(WORDS, CY, NZ)
    current = nozzle_words
    for substep in range(2):
        current = by_blocks(nozzle_piece, wrap_pad(jnp.concatenate([current, nozzle_inflow], axis=0)))

    def pipe_first(piece_cells, offset_rows):
        fields = piece_cells[:WORDS].reshape(5, FX, CY + 4, NZ + 4)
        return pipe_segment(fields, piece_cells[WORDS:], None).reshape(WORDS, CY, NZ)

    def pipe_second(piece_cells, offset_rows):
        fields = piece_cells[:WORDS].reshape(5, FX, CY + 4, NZ + 4)
        start_piece = lax.dynamic_slice_in_dim(pipe_words, offset_rows, CY, 1).reshape(5, FX, CY, NZ)
        return pipe_segment(fields, piece_cells[WORDS:], start_piece).reshape(WORDS, CY, NZ)
    pipe_mid = by_blocks(pipe_first, wrap_pad(jnp.concatenate([pipe_words, pipe_inflow], axis=0)))
    pipe_new = by_blocks(pipe_second, wrap_pad(jnp.concatenate([pipe_mid, pipe_inflow], axis=0)))
    return jnp.stack([to_tiles(current), to_tiles(pipe_new)])
```

```python
import math

import jax
import jax.numpy as jnp
from jax import lax
from jax.experimental import pallas as pl
from jax.experimental.pallas import tpu as pltpu
from jax.sharding import PartitionSpec as P

CY = 16
CZ = 128
LX = 5
FX = 38
N_GY = 16
N_GZ = 8
MESH = pl.DeviceIdType.MESH
F32 = jnp.float32

VELOCITY_TABLE = [
    (0, 0, 0),
    (1, 0, 0),
    (-1, 0, 0),
    (0, 1, 0),
    (0, -1, 0),
    (0, 0, 1),
    (0, 0, -1),
    (1, 1, 0),
    (-1, -1, 0),
    (1, -1, 0),
    (-1, 1, 0),
    (1, 0, 1),
    (-1, 0, -1),
    (1, 0, -1),
    (-1, 0, 1),
    (0, 1, 1),
    (0, -1, -1),
    (0, 1, -1),
    (0, -1, 1),
]
OPPOSITE_TABLE = [0, 2, 1, 4, 3, 6, 5, 8, 7, 10, 9, 12, 11, 14, 13, 16, 15, 18, 17]
RELAX_TIME = 0.8
SURF_TENSION = 0.02
SEGREGATION_BETA = 0.7
GRAD_FLOOR = 0.1
TIME_STEP = 0.2
VISCOSITY = 0.05
DIFFUSION = 0.05
DENSITY_LOG = math.log(2.0)

PLUS_Z = [i for i in range(19) if VELOCITY_TABLE[i][2] == 1]
MINUS_Z = [i for i in range(19) if VELOCITY_TABLE[i][2] == -1]
PLUS_Y = [i for i in range(19) if VELOCITY_TABLE[i][1] == 1]
MINUS_Y = [i for i in range(19) if VELOCITY_TABLE[i][1] == -1]

GROUP = 6
N_GROUPS = 7
LAST_ROWS = FX - GROUP * (N_GROUPS - 1)


def weighted_sum(values):
    faces = values[1]
    for i in range(2, 7):
        faces = faces + values[i]
    edges = values[7]
    for i in range(8, 19):
        edges = edges + values[i]
    return values[0] * (1.0 / 3.0) + faces * (1.0 / 18.0) + edges * (1.0 / 36.0)


def weighted_momentum(values, dim):
    faces = None
    edges = None
    for i in range(1, 19):
        sign = VELOCITY_TABLE[i][dim]
        if sign == 0:
            continue
        if i < 7:
            faces = (
                values[i]
                if faces is None
                else (faces + values[i] if sign > 0 else faces - values[i])
            )
        else:
            edges = (
                values[i]
                if edges is None
                else (edges + values[i] if sign > 0 else edges - values[i])
            )
    return faces * (1.0 / 18.0) + edges * (1.0 / 36.0)


def along(direction, vec):
    total = None
    for sign, part in zip(VELOCITY_TABLE[direction], vec):
        if sign == 0:
            continue
        if total is None:
            total = part if sign > 0 else -part
        else:
            total = total + part if sign > 0 else total - part
    return total


def equilibrium_list(density, vec):
    speed_sq = vec[0] * vec[0] + vec[1] * vec[1] + vec[2] * vec[2]
    rest = density * (1.0 - 1.5 * speed_sq)
    out = [rest]
    for i in range(1, 19, 2):
        proj = along(i, vec)
        even = rest + (4.5 * density) * (proj * proj)
        odd = (3.0 * density) * proj
        out += [even + odd, even - odd]
    return out


def kernel(
    pipe_in,
    nozzle_in,
    solid_ref,
    inlet_ref,
    out_ref,
    prof,
    route_out,
    route_in,
    fields_0,
    fields_1,
    zpack,
    zleft,
    zright,
    pops_0,
    pops_1,
    moved,
    masses,
    phase_buf,
    relaxed,
    ghost_eq,
    nz_plus,
    nz_minus,
    nz_left,
    nz_right,
    qz_plus,
    qz_minus,
    qz_left,
    qz_right,
    in_sem,
    route_send,
    route_recv,
    pipe_send,
    pipe_recv,
    face_send,
    face_recv,
    phase_send,
    phase_recv,
):
    solver = lax.axis_index("solver")
    gy = lax.axis_index("gy")
    gz = lax.axis_index("gz")
    other = 1 - solver
    up = lax.rem(gy + 1, N_GY)
    down = lax.rem(gy + N_GY - 1, N_GY)
    right = lax.rem(gz + 1, N_GZ)
    left = lax.rem(gz + N_GZ - 1, N_GZ)
    is_nozzle = solver == 0
    lane = lax.broadcasted_iota(jnp.int32, (CY, CZ), 1)

    def remote(src, dst, send_sem, recv_sem, device):
        return pltpu.make_async_remote_copy(
            src_ref=src,
            dst_ref=dst,
            send_sem=send_sem,
            recv_sem=recv_sem,
            device_id=device,
            device_id_type=MESH,
        )

    pipe_load = pltpu.make_async_copy(pipe_in, fields_0.at[:, 2 : 2 + FX, 8:24, :], in_sem.at[0])
    nozzle_load = pltpu.make_async_copy(nozzle_in, pops_0.at[:, :, 0:LX, 8:24, :], in_sem.at[0])

    @pl.when(is_nozzle)
    def _():
        nozzle_load.start()

    @pl.when(jnp.logical_not(is_nozzle))
    def _():
        pipe_load.start()

    barrier = pltpu.get_barrier_semaphore()
    for device in (
        (solver, up, gz),
        (solver, down, gz),
        (solver, gy, right),
        (solver, gy, left),
        (solver, up, right),
        (solver, up, left),
        (solver, down, right),
        (solver, down, left),
    ):
        pl.semaphore_signal(barrier, inc=1, device_id=device, device_id_type=MESH)

    def greet(tile, carry):
        pl.semaphore_signal(barrier, inc=1, device_id=(other, tile, gz), device_id_type=MESH)
        return carry

    lax.fori_loop(0, N_GY, greet, 0)

    source = inlet_ref[...]
    row_ids = lax.broadcasted_iota(jnp.int32, (1, 256), 1)
    tile_rows = lax.broadcasted_iota(jnp.int32, (N_GY, 256), 0)
    source_tile = lax.shift_right_logical(source, 4)
    target_tile = lax.shift_right_logical(row_ids, 4)
    member = (tile_rows == source_tile).astype(jnp.bfloat16)
    first = lax.broadcasted_iota(jnp.int32, (256, 256), 0)
    second = lax.broadcasted_iota(jnp.int32, (256, 256), 1)
    before = (
        (first < second)
        & (lax.shift_right_logical(first, 4) == lax.shift_right_logical(second, 4))
    ).astype(jnp.bfloat16)
    counts = jnp.dot(member, before, preferred_element_type=F32)
    rank = jnp.sum(counts * member.astype(F32), axis=0, keepdims=True)
    far_tile = jnp.where(is_nozzle, target_tile, source_tile)
    local_row = jnp.where(is_nozzle, source, row_ids)
    mine = (local_row == tile_rows + gy * CY).astype(jnp.bfloat16)
    slot_rows = []
    row_slots = []
    for slot in range(2):
        taken = ((far_tile == tile_rows) & (rank == float(slot))).astype(jnp.bfloat16)
        dims = (((1,), (1,)), ((), ()))
        slot_rows.append(lax.dot_general(taken, mine, dims, preferred_element_type=F32))
        row_slots.append(lax.dot_general(mine, taken, dims, preferred_element_type=F32))

    @pl.when(is_nozzle)
    def _():
        nozzle_load.wait()
        red = [pops_0[0, i, LX - 1, 8:24, :] for i in range(19)]
        blue = [pops_0[1, i, LX - 1, 8:24, :] for i in range(19)]
        red_mass = weighted_sum(red)
        blue_mass = weighted_sum(blue)
        inverse = 1.0 / (red_mass + blue_mass)
        mixed = [r + b for r, b in zip(red, blue)]
        for dim in range(3):
            prof[:, dim * CZ : (dim + 1) * CZ] = weighted_momentum(mixed, dim) * inverse
        prof[:, 3 * CZ :] = (red_mass - blue_mass) * inverse

    @pl.when(jnp.logical_not(is_nozzle))
    def _():
        pipe_load.wait()
        for slot, field in enumerate((4, 1, 2, 3)):
            prof[:, slot * CZ : (slot + 1) * CZ] = fields_0[field, 2, 8:24, :]

    rows = prof[...]
    for slot in range(2):
        picked = jnp.dot(
            slot_rows[slot], rows, precision=lax.Precision.HIGHEST, preferred_element_type=F32
        )
        for part in range(4):
            route_out[:, slot * 4 + part, :] = picked[:, part * CZ : (part + 1) * CZ]

    pl.semaphore_wait(barrier, 8 + N_GY)

    def route(tile):
        return remote(
            route_out.at[tile],
            route_in.at[gy],
            route_send.at[tile],
            route_recv.at[gy],
            (other, tile, gz),
        )

    def send_route(tile, carry):
        route(tile).start()
        return carry

    lax.fori_loop(0, N_GY, send_route, 0)

    def take_inflow():
        def receive(tile, carry):
            remote(
                route_out.at[tile],
                route_in.at[tile],
                route_send.at[tile],
                route_recv.at[tile],
                (other, tile, gz),
            ).wait_recv()
            return carry

        lax.fori_loop(0, N_GY, receive, 0)
        total = None
        for slot in range(2):
            arrived = jnp.concatenate(
                [route_in[:, slot * 4 + part, :] for part in range(4)], axis=1
            )
            term = jnp.dot(
                row_slots[slot],
                arrived,
                precision=lax.Precision.HIGHEST,
                preferred_element_type=F32,
            )
            total = term if total is None else total + term
        return [total[:, part * CZ : (part + 1) * CZ] for part in range(4)]

    @pl.when(jnp.logical_not(is_nozzle))
    def _():
        lane_word = lax.shift_right_logical(lane, 2)
        from_left = (lane & 3) < 2
        masks = (lane >= 126, lane == 127, lane == 0, lane <= 1)

        def group_copies(step, fields, group, count):
            first_row = 2 + GROUP * group
            span = pl.ds(first_row, count)
            send = lambda k: pipe_send.at[step, group, k]
            recv = lambda k: pipe_recv.at[step, group, k]
            return [
                remote(
                    fields.at[:, span, 22:24, :],
                    fields.at[:, span, 6:8, :],
                    send(0),
                    recv(0),
                    (solver, up, gz),
                ),
                remote(
                    fields.at[:, span, 8:10, :],
                    fields.at[:, span, 24:26, :],
                    send(1),
                    recv(1),
                    (solver, down, gz),
                ),
                remote(
                    zpack.at[step, group],
                    zleft.at[step, group],
                    send(2),
                    recv(2),
                    (solver, gy, right),
                ),
                remote(
                    zpack.at[step, group],
                    zright.at[step, group],
                    send(3),
                    recv(3),
                    (solver, gy, left),
                ),
            ]

        def pack_word(packed, value, word):
            return jnp.where(lane_word == word, pltpu.roll(value, (4 * word + 2) % CZ, 1), packed)

        def send_first(group, count):
            packed = jnp.zeros((CY, CZ), F32)
            for row in range(count):
                for field in range(5):
                    value = fields_0[field, 2 + GROUP * group + row, 8:24, :]
                    packed = pack_word(packed, value, 5 * row + field)
            zpack[0, group] = packed
            for copy in group_copies(0, fields_0, group, count):
                copy.start()

        def moved_row(fields, halo, group, row):
            place = 2 + GROUP * group + row
            centre, grad, smooth = [], [], []
            for field in range(5):
                here = fields[field, place, 8:24, :]
                low_x = fields[field, place - 1, 8:24, :]
                high_x = fields[field, place + 1, 8:24, :]
                d_x = (fields[field, place - 2, 8:24, :] - fields[field, place + 2, 8:24, :]) + (
                    8.0 * (high_x - low_x)
                )
                low_y = fields[field, place, 7:23, :]
                high_y = fields[field, place, 9:25, :]
                d_y = (fields[field, place, 6:22, :] - fields[field, place, 10:26, :]) + (
                    8.0 * (high_y - low_y)
                )
                edge = pltpu.roll(halo, (-(4 * (5 * row + field) + 2)) % CZ, 1)
                far_low = pltpu.roll(jnp.where(masks[0], edge, here), 2, 1)
                low_z = pltpu.roll(jnp.where(masks[1], edge, here), 1, 1)
                high_z = pltpu.roll(jnp.where(masks[2], edge, here), CZ - 1, 1)
                far_high = pltpu.roll(jnp.where(masks[3], edge, here), CZ - 2, 1)
                d_z = (far_low - far_high) + 8.0 * (high_z - low_z)
                centre.append(here)
                grad.append((d_x, d_y, d_z))
                smooth.append(low_x + high_x + low_y + high_y + low_z + high_z)
            scale = TIME_STEP / 12.0
            speed = [scale * centre[k] for k in (1, 2, 3)]
            lift = scale * jnp.exp((1.0 - centre[0]) * DENSITY_LOG)
            spread = TIME_STEP * DIFFUSION
            out = []
            for field in range(4):
                rate = (
                    speed[0] * grad[field][0]
                    + speed[1] * grad[field][1]
                    + speed[2] * grad[field][2]
                )
                if field > 0:
                    rate = rate + lift * grad[4][field - 1]
                out.append((1.0 - 6.0 * spread) * centre[field] + spread * smooth[field] - rate)
            rate = scale * (grad[1][0] + grad[2][1] + grad[3][2])
            out.append((1.0 - 6.0 * spread) * centre[4] + spread * smooth[4] - rate)
            return out

        def run_group(step, fields, group, count):
            for copy in group_copies(step, fields, group, count):
                copy.wait_recv()
            halo = jnp.where(from_left, zleft[step, group], zright[step, group])
            packed = jnp.zeros((CY, CZ), F32)
            for row in range(count):
                values = moved_row(fields, halo, group, row)
                place = GROUP * group + row
                for field in range(5):
                    if step == 0:
                        fields_1[field, 2 + place, 8:24, :] = values[field]
                        packed = pack_word(packed, values[field], 5 * row + field)
                    else:
                        out_ref[field * FX + place] = 0.5 * (
                            fields_0[field, 2 + place, 8:24, :] + values[field]
                        )
            if step == 0:
                zpack[1, group] = packed
                for copy in group_copies(1, fields_1, group, count):
                    copy.start()

        def outlet_ghost(fields):
            for field in range(5):
                end = fields[field, 1 + FX, 8:24, :]
                fields[field, 2 + FX, 8:24, :] = end
                fields[field, 3 + FX, 8:24, :] = end

        send_first(N_GROUPS - 1, LAST_ROWS)

        def send_step(k, carry):
            send_first(N_GROUPS - 2 - k, GROUP)
            return carry

        lax.fori_loop(0, N_GROUPS - 1, send_step, 0)
        outlet_ghost(fields_0)
        run_group(0, fields_0, N_GROUPS - 1, LAST_ROWS)
        outlet_ghost(fields_1)

        def first_step(k, carry):
            group = N_GROUPS - 2 - k

            @pl.when(group == 0)
            def _():
                inflow = take_inflow()
                ghost = [0.5 * (1.0 + inflow[3]), inflow[0], inflow[1], inflow[2]]
                for place in range(2):
                    for field in range(4):
                        fields_0[field, place, 8:24, :] = ghost[field]
                        fields_1[field, place, 8:24, :] = ghost[field]
                    fields_0[4, place, 8:24, :] = fields_0[4, 2, 8:24, :]

            run_group(0, fields_0, group, GROUP)
            return carry

        lax.fori_loop(0, N_GROUPS - 1, first_step, 0)
        for place in range(2):
            fields_1[4, place, 8:24, :] = fields_1[4, 2, 8:24, :]
        run_group(1, fields_1, N_GROUPS - 1, LAST_ROWS)

        def second_step(k, carry):
            run_group(1, fields_1, N_GROUPS - 2 - k, GROUP)
            return carry

        lax.fori_loop(0, N_GROUPS - 1, second_step, 0)

        def finish(step, fields, group, count):
            for copy in group_copies(step, fields, group, count):
                copy.wait_send()

        for step, fields in ((0, fields_0), (1, fields_1)):
            finish(step, fields, N_GROUPS - 1, LAST_ROWS)

            def finish_step(k, carry, step=step, fields=fields):
                finish(step, fields, k, GROUP)
                return carry

            lax.fori_loop(0, N_GROUPS - 1, finish_step, 0)

    @pl.when(is_nozzle)
    def _():
        inflow = take_inflow()
        outflow = equilibrium_list(jnp.exp(inflow[0]), inflow[1:])
        for i in range(19):
            ghost_eq[i] = 0.5 * outflow[i]

        def face_copies(step, pops):
            k = 0
            copies = []

            def add(src, dst, device):
                index = len(copies)
                copies.append(
                    remote(src, dst, face_send.at[step, index], face_recv.at[step, index], device)
                )

            add(nz_plus.at[step], nz_left.at[step, 8:24, :], (solver, gy, right))
            add(nz_minus.at[step], nz_right.at[step, 8:24, :], (solver, gy, left))
            add(nz_plus.at[step, 8:16, :], nz_left.at[step, 0:8, :], (solver, up, right))
            add(nz_plus.at[step, 0:8, :], nz_left.at[step, 24:32, :], (solver, down, right))
            add(nz_minus.at[step, 8:16, :], nz_right.at[step, 0:8, :], (solver, up, left))
            add(nz_minus.at[step, 0:8, :], nz_right.at[step, 24:32, :], (solver, down, left))
            for i in PLUS_Y:
                add(pops.at[:, i, :, 23:24, :], pops.at[:, i, :, 7:8, :], (solver, up, gz))
            for i in MINUS_Y:
                add(pops.at[:, i, :, 8:9, :], pops.at[:, i, :, 24:25, :], (solver, down, gz))
            return copies

        def phase_copies(step):
            send = lambda k: phase_send.at[step, k]
            recv = lambda k: phase_recv.at[step, k]
            grid = phase_buf.at[step]
            return [
                remote(
                    grid.at[1:6, 23:24, :], grid.at[1:6, 7:8, :], send(0), recv(0), (solver, up, gz)
                ),
                remote(
                    grid.at[1:6, 8:9, :],
                    grid.at[1:6, 24:25, :],
                    send(1),
                    recv(1),
                    (solver, down, gz),
                ),
                remote(
                    qz_plus.at[step], qz_left.at[step], send(2), recv(2), (solver, gy, right)
                ),
                remote(
                    qz_minus.at[step], qz_right.at[step], send(3), recv(3), (solver, gy, left)
                ),
            ]

        def word_of(directions, i, colour, row):
            return (directions.index(i) * 2 + colour) * 6 + row

        def run_step(step, pops):
            red_last = weighted_sum([pops[0, i, LX - 1, 8:24, :] for i in range(19)])
            blue_last = weighted_sum([pops[1, i, LX - 1, 8:24, :] for i in range(19)])
            phase_last = (red_last - blue_last) / (red_last + blue_last)
            for i in range(19):
                pops[0, i, LX, 8:24, :] = (1.0 + phase_last) * ghost_eq[i]
                pops[1, i, LX, 8:24, :] = (1.0 - phase_last) * ghost_eq[i]
            packed_plus = jnp.zeros((CY, CZ), F32)
            packed_minus = jnp.zeros((CY, CZ), F32)
            for colour in range(2):
                for row in range(LX + 1):
                    for i in PLUS_Z:
                        word = word_of(PLUS_Z, i, colour, row)
                        value = pltpu.roll(pops[colour, i, row, 8:24, :], word + 1, 1)
                        packed_plus = jnp.where(lane == word, value, packed_plus)
                    for i in MINUS_Z:
                        word = word_of(MINUS_Z, i, colour, row)
                        value = pops[colour, i, row, 8:24, :]
                        if word:
                            value = pltpu.roll(value, word, 1)
                        packed_minus = jnp.where(lane == word, value, packed_minus)
            nz_plus[step] = packed_plus
            nz_minus[step] = packed_minus
            copies = face_copies(step, pops)
            for copy in copies:
                copy.start()
            for copy in copies:
                copy.wait_recv()
            for colour in range(2):
                for i in range(19):
                    shift_y, shift_z = VELOCITY_TABLE[i][1:]
                    span = slice(8 - shift_y, 24 - shift_y)
                    for row in range(LX + 1):
                        value = pops[colour, i, row, span, :]
                        if shift_z == 1:
                            word = word_of(PLUS_Z, i, colour, row)
                            edge = nz_left[step, span, :]
                            if word:
                                edge = pltpu.roll(edge, CZ - word, 1)
                            value = jnp.where(lane == 0, edge, pltpu.roll(value, 1, 1))
                        elif shift_z == -1:
                            word = word_of(MINUS_Z, i, colour, row)
                            edge = pltpu.roll(nz_right[step, span, :], CZ - 1 - word, 1)
                            value = jnp.where(lane == CZ - 1, edge, pltpu.roll(value, CZ - 1, 1))
                        moved[colour, i, row] = value

            def read(colour, i, x):
                shift_x = VELOCITY_TABLE[i][0]
                return moved[colour, i, jnp.clip(x - shift_x, 0, LX)]

            def mass_step(k, carry):
                red = weighted_sum([read(0, i, k - 1) for i in range(19)])
                blue = weighted_sum([read(1, i, k - 1) for i in range(19)])
                masses[0, k] = red
                masses[1, k] = blue
                phase_buf[step, k, 8:24, :] = (red - blue) / (red + blue)
                return carry

            lax.fori_loop(0, LX + 2, mass_step, 0)
            packed_plus = jnp.zeros((CY, CZ), F32)
            packed_minus = jnp.zeros((CY, CZ), F32)
            for x in range(LX):
                value = phase_buf[step, x + 1, 8:24, :]
                packed_plus = jnp.where(lane == x, pltpu.roll(value, x + 1, 1), packed_plus)
                packed_minus = jnp.where(
                    lane == x, pltpu.roll(value, x, 1) if x else value, packed_minus
                )
            qz_plus[step] = packed_plus
            qz_minus[step] = packed_minus
            phases = phase_copies(step)
            for copy in phases:
                copy.start()

            def relax_step(x, carry):
                mixed = [read(0, i, x) + read(1, i, x) for i in range(19)]
                total = masses[0, x + 1] + masses[1, x + 1]
                inverse = 1.0 / total
                vec = [weighted_momentum(mixed, dim) * inverse for dim in range(3)]
                balance = equilibrium_list(total, vec)
                for i in range(19):
                    relaxed[x, i] = mixed[i] - (mixed[i] - balance[i]) * (1.0 / RELAX_TIME)
                return carry

            lax.fori_loop(0, LX, relax_step, 0)
            for copy in phases:
                copy.wait_recv()

            def colour_step(x, carry):
                here = phase_buf[step, x + 1, 8:24, :]
                edge_low = pltpu.roll(qz_left[step], CZ - x, 1)
                edge_high = pltpu.roll(qz_right[step], CZ - 1 - x, 1)
                low_z = jnp.where(lane == 0, edge_low, pltpu.roll(here, 1, 1))
                high_z = jnp.where(lane == CZ - 1, edge_high, pltpu.roll(here, CZ - 1, 1))
                grad = [
                    0.5 * (phase_buf[step, x + 2, 8:24, :] - phase_buf[step, x, 8:24, :]),
                    0.5 * (phase_buf[step, x + 1, 9:25, :] - phase_buf[step, x + 1, 7:23, :]),
                    0.5 * (high_z - low_z),
                ]
                grad_sq = grad[0] * grad[0] + grad[1] * grad[1] + grad[2] * grad[2]
                inverse_norm = 1.0 / jnp.sqrt(grad_sq + GRAD_FLOOR * GRAD_FLOOR)
                red = masses[0, x + 1]
                blue = masses[1, x + 1]
                red_part = red / (red + blue)
                tension = SURF_TENSION * inverse_norm
                level = tension * grad_sq * (1.0 / 3.0)
                split = SEGREGATION_BETA * (red_part * blue) * inverse_norm
                solid = solid_ref[x] != 0
                for i in range(19):
                    value = relaxed[x, i] - level
                    if i:
                        slope = along(i, grad)
                        value = value + tension * (slope * slope)
                        red_value = red_part * value + split * slope
                    else:
                        red_value = red_part * value
                    back = OPPOSITE_TABLE[i]
                    red_new = jnp.where(solid, read(0, back, x), red_value)
                    blue_new = jnp.where(solid, read(1, back, x), value - red_value)
                    if step == 0:
                        pops_1[0, i, x, 8:24, :] = red_new
                        pops_1[1, i, x, 8:24, :] = blue_new
                    else:
                        out_ref[i * LX + x] = red_new
                        out_ref[(19 + i) * LX + x] = blue_new
                return carry

            lax.fori_loop(0, LX, colour_step, 0)
            return copies + phases

        pending = run_step(0, pops_0) + run_step(1, pops_1)
        for copy in pending:
            copy.wait_send()

    def finish_route(tile, carry):
        route(tile).wait_send()
        return carry

    lax.fori_loop(0, N_GY, finish_route, 0)


def on_device(coupled_state, solid_mask, inlet_source):
    words = coupled_state.shape[1]
    vmem = lambda *shape: pltpu.VMEM(shape, F32)
    dma = lambda *shape: pltpu.SemaphoreType.DMA(shape)
    out = pl.pallas_call(
        kernel,
        out_shape=jax.ShapeDtypeStruct((words, CY, CZ), F32),
        in_specs=[
            pl.BlockSpec(memory_space=pl.ANY),
            pl.BlockSpec(memory_space=pl.ANY),
            pl.BlockSpec(memory_space=pltpu.VMEM),
            pl.BlockSpec(memory_space=pltpu.VMEM),
        ],
        out_specs=pl.BlockSpec(memory_space=pltpu.VMEM),
        scratch_shapes=[
            vmem(CY, 4 * CZ),
            vmem(N_GY, 8, CZ),
            vmem(N_GY, 8, CZ),
            vmem(5, FX + 4, 32, CZ),
            vmem(5, FX + 4, 32, CZ),
            vmem(2, N_GROUPS, CY, CZ),
            vmem(2, N_GROUPS, CY, CZ),
            vmem(2, N_GROUPS, CY, CZ),
            vmem(2, 19, LX + 1, 32, CZ),
            vmem(2, 19, LX + 1, 32, CZ),
            vmem(2, 19, LX + 1, CY, CZ),
            vmem(2, LX + 2, CY, CZ),
            vmem(2, LX + 2, 32, CZ),
            vmem(LX, 19, CY, CZ),
            vmem(19, CY, CZ),
            vmem(2, CY, CZ),
            vmem(2, CY, CZ),
            vmem(2, 32, CZ),
            vmem(2, 32, CZ),
            vmem(2, CY, CZ),
            vmem(2, CY, CZ),
            vmem(2, CY, CZ),
            vmem(2, CY, CZ),
            dma(1),
            dma(N_GY),
            dma(N_GY),
            dma(2, N_GROUPS, 4),
            dma(2, N_GROUPS, 4),
            dma(2, 16),
            dma(2, 16),
            dma(2, 4),
            dma(2, 4),
        ],
        compiler_params=pltpu.CompilerParams(
            collective_id=0, has_side_effects=True, vmem_limit_bytes=40 << 20
        ),
    )(
        coupled_state.reshape(5, FX, CY, CZ),
        coupled_state.reshape(2, 19, LX, CY, CZ),
        solid_mask.reshape(LX, CY, CZ),
        inlet_source,
    )
    return out.reshape(coupled_state.shape)


def solution(mesh):
    return jax.shard_map(
        on_device,
        mesh=mesh,
        in_specs=(P("solver", None, "gy", "gz", None), P(None, "gy", "gz", None), P("gz", None)),
        out_specs=P("solver", None, "gy", "gz", None),
        check_vma=False,
    )
```

```python
import math

import jax
import jax.numpy as jnp
from jax import lax
from jax.experimental import pallas as pl
from jax.experimental.pallas import tpu as pltpu
from jax.sharding import PartitionSpec as P

CY = 16
CZ = 128
LX = 5
FX = 38
N_GY = 16
N_GZ = 8
MESH = pl.DeviceIdType.MESH
F32 = jnp.float32

VELOCITY_TABLE = [
    (0, 0, 0),
    (1, 0, 0),
    (-1, 0, 0),
    (0, 1, 0),
    (0, -1, 0),
    (0, 0, 1),
    (0, 0, -1),
    (1, 1, 0),
    (-1, -1, 0),
    (1, -1, 0),
    (-1, 1, 0),
    (1, 0, 1),
    (-1, 0, -1),
    (1, 0, -1),
    (-1, 0, 1),
    (0, 1, 1),
    (0, -1, -1),
    (0, 1, -1),
    (0, -1, 1),
]
OPPOSITE_TABLE = [0, 2, 1, 4, 3, 6, 5, 8, 7, 10, 9, 12, 11, 14, 13, 16, 15, 18, 17]
RELAX_TIME = 0.8
SURF_TENSION = 0.02
SEGREGATION_BETA = 0.7
GRAD_FLOOR = 0.1
TIME_STEP = 0.2
VISCOSITY = 0.05
DIFFUSION = 0.05
DENSITY_LOG = math.log(2.0)

PLUS_Z = [i for i in range(19) if VELOCITY_TABLE[i][2] == 1]
MINUS_Z = [i for i in range(19) if VELOCITY_TABLE[i][2] == -1]
PLUS_Y = [i for i in range(19) if VELOCITY_TABLE[i][1] == 1]
MINUS_Y = [i for i in range(19) if VELOCITY_TABLE[i][1] == -1]

GROUP = 6
N_GROUPS = 7
LAST_ROWS = FX - GROUP * (N_GROUPS - 1)


def weighted_sum(values):
    faces = values[1]
    for i in range(2, 7):
        faces = faces + values[i]
    edges = values[7]
    for i in range(8, 19):
        edges = edges + values[i]
    return values[0] * (1.0 / 3.0) + faces * (1.0 / 18.0) + edges * (1.0 / 36.0)


def weighted_momentum(values, dim):
    faces = None
    edges = None
    for i in range(1, 19):
        sign = VELOCITY_TABLE[i][dim]
        if sign == 0:
            continue
        if i < 7:
            faces = (
                values[i]
                if faces is None
                else (faces + values[i] if sign > 0 else faces - values[i])
            )
        else:
            edges = (
                values[i]
                if edges is None
                else (edges + values[i] if sign > 0 else edges - values[i])
            )
    return faces * (1.0 / 18.0) + edges * (1.0 / 36.0)


def along(direction, vec):
    total = None
    for sign, part in zip(VELOCITY_TABLE[direction], vec):
        if sign == 0:
            continue
        if total is None:
            total = part if sign > 0 else -part
        else:
            total = total + part if sign > 0 else total - part
    return total


def equilibrium_list(density, vec):
    speed_sq = vec[0] * vec[0] + vec[1] * vec[1] + vec[2] * vec[2]
    rest = density * (1.0 - 1.5 * speed_sq)
    out = [rest]
    for i in range(1, 19, 2):
        proj = along(i, vec)
        even = rest + (4.5 * density) * (proj * proj)
        odd = (3.0 * density) * proj
        out += [even + odd, even - odd]
    return out


def kernel(
    pipe_in,
    nozzle_in,
    solid_in,
    inlet_in,
    out_ref,
    solid_ref,
    inlet_ref,
    band,
    prof,
    route_out,
    route_in,
    fields_0,
    fields_1,
    zpack,
    zleft,
    zright,
    pops_0,
    pops_1,
    moved,
    masses,
    phase_buf,
    relaxed,
    ghost_eq,
    nz_plus,
    nz_minus,
    nz_left,
    nz_right,
    qz_plus,
    qz_minus,
    qz_left,
    qz_right,
    in_sem,
    route_send,
    route_recv,
    pipe_send,
    pipe_recv,
    face_send,
    face_recv,
    phase_send,
    phase_recv,
):
    solver = lax.axis_index("solver")
    gy = lax.axis_index("gy")
    gz = lax.axis_index("gz")
    other = 1 - solver
    up = lax.rem(gy + 1, N_GY)
    down = lax.rem(gy + N_GY - 1, N_GY)
    right = lax.rem(gz + 1, N_GZ)
    left = lax.rem(gz + N_GZ - 1, N_GZ)
    is_nozzle = solver == 0
    lane = lax.broadcasted_iota(jnp.int32, (CY, CZ), 1)

    def remote(src, dst, send_sem, recv_sem, device):
        return pltpu.make_async_remote_copy(
            src_ref=src,
            dst_ref=dst,
            send_sem=send_sem,
            recv_sem=recv_sem,
            device_id=device,
            device_id_type=MESH,
        )

    inlet_load = pltpu.make_async_copy(inlet_in, inlet_ref, in_sem.at[1])
    solid_load = pltpu.make_async_copy(solid_in, solid_ref, in_sem.at[2])
    inlet_load.start()
    lane_word = lax.shift_right_logical(lane, 2)

    def pack_word(packed, value, word):
        return jnp.where(lane_word == word, pltpu.roll(value, (4 * word + 2) % CZ, 1), packed)

    def pack_first(group, count):
        packed = jnp.zeros((CY, CZ), F32)
        for row in range(count):
            for field in range(5):
                value = fields_0[field, 2 + GROUP * group + row, 8:24, :]
                packed = pack_word(packed, value, 5 * row + field)
        zpack[0, group] = packed

    def outlet_ghost(fields):
        for field in range(5):
            end = fields[field, 1 + FX, 8:24, :]
            fields[field, 2 + FX, 8:24, :] = end
            fields[field, 3 + FX, 8:24, :] = end

    pipe_load = pltpu.make_async_copy(pipe_in, fields_0.at[:, 2 : 2 + FX, 8:24, :], in_sem.at[0])
    nozzle_load = pltpu.make_async_copy(nozzle_in, pops_0.at[:, :, 0:LX, 8:24, :], in_sem.at[0])

    @pl.when(is_nozzle)
    def _():
        nozzle_load.start()
        solid_load.start()

    @pl.when(jnp.logical_not(is_nozzle))
    def _():
        pipe_load.start()

    barrier = pltpu.get_barrier_semaphore()
    for device in (
        (solver, up, gz),
        (solver, down, gz),
        (solver, gy, right),
        (solver, gy, left),
        (solver, up, right),
        (solver, up, left),
        (solver, down, right),
        (solver, down, left),
    ):
        pl.semaphore_signal(barrier, inc=1, device_id=device, device_id_type=MESH)

    def greet(tile, carry):
        pl.semaphore_signal(barrier, inc=1, device_id=(other, tile, gz), device_id_type=MESH)
        return carry

    lax.fori_loop(0, N_GY, greet, 0)

    inlet_load.wait()
    source = inlet_ref[...]
    row_ids = lax.broadcasted_iota(jnp.int32, (1, 256), 1)
    tile_rows = lax.broadcasted_iota(jnp.int32, (N_GY, 256), 0)
    source_tile = lax.shift_right_logical(source, 4)
    target_tile = lax.shift_right_logical(row_ids, 4)
    member = (tile_rows == source_tile).astype(jnp.bfloat16)
    first = lax.broadcasted_iota(jnp.int32, (256, 256), 0)
    second = lax.broadcasted_iota(jnp.int32, (256, 256), 1)
    before = (
        (first < second)
        & (lax.shift_right_logical(first, 4) == lax.shift_right_logical(second, 4))
    ).astype(jnp.bfloat16)
    counts = jnp.dot(member, before, preferred_element_type=F32)
    rank = jnp.sum(counts * member.astype(F32), axis=0, keepdims=True)
    far_tile = jnp.where(is_nozzle, target_tile, source_tile)
    local_row = jnp.where(is_nozzle, source, row_ids)
    mine = (local_row == tile_rows + gy * CY).astype(jnp.bfloat16)
    slot_rows = []
    row_slots = []
    for slot in range(2):
        taken = ((far_tile == tile_rows) & (rank == float(slot))).astype(jnp.bfloat16)
        dims = (((1,), (1,)), ((), ()))
        slot_rows.append(lax.dot_general(taken, mine, dims, preferred_element_type=F32))
        row_slots.append(lax.dot_general(mine, taken, dims, preferred_element_type=F32))

    @pl.when(is_nozzle)
    def _():
        nozzle_load.wait()
        solid_load.wait()
        red = [pops_0[0, i, LX - 1, 8:24, :] for i in range(19)]
        blue = [pops_0[1, i, LX - 1, 8:24, :] for i in range(19)]
        red_mass = weighted_sum(red)
        blue_mass = weighted_sum(blue)
        inverse = 1.0 / (red_mass + blue_mass)
        mixed = [r + b for r, b in zip(red, blue)]
        for dim in range(3):
            prof[:, dim * CZ : (dim + 1) * CZ] = weighted_momentum(mixed, dim) * inverse
        prof[:, 3 * CZ :] = (red_mass - blue_mass) * inverse

    @pl.when(jnp.logical_not(is_nozzle))
    def _():
        pipe_load.wait()
        for slot, field in enumerate((4, 1, 2, 3)):
            prof[:, slot * CZ : (slot + 1) * CZ] = fields_0[field, 2, 8:24, :]
        lane_in = lax.broadcasted_iota(jnp.int32, (CZ, CZ), 0)
        lane_out = lax.broadcasted_iota(jnp.int32, (CZ, CZ), 1)
        ahead = lane_in - lane_out
        wrapped = jnp.where(
            ahead > 64, ahead - CZ, jnp.where(ahead < -64, ahead + CZ, jnp.zeros_like(ahead))
        )
        for part, apart in enumerate((ahead, wrapped)):
            near = (jnp.abs(apart) == 1).astype(F32)
            far = (jnp.abs(apart) == 2).astype(F32)
            slope = jnp.where(apart > 0, 8.0 * near - far, far - 8.0 * near)
            for copy in range(2):
                rows = slice((2 * part + copy) * CZ, (2 * part + copy + 1) * CZ)
                band[rows, 0:CZ] = slope.astype(jnp.bfloat16)
                band[rows, CZ:] = near.astype(jnp.bfloat16)

        def pack_step(k, carry):
            pack_first(k, GROUP)
            return carry

        lax.fori_loop(0, N_GROUPS - 1, pack_step, 0)
        pack_first(N_GROUPS - 1, LAST_ROWS)
        outlet_ghost(fields_0)

    rows = prof[...]
    for slot in range(2):
        picked = jnp.dot(
            slot_rows[slot], rows, precision=lax.Precision.HIGHEST, preferred_element_type=F32
        )
        for part in range(4):
            route_out[:, slot * 4 + part, :] = picked[:, part * CZ : (part + 1) * CZ]

    pl.semaphore_wait(barrier, 8 + N_GY)

    def route(tile):
        return remote(
            route_out.at[tile],
            route_in.at[gy],
            route_send.at[tile],
            route_recv.at[gy],
            (other, tile, gz),
        )

    def send_route(tile, carry):
        route(tile).start()
        return carry

    lax.fori_loop(0, N_GY, send_route, 0)

    def take_inflow():
        def receive(tile, carry):
            remote(
                route_out.at[tile],
                route_in.at[tile],
                route_send.at[tile],
                route_recv.at[tile],
                (other, tile, gz),
            ).wait_recv()
            return carry

        lax.fori_loop(0, N_GY, receive, 0)
        total = None
        for slot in range(2):
            arrived = jnp.concatenate(
                [route_in[:, slot * 4 + part, :] for part in range(4)], axis=1
            )
            term = jnp.dot(
                row_slots[slot],
                arrived,
                precision=lax.Precision.HIGHEST,
                preferred_element_type=F32,
            )
            total = term if total is None else total + term
        return [total[:, part * CZ : (part + 1) * CZ] for part in range(4)]

    @pl.when(jnp.logical_not(is_nozzle))
    def _():
        from_left = (lane & 3) < 2

        def group_copies(step, fields, group, count):
            first_row = 2 + GROUP * group
            span = pl.ds(first_row, count)
            send = lambda k: pipe_send.at[step, group, k]
            recv = lambda k: pipe_recv.at[step, group, k]
            return [
                remote(
                    fields.at[:, span, 22:24, :],
                    fields.at[:, span, 6:8, :],
                    send(0),
                    recv(0),
                    (solver, up, gz),
                ),
                remote(
                    fields.at[:, span, 8:10, :],
                    fields.at[:, span, 24:26, :],
                    send(1),
                    recv(1),
                    (solver, down, gz),
                ),
                remote(
                    zpack.at[step, group],
                    zleft.at[step, group],
                    send(2),
                    recv(2),
                    (solver, gy, right),
                ),
                remote(
                    zpack.at[step, group],
                    zright.at[step, group],
                    send(3),
                    recv(3),
                    (solver, gy, left),
                ),
            ]

        def send_first(group, count):
            for copy in group_copies(0, fields_0, group, count):
                copy.start()

        def split(value):
            high = value.astype(jnp.bfloat16)
            return [high, (value - high.astype(F32)).astype(jnp.bfloat16)]

        def moved_row(fields, along_z, place):
            centre, grad, smooth = [], [], []
            for field in range(5):
                low_x = fields[field, place - 1, 8:24, :]
                high_x = fields[field, place + 1, 8:24, :]
                d_x = (fields[field, place - 2, 8:24, :] - fields[field, place + 2, 8:24, :]) + (
                    8.0 * (high_x - low_x)
                )
                low_y = fields[field, place, 7:23, :]
                high_y = fields[field, place, 9:25, :]
                d_y = (fields[field, place, 6:22, :] - fields[field, place, 10:26, :]) + (
                    8.0 * (high_y - low_y)
                )
                d_z = along_z[field][:, 0:CZ]
                centre.append(fields[field, place, 8:24, :])
                grad.append((d_x, d_y, d_z))
                smooth.append(low_x + high_x + low_y + high_y + along_z[field][:, CZ:])
            scale = TIME_STEP / 12.0
            speed = [scale * centre[k] for k in (1, 2, 3)]
            lift = scale * jnp.exp((1.0 - centre[0]) * DENSITY_LOG)
            spread = TIME_STEP * DIFFUSION
            out = []
            for field in range(4):
                rate = (
                    speed[0] * grad[field][0]
                    + speed[1] * grad[field][1]
                    + speed[2] * grad[field][2]
                )
                if field > 0:
                    rate = rate + lift * grad[4][field - 1]
                out.append((1.0 - 6.0 * spread) * centre[field] + spread * smooth[field] - rate)
            rate = scale * (grad[1][0] + grad[2][1] + grad[3][2])
            out.append((1.0 - 6.0 * spread) * centre[4] + spread * smooth[4] - rate)
            return out

        def run_chunk(step, fields, groups):
            for group, count in groups:
                for copy in group_copies(step, fields, group, count):
                    copy.wait_recv()
            lanes_in = []
            for group, count in groups:
                halo = jnp.where(from_left, zleft[step, group], zright[step, group])
                for row in range(count):
                    for field in range(5):
                        here = fields[field, 2 + GROUP * group + row, 8:24, :]
                        edge = pltpu.roll(halo, (-(4 * (5 * row + field) + 2)) % CZ, 1)
                        lanes_in.append(jnp.concatenate(split(here) + split(edge), axis=1))
            lanes_out = jnp.dot(
                jnp.concatenate(lanes_in, axis=0), band[...], preferred_element_type=F32
            )
            done = 0
            for group, count in groups:
                packed = jnp.zeros((CY, CZ), F32)
                for row in range(count):
                    along_z = [lanes_out[(done + k) * CY : (done + k + 1) * CY] for k in range(5)]
                    done += 5
                    place = GROUP * group + row
                    values = moved_row(fields, along_z, 2 + place)
                    for field in range(5):
                        if step == 0:
                            fields_1[field, 2 + place, 8:24, :] = values[field]
                            packed = pack_word(packed, values[field], 5 * row + field)
                        else:
                            out_ref[field * FX + place] = 0.5 * (
                                fields_0[field, 2 + place, 8:24, :] + values[field]
                            )
                if step == 0:
                    zpack[1, group] = packed
                    for copy in group_copies(1, fields_1, group, count):
                        copy.start()

        send_first(N_GROUPS - 1, LAST_ROWS)

        def send_step(k, carry):
            send_first(N_GROUPS - 2 - k, GROUP)
            return carry

        lax.fori_loop(0, N_GROUPS - 1, send_step, 0)
        run_chunk(0, fields_0, ((6, LAST_ROWS), (5, GROUP)))
        outlet_ghost(fields_1)

        def first_step(k, carry):
            run_chunk(0, fields_0, ((4 - 2 * k, GROUP), (3 - 2 * k, GROUP)))
            return carry

        lax.fori_loop(0, 2, first_step, 0)
        inflow = take_inflow()
        ghost = [0.5 * (1.0 + inflow[3]), inflow[0], inflow[1], inflow[2]]
        for place in range(2):
            for field in range(4):
                fields_0[field, place, 8:24, :] = ghost[field]
                fields_1[field, place, 8:24, :] = ghost[field]
            fields_0[4, place, 8:24, :] = fields_0[4, 2, 8:24, :]
        run_chunk(0, fields_0, ((0, GROUP),))
        for place in range(2):
            fields_1[4, place, 8:24, :] = fields_1[4, 2, 8:24, :]
        run_chunk(1, fields_1, ((6, LAST_ROWS), (5, GROUP)))

        def second_step(k, carry):
            run_chunk(1, fields_1, ((4 - 2 * k, GROUP), (3 - 2 * k, GROUP)))
            return carry

        lax.fori_loop(0, 2, second_step, 0)
        run_chunk(1, fields_1, ((0, GROUP),))

        def finish(step, fields, group, count):
            for copy in group_copies(step, fields, group, count):
                copy.wait_send()

        for step, fields in ((0, fields_0), (1, fields_1)):
            finish(step, fields, N_GROUPS - 1, LAST_ROWS)

            def finish_step(k, carry, step=step, fields=fields):
                finish(step, fields, k, GROUP)
                return carry

            lax.fori_loop(0, N_GROUPS - 1, finish_step, 0)

    @pl.when(is_nozzle)
    def _():
        inflow = take_inflow()
        outflow = equilibrium_list(jnp.exp(inflow[0]), inflow[1:])
        for i in range(19):
            ghost_eq[i] = 0.5 * outflow[i]

        def face_copies(step, pops):
            k = 0
            copies = []

            def add(src, dst, device):
                index = len(copies)
                copies.append(
                    remote(src, dst, face_send.at[step, index], face_recv.at[step, index], device)
                )

            add(nz_plus.at[step], nz_left.at[step, 8:24, :], (solver, gy, right))
            add(nz_minus.at[step], nz_right.at[step, 8:24, :], (solver, gy, left))
            add(nz_plus.at[step, 8:16, :], nz_left.at[step, 0:8, :], (solver, up, right))
            add(nz_plus.at[step, 0:8, :], nz_left.at[step, 24:32, :], (solver, down, right))
            add(nz_minus.at[step, 8:16, :], nz_right.at[step, 0:8, :], (solver, up, left))
            add(nz_minus.at[step, 0:8, :], nz_right.at[step, 24:32, :], (solver, down, left))
            for i in PLUS_Y:
                add(pops.at[:, i, :, 23:24, :], pops.at[:, i, :, 7:8, :], (solver, up, gz))
            for i in MINUS_Y:
                add(pops.at[:, i, :, 8:9, :], pops.at[:, i, :, 24:25, :], (solver, down, gz))
            return copies

        def phase_copies(step):
            send = lambda k: phase_send.at[step, k]
            recv = lambda k: phase_recv.at[step, k]
            grid = phase_buf.at[step]
            return [
                remote(
                    grid.at[1:6, 23:24, :], grid.at[1:6, 7:8, :], send(0), recv(0), (solver, up, gz)
                ),
                remote(
                    grid.at[1:6, 8:9, :],
                    grid.at[1:6, 24:25, :],
                    send(1),
                    recv(1),
                    (solver, down, gz),
                ),
                remote(
                    qz_plus.at[step], qz_left.at[step], send(2), recv(2), (solver, gy, right)
                ),
                remote(
                    qz_minus.at[step], qz_right.at[step], send(3), recv(3), (solver, gy, left)
                ),
            ]

        def word_of(directions, i, colour, row):
            return (directions.index(i) * 2 + colour) * 6 + row

        def run_step(step, pops):
            red_last = weighted_sum([pops[0, i, LX - 1, 8:24, :] for i in range(19)])
            blue_last = weighted_sum([pops[1, i, LX - 1, 8:24, :] for i in range(19)])
            phase_last = (red_last - blue_last) / (red_last + blue_last)
            for i in range(19):
                pops[0, i, LX, 8:24, :] = (1.0 + phase_last) * ghost_eq[i]
                pops[1, i, LX, 8:24, :] = (1.0 - phase_last) * ghost_eq[i]
            packed_plus = jnp.zeros((CY, CZ), F32)
            packed_minus = jnp.zeros((CY, CZ), F32)
            for colour in range(2):
                for row in range(LX + 1):
                    for i in PLUS_Z:
                        word = word_of(PLUS_Z, i, colour, row)
                        value = pltpu.roll(pops[colour, i, row, 8:24, :], word + 1, 1)
                        packed_plus = jnp.where(lane == word, value, packed_plus)
                    for i in MINUS_Z:
                        word = word_of(MINUS_Z, i, colour, row)
                        value = pops[colour, i, row, 8:24, :]
                        if word:
                            value = pltpu.roll(value, word, 1)
                        packed_minus = jnp.where(lane == word, value, packed_minus)
            nz_plus[step] = packed_plus
            nz_minus[step] = packed_minus
            copies = face_copies(step, pops)
            for copy in copies:
                copy.start()
            for copy in copies:
                copy.wait_recv()
            for colour in range(2):
                for i in range(19):
                    shift_y, shift_z = VELOCITY_TABLE[i][1:]
                    span = slice(8 - shift_y, 24 - shift_y)
                    for row in range(LX + 1):
                        value = pops[colour, i, row, span, :]
                        if shift_z == 1:
                            word = word_of(PLUS_Z, i, colour, row)
                            edge = nz_left[step, span, :]
                            if word:
                                edge = pltpu.roll(edge, CZ - word, 1)
                            value = jnp.where(lane == 0, edge, pltpu.roll(value, 1, 1))
                        elif shift_z == -1:
                            word = word_of(MINUS_Z, i, colour, row)
                            edge = pltpu.roll(nz_right[step, span, :], CZ - 1 - word, 1)
                            value = jnp.where(lane == CZ - 1, edge, pltpu.roll(value, CZ - 1, 1))
                        moved[colour, i, row] = value

            def read(colour, i, x):
                shift_x = VELOCITY_TABLE[i][0]
                return moved[colour, i, jnp.clip(x - shift_x, 0, LX)]

            def mass_step(k, carry):
                red = weighted_sum([read(0, i, k - 1) for i in range(19)])
                blue = weighted_sum([read(1, i, k - 1) for i in range(19)])
                masses[0, k] = red
                masses[1, k] = blue
                phase_buf[step, k, 8:24, :] = (red - blue) / (red + blue)
                return carry

            lax.fori_loop(0, LX + 2, mass_step, 0)
            packed_plus = jnp.zeros((CY, CZ), F32)
            packed_minus = jnp.zeros((CY, CZ), F32)
            for x in range(LX):
                value = phase_buf[step, x + 1, 8:24, :]
                packed_plus = jnp.where(lane == x, pltpu.roll(value, x + 1, 1), packed_plus)
                packed_minus = jnp.where(
                    lane == x, pltpu.roll(value, x, 1) if x else value, packed_minus
                )
            qz_plus[step] = packed_plus
            qz_minus[step] = packed_minus
            phases = phase_copies(step)
            for copy in phases:
                copy.start()

            def relax_step(x, carry):
                mixed = [read(0, i, x) + read(1, i, x) for i in range(19)]
                total = masses[0, x + 1] + masses[1, x + 1]
                inverse = 1.0 / total
                vec = [weighted_momentum(mixed, dim) * inverse for dim in range(3)]
                balance = equilibrium_list(total, vec)
                for i in range(19):
                    relaxed[x, i] = mixed[i] - (mixed[i] - balance[i]) * (1.0 / RELAX_TIME)
                return carry

            lax.fori_loop(0, LX, relax_step, 0)
            for copy in phases:
                copy.wait_recv()

            def colour_step(x, carry):
                here = phase_buf[step, x + 1, 8:24, :]
                edge_low = pltpu.roll(qz_left[step], CZ - x, 1)
                edge_high = pltpu.roll(qz_right[step], CZ - 1 - x, 1)
                low_z = jnp.where(lane == 0, edge_low, pltpu.roll(here, 1, 1))
                high_z = jnp.where(lane == CZ - 1, edge_high, pltpu.roll(here, CZ - 1, 1))
                grad = [
                    0.5 * (phase_buf[step, x + 2, 8:24, :] - phase_buf[step, x, 8:24, :]),
                    0.5 * (phase_buf[step, x + 1, 9:25, :] - phase_buf[step, x + 1, 7:23, :]),
                    0.5 * (high_z - low_z),
                ]
                grad_sq = grad[0] * grad[0] + grad[1] * grad[1] + grad[2] * grad[2]
                inverse_norm = 1.0 / jnp.sqrt(grad_sq + GRAD_FLOOR * GRAD_FLOOR)
                red = masses[0, x + 1]
                blue = masses[1, x + 1]
                red_part = red / (red + blue)
                tension = SURF_TENSION * inverse_norm
                level = tension * grad_sq * (1.0 / 3.0)
                split = SEGREGATION_BETA * (red_part * blue) * inverse_norm
                solid = solid_ref[x] != 0
                for i in range(19):
                    value = relaxed[x, i] - level
                    if i:
                        slope = along(i, grad)
                        value = value + tension * (slope * slope)
                        red_value = red_part * value + split * slope
                    else:
                        red_value = red_part * value
                    back = OPPOSITE_TABLE[i]
                    red_new = jnp.where(solid, read(0, back, x), red_value)
                    blue_new = jnp.where(solid, read(1, back, x), value - red_value)
                    if step == 0:
                        pops_1[0, i, x, 8:24, :] = red_new
                        pops_1[1, i, x, 8:24, :] = blue_new
                    else:
                        out_ref[i * LX + x] = red_new
                        out_ref[(19 + i) * LX + x] = blue_new
                return carry

            lax.fori_loop(0, LX, colour_step, 0)
            return copies + phases

        pending = run_step(0, pops_0) + run_step(1, pops_1)
        for copy in pending:
            copy.wait_send()

    def finish_route(tile, carry):
        route(tile).wait_send()
        return carry

    lax.fori_loop(0, N_GY, finish_route, 0)


def on_device(coupled_state, solid_mask, inlet_source):
    words = coupled_state.shape[1]
    vmem = lambda *shape: pltpu.VMEM(shape, F32)
    in_hbm = lambda array: pltpu.with_memory_space_constraint(array, pltpu.HBM)
    dma = lambda *shape: pltpu.SemaphoreType.DMA(shape)
    out = pl.pallas_call(
        kernel,
        out_shape=pltpu.VMEM((words, CY, CZ), F32),
        in_specs=[
            pl.BlockSpec(memory_space=pltpu.HBM),
            pl.BlockSpec(memory_space=pltpu.HBM),
            pl.BlockSpec(memory_space=pltpu.HBM),
            pl.BlockSpec(memory_space=pltpu.HBM),
        ],
        out_specs=pl.BlockSpec(memory_space=pltpu.VMEM),
        scratch_shapes=[
            pltpu.VMEM((LX, CY, CZ), jnp.int32),
            pltpu.VMEM((1, 256), jnp.int32),
            pltpu.VMEM((512, 256), jnp.bfloat16),
            vmem(CY, 4 * CZ),
            vmem(N_GY, 8, CZ),
            vmem(N_GY, 8, CZ),
            vmem(5, FX + 4, 32, CZ),
            vmem(5, FX + 4, 32, CZ),
            vmem(2, N_GROUPS, CY, CZ),
            vmem(2, N_GROUPS, CY, CZ),
            vmem(2, N_GROUPS, CY, CZ),
            vmem(2, 19, LX + 1, 32, CZ),
            vmem(2, 19, LX + 1, 32, CZ),
            vmem(2, 19, LX + 1, CY, CZ),
            vmem(2, LX + 2, CY, CZ),
            vmem(2, LX + 2, 32, CZ),
            vmem(LX, 19, CY, CZ),
            vmem(19, CY, CZ),
            vmem(2, CY, CZ),
            vmem(2, CY, CZ),
            vmem(2, 32, CZ),
            vmem(2, 32, CZ),
            vmem(2, CY, CZ),
            vmem(2, CY, CZ),
            vmem(2, CY, CZ),
            vmem(2, CY, CZ),
            dma(3),
            dma(N_GY),
            dma(N_GY),
            dma(2, N_GROUPS, 4),
            dma(2, N_GROUPS, 4),
            dma(2, 16),
            dma(2, 16),
            dma(2, 4),
            dma(2, 4),
        ],
        compiler_params=pltpu.CompilerParams(
            collective_id=0, has_side_effects=True, vmem_limit_bytes=40 << 20
        ),
    )(
        in_hbm(coupled_state.reshape(5, FX, CY, CZ)),
        in_hbm(coupled_state.reshape(2, 19, LX, CY, CZ)),
        in_hbm(solid_mask.reshape(LX, CY, CZ)),
        in_hbm(inlet_source),
    )
    return out.reshape(coupled_state.shape)


def solution(mesh):
    return jax.shard_map(
        on_device,
        mesh=mesh,
        in_specs=(P("solver", None, "gy", "gz", None), P(None, "gy", "gz", None), P("gz", None)),
        out_specs=P("solver", None, "gy", "gz", None),
        check_vma=False,
    )
```

```python
import math

import jax
import jax.numpy as jnp
from jax import lax
from jax.experimental import pallas as pl
from jax.experimental.pallas import tpu as pltpu
from jax.sharding import PartitionSpec as P

CY = 16
CZ = 128
LX = 5
FX = 38
N_GY = 16
N_GZ = 8
MESH = pl.DeviceIdType.MESH
F32 = jnp.float32

VELOCITY_TABLE = [
    (0, 0, 0),
    (1, 0, 0),
    (-1, 0, 0),
    (0, 1, 0),
    (0, -1, 0),
    (0, 0, 1),
    (0, 0, -1),
    (1, 1, 0),
    (-1, -1, 0),
    (1, -1, 0),
    (-1, 1, 0),
    (1, 0, 1),
    (-1, 0, -1),
    (1, 0, -1),
    (-1, 0, 1),
    (0, 1, 1),
    (0, -1, -1),
    (0, 1, -1),
    (0, -1, 1),
]
OPPOSITE_TABLE = [0, 2, 1, 4, 3, 6, 5, 8, 7, 10, 9, 12, 11, 14, 13, 16, 15, 18, 17]
RELAX_TIME = 0.8
SURF_TENSION = 0.02
SEGREGATION_BETA = 0.7
GRAD_FLOOR = 0.1
TIME_STEP = 0.2
VISCOSITY = 0.05
DIFFUSION = 0.05
DENSITY_LOG = math.log(2.0)

PLUS_Z = [i for i in range(19) if VELOCITY_TABLE[i][2] == 1]
MINUS_Z = [i for i in range(19) if VELOCITY_TABLE[i][2] == -1]
PLUS_Y = [i for i in range(19) if VELOCITY_TABLE[i][1] == 1]
SIGNS = (0, 1, -1)
CLASSES = [
    [i for i in range(19) if VELOCITY_TABLE[i][1:] == (sy, sz)] for sy in SIGNS for sz in SIGNS
]
MINUS_Y = [i for i in range(19) if VELOCITY_TABLE[i][1] == -1]

GROUP = 6
N_GROUPS = 7
LAST_ROWS = FX - GROUP * (N_GROUPS - 1)


def weighted_sum(values):
    faces = values[1]
    for i in range(2, 7):
        faces = faces + values[i]
    edges = values[7]
    for i in range(8, 19):
        edges = edges + values[i]
    return values[0] * (1.0 / 3.0) + faces * (1.0 / 18.0) + edges * (1.0 / 36.0)


def weight_of(i):
    return 1.0 / 3.0 if i == 0 else (1.0 / 18.0 if i < 7 else 1.0 / 36.0)


def part_sum(directions, read):
    total = None
    for weight in (1.0 / 3.0, 1.0 / 18.0, 1.0 / 36.0):
        values = [read(i) for i in directions if weight_of(i) == weight]
        if values:
            group = values[0]
            for value in values[1:]:
                group = group + value
            total = weight * group if total is None else total + weight * group
    return total


def weighted_momentum(values, dim):
    faces = None
    edges = None
    for i in range(1, 19):
        sign = VELOCITY_TABLE[i][dim]
        if sign == 0:
            continue
        if i < 7:
            faces = (
                values[i]
                if faces is None
                else (faces + values[i] if sign > 0 else faces - values[i])
            )
        else:
            edges = (
                values[i]
                if edges is None
                else (edges + values[i] if sign > 0 else edges - values[i])
            )
    return faces * (1.0 / 18.0) + edges * (1.0 / 36.0)


def along(direction, vec):
    total = None
    for sign, part in zip(VELOCITY_TABLE[direction], vec):
        if sign == 0:
            continue
        if total is None:
            total = part if sign > 0 else -part
        else:
            total = total + part if sign > 0 else total - part
    return total


def equilibrium_list(density, vec):
    speed_sq = vec[0] * vec[0] + vec[1] * vec[1] + vec[2] * vec[2]
    rest = density * (1.0 - 1.5 * speed_sq)
    out = [rest]
    for i in range(1, 19, 2):
        proj = along(i, vec)
        even = rest + (4.5 * density) * (proj * proj)
        odd = (3.0 * density) * proj
        out += [even + odd, even - odd]
    return out


def kernel(
    pipe_in,
    nozzle_in,
    solid_in,
    inlet_in,
    out_ref,
    solid_ref,
    inlet_ref,
    band,
    prof,
    route_out,
    route_in,
    fields_0,
    fields_1,
    zpack,
    zleft,
    zright,
    pops_0,
    pops_1,
    moved,
    masses,
    phase_buf,
    ghost_eq,
    class_sums,
    nz_plus,
    nz_minus,
    nz_left,
    nz_right,
    row_sums,
    own_sums,
    row_sums_in,
    row_corners_in,
    own_sums_in,
    in_sem,
    route_send,
    route_recv,
    pipe_send,
    pipe_recv,
    face_send,
    face_recv,
):
    solver = lax.axis_index("solver")
    gy = lax.axis_index("gy")
    gz = lax.axis_index("gz")
    other = 1 - solver
    up = lax.rem(gy + 1, N_GY)
    down = lax.rem(gy + N_GY - 1, N_GY)
    right = lax.rem(gz + 1, N_GZ)
    left = lax.rem(gz + N_GZ - 1, N_GZ)
    is_nozzle = solver == 0
    lane = lax.broadcasted_iota(jnp.int32, (CY, CZ), 1)

    def remote(src, dst, send_sem, recv_sem, device):
        return pltpu.make_async_remote_copy(
            src_ref=src,
            dst_ref=dst,
            send_sem=send_sem,
            recv_sem=recv_sem,
            device_id=device,
            device_id_type=MESH,
        )

    inlet_load = pltpu.make_async_copy(inlet_in, inlet_ref, in_sem.at[1])
    solid_load = pltpu.make_async_copy(solid_in, solid_ref, in_sem.at[2])
    inlet_load.start()
    lane_word = lax.shift_right_logical(lane, 2)

    def pack_word(packed, value, word):
        return jnp.where(lane_word == word, pltpu.roll(value, (4 * word + 2) % CZ, 1), packed)

    def pack_first(group, count):
        packed = jnp.zeros((CY, CZ), F32)
        for row in range(count):
            for field in range(5):
                value = fields_0[field, 2 + GROUP * group + row, 8:24, :]
                packed = pack_word(packed, value, 5 * row + field)
        zpack[0, group] = packed

    def outlet_ghost(fields):
        for field in range(5):
            end = fields[field, 1 + FX, 8:24, :]
            fields[field, 2 + FX, 8:24, :] = end
            fields[field, 3 + FX, 8:24, :] = end

    pipe_load = pltpu.make_async_copy(pipe_in, fields_0.at[:, 2 : 2 + FX, 8:24, :], in_sem.at[0])
    nozzle_load = pltpu.make_async_copy(nozzle_in, pops_0.at[:, :, 0:LX, 8:24, :], in_sem.at[0])

    @pl.when(is_nozzle)
    def _():
        nozzle_load.start()
        solid_load.start()

    @pl.when(jnp.logical_not(is_nozzle))
    def _():
        pipe_load.start()

    barrier = pltpu.get_barrier_semaphore()
    for device in (
        (solver, up, gz),
        (solver, down, gz),
        (solver, gy, right),
        (solver, gy, left),
        (solver, up, right),
        (solver, up, left),
        (solver, down, right),
        (solver, down, left),
    ):
        pl.semaphore_signal(barrier, inc=1, device_id=device, device_id_type=MESH)

    def greet(tile, carry):
        pl.semaphore_signal(barrier, inc=1, device_id=(other, tile, gz), device_id_type=MESH)
        return carry

    lax.fori_loop(0, N_GY, greet, 0)

    inlet_load.wait()
    source = inlet_ref[...]
    row_ids = lax.broadcasted_iota(jnp.int32, (1, 256), 1)
    tile_rows = lax.broadcasted_iota(jnp.int32, (N_GY, 256), 0)
    source_tile = lax.shift_right_logical(source, 4)
    target_tile = lax.shift_right_logical(row_ids, 4)
    member = (tile_rows == source_tile).astype(jnp.bfloat16)
    first = lax.broadcasted_iota(jnp.int32, (256, 256), 0)
    second = lax.broadcasted_iota(jnp.int32, (256, 256), 1)
    before = (
        (first < second)
        & (lax.shift_right_logical(first, 4) == lax.shift_right_logical(second, 4))
    ).astype(jnp.bfloat16)
    counts = jnp.dot(member, before, preferred_element_type=F32)
    rank = jnp.sum(counts * member.astype(F32), axis=0, keepdims=True)
    far_tile = jnp.where(is_nozzle, target_tile, source_tile)
    local_row = jnp.where(is_nozzle, source, row_ids)
    mine = (local_row == tile_rows + gy * CY).astype(jnp.bfloat16)
    slot_rows = []
    row_slots = []
    for slot in range(2):
        taken = ((far_tile == tile_rows) & (rank == float(slot))).astype(jnp.bfloat16)
        dims = (((1,), (1,)), ((), ()))
        slot_rows.append(lax.dot_general(taken, mine, dims, preferred_element_type=F32))
        row_slots.append(lax.dot_general(mine, taken, dims, preferred_element_type=F32))

    @pl.when(is_nozzle)
    def _():
        nozzle_load.wait()
        solid_load.wait()
        red = [pops_0[0, i, LX - 1, 8:24, :] for i in range(19)]
        blue = [pops_0[1, i, LX - 1, 8:24, :] for i in range(19)]
        red_mass = weighted_sum(red)
        blue_mass = weighted_sum(blue)
        inverse = 1.0 / (red_mass + blue_mass)
        mixed = [r + b for r, b in zip(red, blue)]
        for dim in range(3):
            prof[:, dim * CZ : (dim + 1) * CZ] = weighted_momentum(mixed, dim) * inverse
        prof[:, 3 * CZ :] = (red_mass - blue_mass) * inverse

    @pl.when(jnp.logical_not(is_nozzle))
    def _():
        pipe_load.wait()
        for slot, field in enumerate((4, 1, 2, 3)):
            prof[:, slot * CZ : (slot + 1) * CZ] = fields_0[field, 2, 8:24, :]
        lane_in = lax.broadcasted_iota(jnp.int32, (CZ, CZ), 0)
        lane_out = lax.broadcasted_iota(jnp.int32, (CZ, CZ), 1)
        ahead = lane_in - lane_out
        wrapped = jnp.where(
            ahead > 64, ahead - CZ, jnp.where(ahead < -64, ahead + CZ, jnp.zeros_like(ahead))
        )
        for part, apart in enumerate((ahead, wrapped)):
            near = (jnp.abs(apart) == 1).astype(F32)
            far = (jnp.abs(apart) == 2).astype(F32)
            slope = jnp.where(apart > 0, 8.0 * near - far, far - 8.0 * near)
            for copy in range(2):
                rows = slice((2 * part + copy) * CZ, (2 * part + copy + 1) * CZ)
                band[rows, 0:CZ] = slope.astype(jnp.bfloat16)
                band[rows, CZ:] = near.astype(jnp.bfloat16)

        def pack_step(k, carry):
            pack_first(k, GROUP)
            return carry

        lax.fori_loop(0, N_GROUPS - 1, pack_step, 0)
        pack_first(N_GROUPS - 1, LAST_ROWS)
        outlet_ghost(fields_0)

    rows = prof[...]
    for slot in range(2):
        picked = jnp.dot(
            slot_rows[slot], rows, precision=lax.Precision.HIGHEST, preferred_element_type=F32
        )
        for part in range(4):
            route_out[:, slot * 4 + part, :] = picked[:, part * CZ : (part + 1) * CZ]

    pl.semaphore_wait(barrier, 8 + N_GY)

    def route(tile):
        return remote(
            route_out.at[tile],
            route_in.at[gy],
            route_send.at[tile],
            route_recv.at[gy],
            (other, tile, gz),
        )

    def send_route(tile, carry):
        route(tile).start()
        return carry

    lax.fori_loop(0, N_GY, send_route, 0)

    def take_inflow():
        def receive(tile, carry):
            remote(
                route_out.at[tile],
                route_in.at[tile],
                route_send.at[tile],
                route_recv.at[tile],
                (other, tile, gz),
            ).wait_recv()
            return carry

        lax.fori_loop(0, N_GY, receive, 0)
        total = None
        for slot in range(2):
            arrived = jnp.concatenate(
                [route_in[:, slot * 4 + part, :] for part in range(4)], axis=1
            )
            term = jnp.dot(
                row_slots[slot],
                arrived,
                precision=lax.Precision.HIGHEST,
                preferred_element_type=F32,
            )
            total = term if total is None else total + term
        return [total[:, part * CZ : (part + 1) * CZ] for part in range(4)]

    @pl.when(jnp.logical_not(is_nozzle))
    def _():
        from_left = (lane & 3) < 2

        def group_copies(step, fields, group, count):
            first_row = 2 + GROUP * group
            span = pl.ds(first_row, count)
            send = lambda k: pipe_send.at[step, group, k]
            recv = lambda k: pipe_recv.at[step, group, k]
            return [
                remote(
                    fields.at[:, span, 22:24, :],
                    fields.at[:, span, 6:8, :],
                    send(0),
                    recv(0),
                    (solver, up, gz),
                ),
                remote(
                    fields.at[:, span, 8:10, :],
                    fields.at[:, span, 24:26, :],
                    send(1),
                    recv(1),
                    (solver, down, gz),
                ),
                remote(
                    zpack.at[step, group],
                    zleft.at[step, group],
                    send(2),
                    recv(2),
                    (solver, gy, right),
                ),
                remote(
                    zpack.at[step, group],
                    zright.at[step, group],
                    send(3),
                    recv(3),
                    (solver, gy, left),
                ),
            ]

        def send_first(group, count):
            for copy in group_copies(0, fields_0, group, count):
                copy.start()

        def split(value):
            high = value.astype(jnp.bfloat16)
            return [high, (value - high.astype(F32)).astype(jnp.bfloat16)]

        def moved_row(fields, along_z, place):
            centre, grad, smooth = [], [], []
            for field in range(5):
                low_x = fields[field, place - 1, 8:24, :]
                high_x = fields[field, place + 1, 8:24, :]
                d_x = (fields[field, place - 2, 8:24, :] - fields[field, place + 2, 8:24, :]) + (
                    8.0 * (high_x - low_x)
                )
                low_y = fields[field, place, 7:23, :]
                high_y = fields[field, place, 9:25, :]
                d_y = (fields[field, place, 6:22, :] - fields[field, place, 10:26, :]) + (
                    8.0 * (high_y - low_y)
                )
                d_z = along_z[field][:, 0:CZ]
                centre.append(fields[field, place, 8:24, :])
                grad.append((d_x, d_y, d_z))
                smooth.append(low_x + high_x + low_y + high_y + along_z[field][:, CZ:])
            scale = TIME_STEP / 12.0
            speed = [scale * centre[k] for k in (1, 2, 3)]
            lift = scale * jnp.exp((1.0 - centre[0]) * DENSITY_LOG)
            spread = TIME_STEP * DIFFUSION
            out = []
            for field in range(4):
                rate = (
                    speed[0] * grad[field][0]
                    + speed[1] * grad[field][1]
                    + speed[2] * grad[field][2]
                )
                if field > 0:
                    rate = rate + lift * grad[4][field - 1]
                out.append((1.0 - 6.0 * spread) * centre[field] + spread * smooth[field] - rate)
            rate = scale * (grad[1][0] + grad[2][1] + grad[3][2])
            out.append((1.0 - 6.0 * spread) * centre[4] + spread * smooth[4] - rate)
            return out

        def run_chunk(step, fields, groups):
            for group, count in groups:
                for copy in group_copies(step, fields, group, count):
                    copy.wait_recv()
            lanes_in = []
            for group, count in groups:
                halo = jnp.where(from_left, zleft[step, group], zright[step, group])
                for row in range(count):
                    for field in range(5):
                        here = fields[field, 2 + GROUP * group + row, 8:24, :]
                        edge = pltpu.roll(halo, (-(4 * (5 * row + field) + 2)) % CZ, 1)
                        lanes_in.append(jnp.concatenate(split(here) + split(edge), axis=1))
            lanes_out = jnp.dot(
                jnp.concatenate(lanes_in, axis=0), band[...], preferred_element_type=F32
            )
            done = 0
            for group, count in groups:
                packed = jnp.zeros((CY, CZ), F32)
                for row in range(count):
                    along_z = [lanes_out[(done + k) * CY : (done + k + 1) * CY] for k in range(5)]
                    done += 5
                    place = GROUP * group + row
                    values = moved_row(fields, along_z, 2 + place)
                    for field in range(5):
                        if step == 0:
                            fields_1[field, 2 + place, 8:24, :] = values[field]
                            packed = pack_word(packed, values[field], 5 * row + field)
                        else:
                            out_ref[field * FX + place] = 0.5 * (
                                fields_0[field, 2 + place, 8:24, :] + values[field]
                            )
                if step == 0:
                    zpack[1, group] = packed
                    for copy in group_copies(1, fields_1, group, count):
                        copy.start()

        send_first(N_GROUPS - 1, LAST_ROWS)

        def send_step(k, carry):
            send_first(N_GROUPS - 2 - k, GROUP)
            return carry

        lax.fori_loop(0, N_GROUPS - 1, send_step, 0)
        run_chunk(0, fields_0, ((6, LAST_ROWS), (5, GROUP)))
        outlet_ghost(fields_1)

        def first_step(k, carry):
            run_chunk(0, fields_0, ((4 - 2 * k, GROUP), (3 - 2 * k, GROUP)))
            return carry

        lax.fori_loop(0, 2, first_step, 0)
        inflow = take_inflow()
        ghost = [0.5 * (1.0 + inflow[3]), inflow[0], inflow[1], inflow[2]]
        for place in range(2):
            for field in range(4):
                fields_0[field, place, 8:24, :] = ghost[field]
                fields_1[field, place, 8:24, :] = ghost[field]
            fields_0[4, place, 8:24, :] = fields_0[4, 2, 8:24, :]
        run_chunk(0, fields_0, ((0, GROUP),))
        for place in range(2):
            fields_1[4, place, 8:24, :] = fields_1[4, 2, 8:24, :]
        run_chunk(1, fields_1, ((6, LAST_ROWS), (5, GROUP)))

        def second_step(k, carry):
            run_chunk(1, fields_1, ((4 - 2 * k, GROUP), (3 - 2 * k, GROUP)))
            return carry

        lax.fori_loop(0, 2, second_step, 0)
        run_chunk(1, fields_1, ((0, GROUP),))

        def finish(step, fields, group, count):
            for copy in group_copies(step, fields, group, count):
                copy.wait_send()

        for step, fields in ((0, fields_0), (1, fields_1)):
            finish(step, fields, N_GROUPS - 1, LAST_ROWS)

            def finish_step(k, carry, step=step, fields=fields):
                finish(step, fields, k, GROUP)
                return carry

            lax.fori_loop(0, N_GROUPS - 1, finish_step, 0)

    @pl.when(is_nozzle)
    def _():
        inflow = take_inflow()
        outflow = equilibrium_list(jnp.exp(inflow[0]), inflow[1:])
        for i in range(19):
            ghost_eq[i] = 0.5 * outflow[i]

        def face_copies(step, pops):
            k = 0
            copies = []

            def add(src, dst, device):
                index = len(copies)
                copies.append(
                    remote(src, dst, face_send.at[step, index], face_recv.at[step, index], device)
                )

            add(nz_plus.at[step], nz_left.at[step, 8:24, :], (solver, gy, right))
            add(nz_minus.at[step], nz_right.at[step, 8:24, :], (solver, gy, left))
            add(nz_plus.at[step, 8:16, :], nz_left.at[step, 0:8, :], (solver, up, right))
            add(nz_plus.at[step, 0:8, :], nz_left.at[step, 24:32, :], (solver, down, right))
            add(nz_minus.at[step, 8:16, :], nz_right.at[step, 0:8, :], (solver, up, left))
            add(nz_minus.at[step, 0:8, :], nz_right.at[step, 24:32, :], (solver, down, left))
            for i in PLUS_Y:
                add(pops.at[:, i, :, 23:24, :], pops.at[:, i, :, 7:8, :], (solver, up, gz))
            for i in MINUS_Y:
                add(pops.at[:, i, :, 8:9, :], pops.at[:, i, :, 24:25, :], (solver, down, gz))
            add(row_sums.at[step, 0], row_sums_in.at[step, 0], (solver, up, gz))
            add(row_sums.at[step, 1], row_sums_in.at[step, 1], (solver, down, gz))
            for side, row in ((0, up), (1, down)):
                for k, column in ((0, right), (1, left)):
                    add(
                        row_sums.at[step, side, 1 + k],
                        row_corners_in.at[step, side, k],
                        (solver, row, column),
                    )
            add(own_sums.at[step, 1], own_sums_in.at[step, 0], (solver, gy, right))
            add(own_sums.at[step, 2], own_sums_in.at[step, 1], (solver, gy, left))
            return copies

        def word_of(directions, i, colour, row):
            return (directions.index(i) * 2 + colour) * 6 + row

        def run_step(step, pops):
            red_last = weighted_sum([pops[0, i, LX - 1, 8:24, :] for i in range(19)])
            blue_last = weighted_sum([pops[1, i, LX - 1, 8:24, :] for i in range(19)])
            phase_last = (red_last - blue_last) / (red_last + blue_last)
            for i in range(19):
                pops[0, i, LX, 8:24, :] = (1.0 + phase_last) * ghost_eq[i]
                pops[1, i, LX, 8:24, :] = (1.0 - phase_last) * ghost_eq[i]
            packed_plus = jnp.zeros((CY, CZ), F32)
            packed_minus = jnp.zeros((CY, CZ), F32)
            for colour in range(2):
                for row in range(LX + 1):
                    for i in PLUS_Z:
                        word = word_of(PLUS_Z, i, colour, row)
                        value = pltpu.roll(pops[colour, i, row, 8:24, :], word + 1, 1)
                        packed_plus = jnp.where(lane == word, value, packed_plus)
                    for i in MINUS_Z:
                        word = word_of(MINUS_Z, i, colour, row)
                        value = pops[colour, i, row, 8:24, :]
                        if word:
                            value = pltpu.roll(value, word, 1)
                        packed_minus = jnp.where(lane == word, value, packed_minus)
            def class_step(x, packed):
                for colour in range(2):
                    sums = []
                    for k, directions in enumerate(CLASSES):
                        value = part_sum(
                            directions,
                            lambda i: pops[
                                colour, i, jnp.clip(x - VELOCITY_TABLE[i][0], 0, LX), 8:24, :
                            ],
                        )
                        class_sums[k, colour, x] = value
                        sums.append(value)
                    for k in range(3):
                        high = sums[3 * k] + pltpu.roll(sums[3 * k + 1], 1, 1)
                        low = sums[3 * k] + pltpu.roll(sums[3 * k + 2], CZ - 1, 1)
                        word = 64 + 20 * k + 10 * colour + 2 * x
                        packed = (
                            jnp.where(lane == word, pltpu.roll(high, word + 1, 1), packed[0]),
                            jnp.where(lane == word + 1, pltpu.roll(low, word + 1, 1), packed[1]),
                        )
                return packed

            packed_plus, packed_minus = lax.fori_loop(
                0, LX, class_step, (packed_plus, packed_minus)
            )
            nz_plus[step] = packed_plus
            nz_minus[step] = packed_minus
            for colour in range(2):
                span = slice(8 * colour, 8 * colour + 8)
                for k in range(3):
                    row_sums[step, 0, k, span, :] = (
                        class_sums[k, colour, :, 15, :] + class_sums[3 + k, colour, :, 14, :]
                    )
                    row_sums[step, 1, k, span, :] = (
                        class_sums[k, colour, :, 0, :] + class_sums[6 + k, colour, :, 1, :]
                    )
                    own_sums[step, k, 0, span, :] = class_sums[6 + k, colour, :, 0, :]
                    own_sums[step, k, 1, span, :] = class_sums[3 + k, colour, :, 15, :]
            copies = face_copies(step, pops)
            for copy in copies:
                copy.start()
            for copy in copies:
                copy.wait_recv()
            for colour in range(2):
                for i in range(19):
                    shift_y, shift_z = VELOCITY_TABLE[i][1:]
                    span = slice(8 - shift_y, 24 - shift_y)
                    for row in range(LX + 1):
                        value = pops[colour, i, row, span, :]
                        if shift_z == 1:
                            word = word_of(PLUS_Z, i, colour, row)
                            edge = nz_left[step, span, :]
                            if word:
                                edge = pltpu.roll(edge, CZ - word, 1)
                            value = jnp.where(lane == 0, edge, pltpu.roll(value, 1, 1))
                        elif shift_z == -1:
                            word = word_of(MINUS_Z, i, colour, row)
                            edge = pltpu.roll(nz_right[step, span, :], CZ - 1 - word, 1)
                            value = jnp.where(lane == CZ - 1, edge, pltpu.roll(value, CZ - 1, 1))
                        moved[colour, i, row] = value

            def read(colour, i, x):
                shift_x = VELOCITY_TABLE[i][0]
                return moved[colour, i, jnp.clip(x - shift_x, 0, LX)]

            def mass_step(k, carry):
                red = weighted_sum([read(0, i, k - 1) for i in range(19)])
                blue = weighted_sum([read(1, i, k - 1) for i in range(19)])
                masses[0, k] = red
                masses[1, k] = blue
                phase_buf[k, 8:24, :] = (red - blue) / (red + blue)
                return carry

            lax.fori_loop(0, LX + 2, mass_step, 0)
            for side, place in ((0, 7), (1, 24)):
                part = [row_sums_in[step, side, k] + own_sums[step, k, side] for k in range(3)]
                corner = [
                    row_corners_in[step, side, k] + own_sums_in[step, k, side] for k in range(2)
                ]
                edge_lane = lax.broadcasted_iota(jnp.int32, (16, CZ), 1)
                total = (
                    part[0]
                    + pltpu.roll(jnp.where(edge_lane == CZ - 1, corner[0], part[1]), 1, 1)
                    + pltpu.roll(jnp.where(edge_lane == 0, corner[1], part[2]), CZ - 1, 1)
                )
                red = total[0:8]
                blue = total[8:16]
                phase_buf[1 : 1 + LX, place, :] = ((red - blue) / (red + blue))[0:LX]
            beside = [
                edges[step, 8:24, :]
                + pltpu.roll(edges[step, 7:23, :], CZ - 20, 1)
                + pltpu.roll(edges[step, 9:25, :], CZ - 40, 1)
                for edges in (nz_left, nz_right)
            ]
            beside = jnp.where((lane & 1) == 0, beside[0], beside[1])

            def side_mass(colour, x):
                def shifted(i):
                    shift_x, shift_y = VELOCITY_TABLE[i][0:2]
                    row = jnp.clip(x - shift_x, 0, LX)
                    return pops[colour, i, row, 8 - shift_y : 24 - shift_y, :]

                low = pltpu.roll(part_sum(MINUS_Z, shifted), CZ - 1, 1)
                high = pltpu.roll(part_sum(PLUS_Z, shifted), 1, 1)
                far = pltpu.roll(beside, CZ - 1 - (64 + 10 * colour + 2 * x), 1)
                return far + jnp.where(lane == CZ - 1, low, high)

            def collide_step(x, carry):
                red = masses[0, x + 1]
                blue = masses[1, x + 1]
                total = red + blue
                inverse = 1.0 / total
                mixed = [read(0, i, x) + read(1, i, x) for i in range(19)]
                vec = [weighted_momentum(mixed, dim) * inverse for dim in range(3)]
                balance = equilibrium_list(total, vec)
                here = phase_buf[x + 1, 8:24, :]
                side_red = side_mass(0, x)
                side_blue = side_mass(1, x)
                side = (side_red - side_blue) / (side_red + side_blue)
                low_z = pltpu.roll(jnp.where(lane == CZ - 1, side, here), 1, 1)
                high_z = pltpu.roll(jnp.where(lane == 0, side, here), CZ - 1, 1)
                grad = [
                    0.5 * (phase_buf[x + 2, 8:24, :] - phase_buf[x, 8:24, :]),
                    0.5 * (phase_buf[x + 1, 9:25, :] - phase_buf[x + 1, 7:23, :]),
                    0.5 * (high_z - low_z),
                ]
                grad_sq = grad[0] * grad[0] + grad[1] * grad[1] + grad[2] * grad[2]
                inverse_norm = 1.0 / jnp.sqrt(grad_sq + GRAD_FLOOR * GRAD_FLOOR)
                red_part = red * inverse
                tension = SURF_TENSION * inverse_norm
                level = tension * grad_sq * (1.0 / 3.0)
                split = SEGREGATION_BETA * (red_part * blue) * inverse_norm
                solid = solid_ref[x] != 0
                for i in range(19):
                    value = mixed[i] - (mixed[i] - balance[i]) * (1.0 / RELAX_TIME) - level
                    if i:
                        slope = along(i, grad)
                        value = value + tension * (slope * slope)
                        red_value = red_part * value + split * slope
                    else:
                        red_value = red_part * value
                    back = OPPOSITE_TABLE[i]
                    red_new = jnp.where(solid, read(0, back, x), red_value)
                    blue_new = jnp.where(solid, read(1, back, x), value - red_value)
                    if step == 0:
                        pops_1[0, i, x, 8:24, :] = red_new
                        pops_1[1, i, x, 8:24, :] = blue_new
                    else:
                        out_ref[i * LX + x] = red_new
                        out_ref[(19 + i) * LX + x] = blue_new
                return carry

            lax.fori_loop(0, LX, collide_step, 0)
            return copies

        pending = run_step(0, pops_0) + run_step(1, pops_1)
        for copy in pending:
            copy.wait_send()

    def finish_route(tile, carry):
        route(tile).wait_send()
        return carry

    lax.fori_loop(0, N_GY, finish_route, 0)


def on_device(coupled_state, solid_mask, inlet_source):
    words = coupled_state.shape[1]
    vmem = lambda *shape: pltpu.VMEM(shape, F32)
    in_hbm = lambda array: pltpu.with_memory_space_constraint(array, pltpu.HBM)
    dma = lambda *shape: pltpu.SemaphoreType.DMA(shape)
    out = pl.pallas_call(
        kernel,
        out_shape=pltpu.VMEM((words, CY, CZ), F32),
        in_specs=[
            pl.BlockSpec(memory_space=pltpu.HBM),
            pl.BlockSpec(memory_space=pltpu.HBM),
            pl.BlockSpec(memory_space=pltpu.HBM),
            pl.BlockSpec(memory_space=pltpu.HBM),
        ],
        out_specs=pl.BlockSpec(memory_space=pltpu.VMEM),
        scratch_shapes=[
            pltpu.VMEM((LX, CY, CZ), jnp.int32),
            pltpu.VMEM((1, 256), jnp.int32),
            pltpu.VMEM((512, 256), jnp.bfloat16),
            vmem(CY, 4 * CZ),
            vmem(N_GY, 8, CZ),
            vmem(N_GY, 8, CZ),
            vmem(5, FX + 4, 32, CZ),
            vmem(5, FX + 4, 32, CZ),
            vmem(2, N_GROUPS, CY, CZ),
            vmem(2, N_GROUPS, CY, CZ),
            vmem(2, N_GROUPS, CY, CZ),
            vmem(2, 19, LX + 1, 32, CZ),
            vmem(2, 19, LX + 1, 32, CZ),
            vmem(2, 19, LX + 1, CY, CZ),
            vmem(2, LX + 2, CY, CZ),
            vmem(LX + 2, 32, CZ),
            vmem(19, CY, CZ),
            vmem(9, 2, 8, CY, CZ),
            vmem(2, CY, CZ),
            vmem(2, CY, CZ),
            vmem(2, 32, CZ),
            vmem(2, 32, CZ),
            vmem(2, 2, 3, 16, CZ),
            vmem(2, 3, 2, 16, CZ),
            vmem(2, 2, 3, 16, CZ),
            vmem(2, 2, 2, 16, CZ),
            vmem(2, 2, 2, 16, CZ),
            dma(3),
            dma(N_GY),
            dma(N_GY),
            dma(2, N_GROUPS, 4),
            dma(2, N_GROUPS, 4),
            dma(2, 24),
            dma(2, 24),
        ],
        compiler_params=pltpu.CompilerParams(
            collective_id=0, has_side_effects=True, vmem_limit_bytes=40 << 20
        ),
    )(
        in_hbm(coupled_state.reshape(5, FX, CY, CZ)),
        in_hbm(coupled_state.reshape(2, 19, LX, CY, CZ)),
        in_hbm(solid_mask.reshape(LX, CY, CZ)),
        in_hbm(inlet_source),
    )
    return out.reshape(coupled_state.shape)


def solution(mesh):
    return jax.shard_map(
        on_device,
        mesh=mesh,
        in_specs=(P("solver", None, "gy", "gz", None), P(None, "gy", "gz", None), P("gz", None)),
        out_specs=P("solver", None, "gy", "gz", None),
        check_vma=False,
    )
```

```python
import math

import jax
import jax.numpy as jnp
from jax import lax
from jax.experimental import pallas as pl
from jax.experimental.pallas import tpu as pltpu
from jax.sharding import PartitionSpec as P

CY = 16
CZ = 128
LX = 5
FX = 38
N_GY = 16
N_GZ = 8
MESH = pl.DeviceIdType.MESH
F32 = jnp.float32

VELOCITY_TABLE = [
    (0, 0, 0),
    (1, 0, 0),
    (-1, 0, 0),
    (0, 1, 0),
    (0, -1, 0),
    (0, 0, 1),
    (0, 0, -1),
    (1, 1, 0),
    (-1, -1, 0),
    (1, -1, 0),
    (-1, 1, 0),
    (1, 0, 1),
    (-1, 0, -1),
    (1, 0, -1),
    (-1, 0, 1),
    (0, 1, 1),
    (0, -1, -1),
    (0, 1, -1),
    (0, -1, 1),
]
OPPOSITE_TABLE = [0, 2, 1, 4, 3, 6, 5, 8, 7, 10, 9, 12, 11, 14, 13, 16, 15, 18, 17]
RELAX_TIME = 0.8
SURF_TENSION = 0.02
SEGREGATION_BETA = 0.7
GRAD_FLOOR = 0.1
TIME_STEP = 0.2
VISCOSITY = 0.05
DIFFUSION = 0.05
DENSITY_LOG = math.log(2.0)

PLUS_Z = [i for i in range(19) if VELOCITY_TABLE[i][2] == 1]
MINUS_Z = [i for i in range(19) if VELOCITY_TABLE[i][2] == -1]
PLUS_Y = [i for i in range(19) if VELOCITY_TABLE[i][1] == 1]
SIGNS = (0, 1, -1)
CLASSES = [
    [i for i in range(19) if VELOCITY_TABLE[i][1:] == (sy, sz)] for sy in SIGNS for sz in SIGNS
]
MINUS_Y = [i for i in range(19) if VELOCITY_TABLE[i][1] == -1]

GROUP = 6
N_GROUPS = 7
LAST_ROWS = FX - GROUP * (N_GROUPS - 1)
CHUNKS = (
    ((6, LAST_ROWS), (5, GROUP)),
    ((4, GROUP), (3, GROUP)),
    ((2, GROUP), (1, GROUP)),
    ((0, GROUP),),
)


ROUTE_ROWS = 8 * N_GY
PIPE_ROWS = 2 * (2 * 2 * 5 * FX + 2 * CY * N_GROUPS)
FACE_ROWS = 2 * CY + 4 * 8 + 2 * 3 * 16 + 4 * 16 + 2 * 2 * 16
POP_ROWS = 2 * 5 * 2
NOZZLE_ROWS = 4 * FACE_ROWS + POP_ROWS * 2 * (LX + 1)
MOST_ROWS = ROUTE_ROWS + max(PIPE_ROWS, NOZZLE_ROWS)


def weighted_sum(values):
    faces = values[1]
    for i in range(2, 7):
        faces = faces + values[i]
    edges = values[7]
    for i in range(8, 19):
        edges = edges + values[i]
    return values[0] * (1.0 / 3.0) + faces * (1.0 / 18.0) + edges * (1.0 / 36.0)


def weight_of(i):
    return 1.0 / 3.0 if i == 0 else (1.0 / 18.0 if i < 7 else 1.0 / 36.0)


def part_sum(directions, read):
    total = None
    for weight in (1.0 / 3.0, 1.0 / 18.0, 1.0 / 36.0):
        values = [read(i) for i in directions if weight_of(i) == weight]
        if values:
            group = values[0]
            for value in values[1:]:
                group = group + value
            total = weight * group if total is None else total + weight * group
    return total


def weighted_momentum(values, dim):
    faces = None
    edges = None
    for i in range(1, 19):
        sign = VELOCITY_TABLE[i][dim]
        if sign == 0:
            continue
        if i < 7:
            faces = (
                values[i]
                if faces is None
                else (faces + values[i] if sign > 0 else faces - values[i])
            )
        else:
            edges = (
                values[i]
                if edges is None
                else (edges + values[i] if sign > 0 else edges - values[i])
            )
    return faces * (1.0 / 18.0) + edges * (1.0 / 36.0)


def along(direction, vec):
    total = None
    for sign, part in zip(VELOCITY_TABLE[direction], vec):
        if sign == 0:
            continue
        if total is None:
            total = part if sign > 0 else -part
        else:
            total = total + part if sign > 0 else total - part
    return total


def equilibrium_list(density, vec):
    speed_sq = vec[0] * vec[0] + vec[1] * vec[1] + vec[2] * vec[2]
    rest = density * (1.0 - 1.5 * speed_sq)
    out = [rest]
    for i in range(1, 19, 2):
        proj = along(i, vec)
        even = rest + (4.5 * density) * (proj * proj)
        odd = (3.0 * density) * proj
        out += [even + odd, even - odd]
    return out


def kernel(
    pipe_in,
    nozzle_in,
    solid_in,
    inlet_in,
    out_ref,
    stage_pipe,
    stage_nozzle,
    solid_ref,
    inlet_ref,
    band,
    prof,
    route_out,
    route_in,
    fields_0,
    fields_1,
    zpack,
    zleft,
    zright,
    pops_0,
    pops_1,
    moved,
    masses,
    phase_buf,
    ghost_eq,
    class_sums,
    nz_plus,
    nz_minus,
    nz_left,
    nz_right,
    row_sums,
    own_sums,
    row_sums_in,
    row_corners_in,
    own_sums_in,
    tally,
    in_sem,
    out_sem,
    send_sem,
    route_recv,
    recv_sem,
):
    solver = lax.axis_index("solver")
    gy = lax.axis_index("gy")
    gz = lax.axis_index("gz")
    other = 1 - solver
    up = lax.rem(gy + 1, N_GY)
    down = lax.rem(gy + N_GY - 1, N_GY)
    right = lax.rem(gz + 1, N_GZ)
    left = lax.rem(gz + N_GZ - 1, N_GZ)
    is_nozzle = solver == 0
    lane = lax.broadcasted_iota(jnp.int32, (CY, CZ), 1)

    def remote(src, dst, send_sem, recv_sem, device):
        return pltpu.make_async_remote_copy(
            src_ref=src,
            dst_ref=dst,
            send_sem=send_sem,
            recv_sem=recv_sem,
            device_id=device,
            device_id_type=MESH,
        )

    def wait_rows(sem, rows):
        part = tally.at[0:rows, :]
        pltpu.make_async_copy(part, part, sem).wait()

    inlet_load = pltpu.make_async_copy(inlet_in, inlet_ref, in_sem.at[1])
    solid_load = pltpu.make_async_copy(solid_in, solid_ref, in_sem.at[2])
    inlet_load.start()
    lane_word = lax.shift_right_logical(lane, 2)

    def pack_word(packed, value, word):
        return jnp.where(lane_word == word, pltpu.roll(value, (4 * word + 2) % CZ, 1), packed)

    def pack_first(group, count):
        packed = jnp.zeros((CY, CZ), F32)
        for row in range(count):
            for field in range(5):
                value = fields_0[field, 2 + GROUP * group + row, 8:24, :]
                packed = pack_word(packed, value, 5 * row + field)
        zpack[0, group] = packed

    def outlet_ghost(fields):
        for field in range(5):
            end = fields[field, 1 + FX, 8:24, :]
            fields[field, 2 + FX, 8:24, :] = end
            fields[field, 3 + FX, 8:24, :] = end

    nozzle_loads = [
        pltpu.make_async_copy(
            nozzle_in.at[:, :, rows, :, :], pops_0.at[:, :, rows, 8:24, :], in_sem.at[k]
        )
        for k, rows in ((0, slice(LX - 1, LX)), (3, slice(0, LX - 1)))
    ]
    pipe_loads = [
        pltpu.make_async_copy(
            pipe_in.at[part, rows, :, :],
            fields_0.at[part, slice(rows.start + 2, rows.stop + 2), 8:24, :],
            in_sem.at[k],
        )
        for k, part, rows in (
            (0, slice(1, 5), slice(0, 1)),
            (2, slice(0, 5), slice(1, FX)),
            (3, slice(0, 1), slice(0, 1)),
        )
    ]

    @pl.when(is_nozzle)
    def _():
        for copy in nozzle_loads:
            copy.start()
        solid_load.start()

    @pl.when(jnp.logical_not(is_nozzle))
    def _():
        for copy in pipe_loads:
            copy.start()

    barrier = pltpu.get_barrier_semaphore()
    for device in (
        (solver, up, gz),
        (solver, down, gz),
        (solver, gy, right),
        (solver, gy, left),
        (solver, up, right),
        (solver, up, left),
        (solver, down, right),
        (solver, down, left),
    ):
        pl.semaphore_signal(barrier, inc=1, device_id=device, device_id_type=MESH)

    def greet(tile, carry):
        pl.semaphore_signal(barrier, inc=1, device_id=(other, tile, gz), device_id_type=MESH)
        return carry

    lax.fori_loop(0, N_GY, greet, 0)

    inlet_load.wait()
    source = inlet_ref[...]
    row_ids = lax.broadcasted_iota(jnp.int32, (1, 256), 1)
    tile_rows = lax.broadcasted_iota(jnp.int32, (N_GY, 256), 0)
    source_tile = lax.shift_right_logical(source, 4)
    target_tile = lax.shift_right_logical(row_ids, 4)
    member = (tile_rows == source_tile).astype(jnp.bfloat16)
    first = lax.broadcasted_iota(jnp.int32, (256, 256), 0)
    second = lax.broadcasted_iota(jnp.int32, (256, 256), 1)
    before = (
        (first < second)
        & (lax.shift_right_logical(first, 4) == lax.shift_right_logical(second, 4))
    ).astype(jnp.bfloat16)
    counts = jnp.dot(member, before, preferred_element_type=F32)
    rank = jnp.sum(counts * member.astype(F32), axis=0, keepdims=True)
    far_tile = jnp.where(is_nozzle, target_tile, source_tile)
    local_row = jnp.where(is_nozzle, source, row_ids)
    mine = (local_row == tile_rows + gy * CY).astype(jnp.bfloat16)
    slot_rows = []
    row_slots = []
    for slot in range(2):
        taken = ((far_tile == tile_rows) & (rank == float(slot))).astype(jnp.bfloat16)
        dims = (((1,), (1,)), ((), ()))
        slot_rows.append(lax.dot_general(taken, mine, dims, preferred_element_type=F32))
        row_slots.append(lax.dot_general(mine, taken, dims, preferred_element_type=F32))

    @pl.when(is_nozzle)
    def _():
        nozzle_loads[0].wait()
        red = [pops_0[0, i, LX - 1, 8:24, :] for i in range(19)]
        blue = [pops_0[1, i, LX - 1, 8:24, :] for i in range(19)]
        red_mass = weighted_sum(red)
        blue_mass = weighted_sum(blue)
        inverse = 1.0 / (red_mass + blue_mass)
        mixed = [r + b for r, b in zip(red, blue)]
        for dim in range(3):
            prof[:, dim * CZ : (dim + 1) * CZ] = weighted_momentum(mixed, dim) * inverse
        prof[:, 3 * CZ :] = (red_mass - blue_mass) * inverse

    @pl.when(jnp.logical_not(is_nozzle))
    def _():
        pipe_loads[0].wait()
        for slot, field in enumerate((4, 1, 2, 3)):
            prof[:, slot * CZ : (slot + 1) * CZ] = fields_0[field, 2, 8:24, :]

    rows = prof[...]
    for slot in range(2):
        picked = jnp.dot(
            slot_rows[slot], rows, precision=lax.Precision.HIGHEST, preferred_element_type=F32
        )
        for part in range(4):
            route_out[:, slot * 4 + part, :] = picked[:, part * CZ : (part + 1) * CZ]

    pl.semaphore_wait(barrier, 8 + N_GY)

    def route(tile):
        return remote(
            route_out.at[tile],
            route_in.at[gy],
            send_sem.at[0],
            route_recv.at[0],
            (other, tile, gz),
        )

    def send_route(tile, carry):
        route(tile).start()
        return carry

    lax.fori_loop(0, N_GY, send_route, 0)

    def take_inflow():
        wait_rows(route_recv.at[0], ROUTE_ROWS)
        total = None
        for slot in range(2):
            arrived = jnp.concatenate(
                [route_in[:, slot * 4 + part, :] for part in range(4)], axis=1
            )
            term = jnp.dot(
                row_slots[slot],
                arrived,
                precision=lax.Precision.HIGHEST,
                preferred_element_type=F32,
            )
            total = term if total is None else total + term
        return [total[:, part * CZ : (part + 1) * CZ] for part in range(4)]

    @pl.when(jnp.logical_not(is_nozzle))
    def _():
        from_left = (lane & 3) < 2

        def group_copies(step, fields, group, count, kinds=range(4)):
            first_row = 2 + GROUP * group
            span = pl.ds(first_row, count)
            arrived = recv_sem.at[4 * step + (N_GROUPS - 1 - group) // 2]
            ends = [
                (fields.at[:, span, 22:24, :], fields.at[:, span, 6:8, :], (solver, up, gz)),
                (fields.at[:, span, 8:10, :], fields.at[:, span, 24:26, :], (solver, down, gz)),
                (zpack.at[step, group], zleft.at[step, group], (solver, gy, right)),
                (zpack.at[step, group], zright.at[step, group], (solver, gy, left)),
            ]
            return [
                remote(ends[k][0], ends[k][1], send_sem.at[0], arrived, ends[k][2]) for k in kinds
            ]

        def send_rows(group, count):
            for copy in group_copies(0, fields_0, group, count, (0, 1)):
                copy.start()

        def send_lanes(group, count):
            pack_first(group, count)
            for copy in group_copies(0, fields_0, group, count, (2, 3)):
                copy.start()

        out_fields = out_ref.reshape(5, FX, CY, CZ)

        def copy_out(groups):
            first_row = GROUP * groups[-1][0]
            span = pl.ds(first_row, sum(count for _, count in groups))
            return pltpu.make_async_copy(
                stage_pipe.at[:, span, :, :],
                out_fields.at[:, span, :, :],
                out_sem.at[0],
            )

        def split(value):
            high = value.astype(jnp.bfloat16)
            return [high, (value - high.astype(F32)).astype(jnp.bfloat16)]

        def moved_row(fields, along_z, place):
            centre, grad, smooth = [], [], []
            for field in range(5):
                low_x = fields[field, place - 1, 8:24, :]
                high_x = fields[field, place + 1, 8:24, :]
                d_x = (fields[field, place - 2, 8:24, :] - fields[field, place + 2, 8:24, :]) + (
                    8.0 * (high_x - low_x)
                )
                low_y = fields[field, place, 7:23, :]
                high_y = fields[field, place, 9:25, :]
                d_y = (fields[field, place, 6:22, :] - fields[field, place, 10:26, :]) + (
                    8.0 * (high_y - low_y)
                )
                d_z = along_z[field][:, 0:CZ]
                centre.append(fields[field, place, 8:24, :])
                grad.append((d_x, d_y, d_z))
                smooth.append(low_x + high_x + low_y + high_y + along_z[field][:, CZ:])
            scale = TIME_STEP / 12.0
            speed = [scale * centre[k] for k in (1, 2, 3)]
            lift = scale * jnp.exp((1.0 - centre[0]) * DENSITY_LOG)
            spread = TIME_STEP * DIFFUSION
            out = []
            for field in range(4):
                rate = (
                    speed[0] * grad[field][0]
                    + speed[1] * grad[field][1]
                    + speed[2] * grad[field][2]
                )
                if field > 0:
                    rate = rate + lift * grad[4][field - 1]
                out.append((1.0 - 6.0 * spread) * centre[field] + spread * smooth[field] - rate)
            rate = scale * (grad[1][0] + grad[2][1] + grad[3][2])
            out.append((1.0 - 6.0 * spread) * centre[4] + spread * smooth[4] - rate)
            return out

        def run_chunk(step, fields, groups):
            wait_rows(
                recv_sem.at[4 * step + (N_GROUPS - 1 - groups[0][0]) // 2],
                sum(2 * 2 * 5 * count + 2 * CY for _, count in groups),
            )
            lanes_in = []
            for group, count in groups:
                halo = jnp.where(from_left, zleft[step, group], zright[step, group])
                for row in range(count):
                    for field in range(5):
                        here = fields[field, 2 + GROUP * group + row, 8:24, :]
                        edge = pltpu.roll(halo, (-(4 * (5 * row + field) + 2)) % CZ, 1)
                        lanes_in.append(jnp.concatenate(split(here) + split(edge), axis=1))
            lanes_out = jnp.dot(
                jnp.concatenate(lanes_in, axis=0), band[...], preferred_element_type=F32
            )
            done = 0
            for group, count in groups:
                packed = jnp.zeros((CY, CZ), F32)
                for row in range(count):
                    along_z = [lanes_out[(done + k) * CY : (done + k + 1) * CY] for k in range(5)]
                    done += 5
                    place = GROUP * group + row
                    values = moved_row(fields, along_z, 2 + place)
                    for field in range(5):
                        if step == 0:
                            fields_1[field, 2 + place, 8:24, :] = values[field]
                            packed = pack_word(packed, values[field], 5 * row + field)
                        else:
                            stage_pipe[field, place] = 0.5 * (
                                fields_0[field, 2 + place, 8:24, :] + values[field]
                            )
                if step == 0:
                    zpack[1, group] = packed
                    for copy in group_copies(1, fields_1, group, count):
                        copy.start()
            if step == 1:
                copy_out(groups).start()

        for copy in pipe_loads[1:]:
            copy.wait()
        send_rows(N_GROUPS - 1, LAST_ROWS)

        def send_step(k, carry):
            send_rows(N_GROUPS - 2 - k, GROUP)
            return carry

        lax.fori_loop(0, N_GROUPS - 1, send_step, 0)
        send_lanes(N_GROUPS - 1, LAST_ROWS)

        def pack_step(k, carry):
            send_lanes(N_GROUPS - 2 - k, GROUP)
            return carry

        lax.fori_loop(0, N_GROUPS - 1, pack_step, 0)
        outlet_ghost(fields_0)
        lane_in = lax.broadcasted_iota(jnp.int32, (CZ, CZ), 0)
        lane_out = lax.broadcasted_iota(jnp.int32, (CZ, CZ), 1)
        ahead = lane_in - lane_out
        wrapped = jnp.where(
            ahead > 64, ahead - CZ, jnp.where(ahead < -64, ahead + CZ, jnp.zeros_like(ahead))
        )
        for part, apart in enumerate((ahead, wrapped)):
            near = (jnp.abs(apart) == 1).astype(F32)
            far = (jnp.abs(apart) == 2).astype(F32)
            slope = jnp.where(apart > 0, 8.0 * near - far, far - 8.0 * near)
            for copy in range(2):
                rows = slice((2 * part + copy) * CZ, (2 * part + copy + 1) * CZ)
                band[rows, 0:CZ] = slope.astype(jnp.bfloat16)
                band[rows, CZ:] = near.astype(jnp.bfloat16)

        run_chunk(0, fields_0, ((6, LAST_ROWS), (5, GROUP)))
        outlet_ghost(fields_1)

        def first_step(k, carry):
            run_chunk(0, fields_0, ((4 - 2 * k, GROUP), (3 - 2 * k, GROUP)))
            return carry

        lax.fori_loop(0, 2, first_step, 0)
        inflow = take_inflow()
        ghost = [0.5 * (1.0 + inflow[3]), inflow[0], inflow[1], inflow[2]]
        for place in range(2):
            for field in range(4):
                fields_0[field, place, 8:24, :] = ghost[field]
                fields_1[field, place, 8:24, :] = ghost[field]
            fields_0[4, place, 8:24, :] = fields_0[4, 2, 8:24, :]
        run_chunk(0, fields_0, ((0, GROUP),))
        for place in range(2):
            fields_1[4, place, 8:24, :] = fields_1[4, 2, 8:24, :]
        run_chunk(1, fields_1, ((6, LAST_ROWS), (5, GROUP)))

        def second_step(k, carry):
            run_chunk(1, fields_1, ((4 - 2 * k, GROUP), (3 - 2 * k, GROUP)))
            return carry

        lax.fori_loop(0, 2, second_step, 0)
        run_chunk(1, fields_1, ((0, GROUP),))

        pltpu.make_async_copy(stage_pipe, out_fields, out_sem.at[0]).wait()
        wait_rows(send_sem.at[0], ROUTE_ROWS + PIPE_ROWS)

    @pl.when(is_nozzle)
    def _():
        def face_copies(step, pops, rows):
            copies = []

            def add(src, dst, device):
                copies.append(remote(src, dst, send_sem.at[0], recv_sem.at[step], device))

            add(nz_plus.at[step], nz_left.at[step, 8:24, :], (solver, gy, right))
            add(nz_minus.at[step], nz_right.at[step, 8:24, :], (solver, gy, left))
            add(nz_plus.at[step, 8:16, :], nz_left.at[step, 0:8, :], (solver, up, right))
            add(nz_plus.at[step, 0:8, :], nz_left.at[step, 24:32, :], (solver, down, right))
            add(nz_minus.at[step, 8:16, :], nz_right.at[step, 0:8, :], (solver, up, left))
            add(nz_minus.at[step, 0:8, :], nz_right.at[step, 24:32, :], (solver, down, left))
            for i in PLUS_Y:
                add(pops.at[:, i, rows, 23:24, :], pops.at[:, i, rows, 7:8, :], (solver, up, gz))
            for i in MINUS_Y:
                add(pops.at[:, i, rows, 8:9, :], pops.at[:, i, rows, 24:25, :], (solver, down, gz))
            add(row_sums.at[step, 0], row_sums_in.at[step, 0], (solver, up, gz))
            add(row_sums.at[step, 1], row_sums_in.at[step, 1], (solver, down, gz))
            for side, row in ((0, up), (1, down)):
                for k, column in ((0, right), (1, left)):
                    add(
                        row_sums.at[step, side, 1 + k],
                        row_corners_in.at[step, side, k],
                        (solver, row, column),
                    )
            add(own_sums.at[step, 1], own_sums_in.at[step, 0], (solver, gy, right))
            add(own_sums.at[step, 2], own_sums_in.at[step, 1], (solver, gy, left))
            return copies

        def word_of(directions, i, colour, row):
            return (directions.index(i) * 2 + colour) * 6 + row

        def ghost_row(pops, phase_last):
            for i in range(19):
                pops[0, i, LX, 8:24, :] = (1.0 + phase_last) * ghost_eq[i]
                pops[1, i, LX, 8:24, :] = (1.0 - phase_last) * ghost_eq[i]

        def pack_faces(pops, rows, packed):
            packed_plus, packed_minus = packed
            for row in rows:
                for colour in range(2):
                    for i in PLUS_Z:
                        word = word_of(PLUS_Z, i, colour, row)
                        value = pltpu.roll(pops[colour, i, row, 8:24, :], word + 1, 1)
                        packed_plus = jnp.where(lane == word, value, packed_plus)
                    for i in MINUS_Z:
                        word = word_of(MINUS_Z, i, colour, row)
                        value = pops[colour, i, row, 8:24, :]
                        if word:
                            value = pltpu.roll(value, word, 1)
                        packed_minus = jnp.where(lane == word, value, packed_minus)
            return packed_plus, packed_minus

        def pack_classes(pops, cells, packed):
            packed_plus, packed_minus = packed
            for x in cells:
                for colour in range(2):
                    sums = []
                    for k, directions in enumerate(CLASSES):
                        value = part_sum(
                            directions,
                            lambda i: pops[
                                colour, i, min(max(x - VELOCITY_TABLE[i][0], 0), LX), 8:24, :
                            ],
                        )
                        class_sums[k, colour, x] = value
                        sums.append(value)
                    for k in range(3):
                        high = sums[3 * k] + pltpu.roll(sums[3 * k + 1], 1, 1)
                        low = sums[3 * k] + pltpu.roll(sums[3 * k + 2], CZ - 1, 1)
                        word = 64 + 20 * k + 10 * colour + 2 * x
                        packed_plus = jnp.where(
                            lane == word, pltpu.roll(high, word + 1, 1), packed_plus
                        )
                        packed_minus = jnp.where(
                            lane == word + 1, pltpu.roll(low, word + 1, 1), packed_minus
                        )
            return packed_plus, packed_minus

        def edge_rows(step):
            for colour in range(2):
                span = slice(8 * colour, 8 * colour + 8)
                for k in range(3):
                    row_sums[step, 0, k, span, :] = (
                        class_sums[k, colour, :, 15, :] + class_sums[3 + k, colour, :, 14, :]
                    )
                    row_sums[step, 1, k, span, :] = (
                        class_sums[k, colour, :, 0, :] + class_sums[6 + k, colour, :, 1, :]
                    )
                    own_sums[step, k, 0, span, :] = class_sums[6 + k, colour, :, 0, :]
                    own_sums[step, k, 1, span, :] = class_sums[3 + k, colour, :, 15, :]

        def pack(step, pops, rows, cells, packed):
            packed = pack_classes(pops, cells, pack_faces(pops, rows, packed))
            nz_plus[step], nz_minus[step] = packed

        def send_faces(step, pops, rows):
            edge_rows(step)
            copies = face_copies(step, pops, rows)
            for copy in copies:
                copy.start()

        def arrive(step, rows):
            wait_rows(recv_sem.at[step], FACE_ROWS + POP_ROWS * rows)

        def stream(step, pops, rows):
            for colour in range(2):
                for i in range(19):
                    shift_y, shift_z = VELOCITY_TABLE[i][1:]
                    span = slice(8 - shift_y, 24 - shift_y)
                    for row in rows:
                        value = pops[colour, i, row, span, :]
                        if shift_z == 1:
                            word = word_of(PLUS_Z, i, colour, row)
                            edge = nz_left[step, span, :]
                            if word:
                                edge = pltpu.roll(edge, CZ - word, 1)
                            value = jnp.where(lane == 0, edge, pltpu.roll(value, 1, 1))
                        elif shift_z == -1:
                            word = word_of(MINUS_Z, i, colour, row)
                            edge = pltpu.roll(nz_right[step, span, :], CZ - 1 - word, 1)
                            value = jnp.where(lane == CZ - 1, edge, pltpu.roll(value, CZ - 1, 1))
                        moved[colour, i, row] = value


        def read(colour, i, x):
            shift_x = VELOCITY_TABLE[i][0]
            return moved[colour, i, jnp.clip(x - shift_x, 0, LX)]

        def mass_step(k, carry):
            red = weighted_sum([read(0, i, k - 1) for i in range(19)])
            blue = weighted_sum([read(1, i, k - 1) for i in range(19)])
            masses[0, k] = red
            masses[1, k] = blue
            phase_buf[k, 8:24, :] = (red - blue) / (red + blue)
            return carry

        def phase_rows(step):
            for side, place in ((0, 7), (1, 24)):
                part = [row_sums_in[step, side, k] + own_sums[step, k, side] for k in range(3)]
                corner = [
                    row_corners_in[step, side, k] + own_sums_in[step, k, side] for k in range(2)
                ]
                edge_lane = lax.broadcasted_iota(jnp.int32, (16, CZ), 1)
                total = (
                    part[0]
                    + pltpu.roll(jnp.where(edge_lane == CZ - 1, corner[0], part[1]), 1, 1)
                    + pltpu.roll(jnp.where(edge_lane == 0, corner[1], part[2]), CZ - 1, 1)
                )
                red = total[0:8]
                blue = total[8:16]
                phase_buf[1 : 1 + LX, place, :] = ((red - blue) / (red + blue))[0:LX]
        def collide(step, pops, first, last):
            beside = [
                edges[step, 8:24, :]
                + pltpu.roll(edges[step, 7:23, :], CZ - 20, 1)
                + pltpu.roll(edges[step, 9:25, :], CZ - 40, 1)
                for edges in (nz_left, nz_right)
            ]
            beside = jnp.where((lane & 1) == 0, beside[0], beside[1])

            def side_mass(colour, x):
                def shifted(i):
                    shift_x, shift_y = VELOCITY_TABLE[i][0:2]
                    row = jnp.clip(x - shift_x, 0, LX)
                    return pops[colour, i, row, 8 - shift_y : 24 - shift_y, :]

                low = pltpu.roll(part_sum(MINUS_Z, shifted), CZ - 1, 1)
                high = pltpu.roll(part_sum(PLUS_Z, shifted), 1, 1)
                far = pltpu.roll(beside, CZ - 1 - (64 + 10 * colour + 2 * x), 1)
                return far + jnp.where(lane == CZ - 1, low, high)

            def collide_step(x, carry):
                red = masses[0, x + 1]
                blue = masses[1, x + 1]
                total = red + blue
                inverse = 1.0 / total
                mixed = [read(0, i, x) + read(1, i, x) for i in range(19)]
                vec = [weighted_momentum(mixed, dim) * inverse for dim in range(3)]
                balance = equilibrium_list(total, vec)
                here = phase_buf[x + 1, 8:24, :]
                side_red = side_mass(0, x)
                side_blue = side_mass(1, x)
                side = (side_red - side_blue) / (side_red + side_blue)
                low_z = pltpu.roll(jnp.where(lane == CZ - 1, side, here), 1, 1)
                high_z = pltpu.roll(jnp.where(lane == 0, side, here), CZ - 1, 1)
                grad = [
                    0.5 * (phase_buf[x + 2, 8:24, :] - phase_buf[x, 8:24, :]),
                    0.5 * (phase_buf[x + 1, 9:25, :] - phase_buf[x + 1, 7:23, :]),
                    0.5 * (high_z - low_z),
                ]
                grad_sq = grad[0] * grad[0] + grad[1] * grad[1] + grad[2] * grad[2]
                inverse_norm = 1.0 / jnp.sqrt(grad_sq + GRAD_FLOOR * GRAD_FLOOR)
                red_part = red * inverse
                tension = SURF_TENSION * inverse_norm
                level = tension * grad_sq * (1.0 / 3.0)
                split = SEGREGATION_BETA * (red_part * blue) * inverse_norm
                solid = solid_ref[x] != 0
                for i in range(19):
                    value = mixed[i] - (mixed[i] - balance[i]) * (1.0 / RELAX_TIME) - level
                    if i:
                        slope = along(i, grad)
                        value = value + tension * (slope * slope)
                        red_value = red_part * value + split * slope
                    else:
                        red_value = red_part * value
                    back = OPPOSITE_TABLE[i]
                    red_new = jnp.where(solid, read(0, back, x), red_value)
                    blue_new = jnp.where(solid, read(1, back, x), value - red_value)
                    if step < 2:
                        pops_1[0, i, x, 8:24, :] = red_new
                        pops_1[1, i, x, 8:24, :] = blue_new
                    else:
                        stage_nozzle[i, x] = red_new
                        stage_nozzle[19 + i, x] = blue_new
                if step >= 2:
                    copy_out(x).start()
                return carry

            lax.fori_loop(first, last, collide_step, 0)

        out_pops = out_ref.reshape(2 * 19, LX, CY, CZ)

        def copy_out(x):
            return pltpu.make_async_copy(
                stage_nozzle.at[:, pl.ds(x, 1), :, :],
                out_pops.at[:, pl.ds(x, 1), :, :],
                out_sem.at[0],
            )

        empty = (jnp.zeros((CY, CZ), F32), jnp.zeros((CY, CZ), F32))
        nozzle_loads[1].wait()
        solid_load.wait()
        pack(0, pops_0, range(LX), range(LX - 1), empty)
        send_faces(0, pops_0, slice(0, LX))
        inflow = take_inflow()
        outflow = equilibrium_list(jnp.exp(inflow[0]), inflow[1:])
        for i in range(19):
            ghost_eq[i] = 0.5 * outflow[i]
        ghost_row(pops_0, prof[:, 3 * CZ :])
        pack(1, pops_0, (LX,), (LX - 1,), (nz_plus[0], nz_minus[0]))
        send_faces(1, pops_0, slice(LX, LX + 1))
        arrive(0, LX)
        stream(0, pops_0, range(LX))
        lax.fori_loop(0, LX, mass_step, 0)
        phase_rows(0)
        collide(0, pops_0, 0, LX - 2)
        pack(2, pops_1, range(LX - 2), range(LX - 3), empty)
        send_faces(2, pops_1, slice(0, LX - 2))
        arrive(1, 1)
        stream(1, pops_0, (LX,))
        lax.fori_loop(LX, LX + 2, mass_step, 0)
        phase_rows(1)
        collide(1, pops_0, LX - 2, LX)
        red_last = weighted_sum([pops_1[0, i, LX - 1, 8:24, :] for i in range(19)])
        blue_last = weighted_sum([pops_1[1, i, LX - 1, 8:24, :] for i in range(19)])
        ghost_row(pops_1, (red_last - blue_last) / (red_last + blue_last))
        pack(3, pops_1, range(LX - 2, LX + 1), range(LX - 3, LX), (nz_plus[2], nz_minus[2]))
        send_faces(3, pops_1, slice(LX - 2, LX + 1))
        arrive(2, LX - 2)
        stream(2, pops_1, range(LX - 2))
        lax.fori_loop(0, LX - 2, mass_step, 0)
        phase_rows(2)
        collide(2, pops_1, 0, LX - 4)
        arrive(3, 3)
        stream(3, pops_1, range(LX - 2, LX + 1))
        lax.fori_loop(LX - 2, LX + 2, mass_step, 0)
        phase_rows(3)
        collide(3, pops_1, LX - 4, LX)
        pltpu.make_async_copy(stage_nozzle, out_pops, out_sem.at[0]).wait()
        wait_rows(send_sem.at[0], ROUTE_ROWS + NOZZLE_ROWS)


def on_device(coupled_state, solid_mask, inlet_source):
    words = coupled_state.shape[1]
    vmem = lambda *shape: pltpu.VMEM(shape, F32)
    in_hbm = lambda array: pltpu.with_memory_space_constraint(array, pltpu.HBM)
    dma = lambda *shape: pltpu.SemaphoreType.DMA(shape)
    out = pl.pallas_call(
        kernel,
        out_shape=pltpu.VMEM((words, CY, CZ), F32),
        in_specs=[
            pl.BlockSpec(memory_space=pltpu.HBM),
            pl.BlockSpec(memory_space=pltpu.HBM),
            pl.BlockSpec(memory_space=pltpu.HBM),
            pl.BlockSpec(memory_space=pltpu.HBM),
        ],
        out_specs=pl.BlockSpec(memory_space=pl.ANY),
        scratch_shapes=[
            vmem(5, FX, CY, CZ),
            vmem(2 * 19, LX, CY, CZ),
            pltpu.VMEM((LX, CY, CZ), jnp.int32),
            pltpu.VMEM((1, 256), jnp.int32),
            pltpu.VMEM((512, 256), jnp.bfloat16),
            vmem(CY, 4 * CZ),
            vmem(N_GY, 8, CZ),
            vmem(N_GY, 8, CZ),
            vmem(5, FX + 4, 32, CZ),
            vmem(5, FX + 4, 32, CZ),
            vmem(2, N_GROUPS, CY, CZ),
            vmem(2, N_GROUPS, CY, CZ),
            vmem(2, N_GROUPS, CY, CZ),
            vmem(2, 19, LX + 1, 32, CZ),
            vmem(2, 19, LX + 1, 32, CZ),
            vmem(2, 19, LX + 1, CY, CZ),
            vmem(2, LX + 2, CY, CZ),
            vmem(LX + 2, 32, CZ),
            vmem(19, CY, CZ),
            vmem(9, 2, 8, CY, CZ),
            vmem(4, CY, CZ),
            vmem(4, CY, CZ),
            vmem(4, 32, CZ),
            vmem(4, 32, CZ),
            vmem(4, 2, 3, 16, CZ),
            vmem(4, 3, 2, 16, CZ),
            vmem(4, 2, 3, 16, CZ),
            vmem(4, 2, 2, 16, CZ),
            vmem(4, 2, 2, 16, CZ),
            vmem(MOST_ROWS, CZ),
            dma(4),
            dma(1),
            dma(1),
            dma(1),
            dma(8),
        ],
        compiler_params=pltpu.CompilerParams(
            collective_id=0, has_side_effects=True, vmem_limit_bytes=40 << 20
        ),
    )(
        in_hbm(coupled_state.reshape(5, FX, CY, CZ)),
        in_hbm(coupled_state.reshape(2, 19, LX, CY, CZ)),
        in_hbm(solid_mask.reshape(LX, CY, CZ)),
        in_hbm(inlet_source),
    )
    return out.reshape(coupled_state.shape)


def solution(mesh):
    return jax.shard_map(
        on_device,
        mesh=mesh,
        in_specs=(P("solver", None, "gy", "gz", None), P(None, "gy", "gz", None), P("gz", None)),
        out_specs=P("solver", None, "gy", "gz", None),
        check_vma=False,
    )
```

```python
import math

import jax
import jax.numpy as jnp
from jax import lax
from jax.experimental import pallas as pl
from jax.experimental.pallas import tpu as pltpu
from jax.sharding import PartitionSpec as P

CY = 16
CZ = 128
LX = 5
FX = 38
N_GY = 16
N_GZ = 8
MESH = pl.DeviceIdType.MESH
F32 = jnp.float32

VELOCITY_TABLE = [
    (0, 0, 0),
    (1, 0, 0),
    (-1, 0, 0),
    (0, 1, 0),
    (0, -1, 0),
    (0, 0, 1),
    (0, 0, -1),
    (1, 1, 0),
    (-1, -1, 0),
    (1, -1, 0),
    (-1, 1, 0),
    (1, 0, 1),
    (-1, 0, -1),
    (1, 0, -1),
    (-1, 0, 1),
    (0, 1, 1),
    (0, -1, -1),
    (0, 1, -1),
    (0, -1, 1),
]
OPPOSITE_TABLE = [0, 2, 1, 4, 3, 6, 5, 8, 7, 10, 9, 12, 11, 14, 13, 16, 15, 18, 17]
RELAX_TIME = 0.8
SURF_TENSION = 0.02
SEGREGATION_BETA = 0.7
GRAD_FLOOR = 0.1
TIME_STEP = 0.2
VISCOSITY = 0.05
DIFFUSION = 0.05
DENSITY_LOG = math.log(2.0)

PLUS_Z = [i for i in range(19) if VELOCITY_TABLE[i][2] == 1]
MINUS_Z = [i for i in range(19) if VELOCITY_TABLE[i][2] == -1]
PLUS_Y = [i for i in range(19) if VELOCITY_TABLE[i][1] == 1]
SIGNS = (0, 1, -1)
CLASSES = [
    [i for i in range(19) if VELOCITY_TABLE[i][1:] == (sy, sz)] for sy in SIGNS for sz in SIGNS
]
MINUS_Y = [i for i in range(19) if VELOCITY_TABLE[i][1] == -1]

GROUP = 6
N_GROUPS = 7
LAST_ROWS = FX - GROUP * (N_GROUPS - 1)
CHUNKS = (
    ((6, LAST_ROWS), (5, GROUP)),
    ((4, GROUP), (3, GROUP)),
    ((2, GROUP), (1, GROUP)),
    ((0, GROUP),),
)


ROUTE_ROWS = 8 * N_GY
PIPE_ROWS = 2 * (2 * 2 * 5 * FX + 2 * CY * N_GROUPS)
FACE_ROWS = 2 * 2 * CY + 4 * 2 * 8 + 2 * 3 * 16 + 4 * 16 + 2 * 2 * 16
POP_ROWS = 2 * 5 * 2
NOZZLE_ROWS = 4 * FACE_ROWS + POP_ROWS * 2 * (LX + 1)
MOST_ROWS = ROUTE_ROWS + max(PIPE_ROWS, NOZZLE_ROWS)


def weighted_sum(values):
    faces = values[1]
    for i in range(2, 7):
        faces = faces + values[i]
    edges = values[7]
    for i in range(8, 19):
        edges = edges + values[i]
    return values[0] * (1.0 / 3.0) + faces * (1.0 / 18.0) + edges * (1.0 / 36.0)


def clip_row(row):
    return min(max(row, 0), LX) if isinstance(row, int) else jnp.clip(row, 0, LX)


def weight_of(i):
    return 1.0 / 3.0 if i == 0 else (1.0 / 18.0 if i < 7 else 1.0 / 36.0)


def part_sum(directions, read):
    total = None
    for weight in (1.0 / 3.0, 1.0 / 18.0, 1.0 / 36.0):
        values = [read(i) for i in directions if weight_of(i) == weight]
        if values:
            group = values[0]
            for value in values[1:]:
                group = group + value
            total = weight * group if total is None else total + weight * group
    return total


def weighted_momentum(values, dim):
    faces = None
    edges = None
    for i in range(1, 19):
        sign = VELOCITY_TABLE[i][dim]
        if sign == 0:
            continue
        if i < 7:
            faces = (
                values[i]
                if faces is None
                else (faces + values[i] if sign > 0 else faces - values[i])
            )
        else:
            edges = (
                values[i]
                if edges is None
                else (edges + values[i] if sign > 0 else edges - values[i])
            )
    return faces * (1.0 / 18.0) + edges * (1.0 / 36.0)


def along(direction, vec):
    total = None
    for sign, part in zip(VELOCITY_TABLE[direction], vec):
        if sign == 0:
            continue
        if total is None:
            total = part if sign > 0 else -part
        else:
            total = total + part if sign > 0 else total - part
    return total


def equilibrium_list(density, vec):
    speed_sq = vec[0] * vec[0] + vec[1] * vec[1] + vec[2] * vec[2]
    rest = density * (1.0 - 1.5 * speed_sq)
    out = [rest]
    for i in range(1, 19, 2):
        proj = along(i, vec)
        even = rest + (4.5 * density) * (proj * proj)
        odd = (3.0 * density) * proj
        out += [even + odd, even - odd]
    return out


def kernel(
    pipe_in,
    nozzle_in,
    solid_in,
    inlet_in,
    out_ref,
    stage_pipe,
    stage_nozzle,
    solid_ref,
    inlet_ref,
    band,
    prof,
    route_out,
    route_in,
    fields_0,
    fields_1,
    zpack,
    zleft,
    zright,
    pops_0,
    pops_1,
    moved,
    masses,
    phase_buf,
    ghost_eq,
    slopes,
    class_sums,
    nz_out,
    nz_left,
    nz_right,
    row_sums,
    own_sums,
    row_sums_in,
    row_corners_in,
    own_sums_in,
    tally,
    in_sem,
    out_sem,
    send_sem,
    route_recv,
    recv_sem,
):
    solver = lax.axis_index("solver")
    gy = lax.axis_index("gy")
    gz = lax.axis_index("gz")
    other = 1 - solver
    up = lax.rem(gy + 1, N_GY)
    down = lax.rem(gy + N_GY - 1, N_GY)
    right = lax.rem(gz + 1, N_GZ)
    left = lax.rem(gz + N_GZ - 1, N_GZ)
    is_nozzle = solver == 0
    inlet_load = pltpu.make_async_copy(inlet_in, inlet_ref, in_sem.at[1])
    inlet_load.start()
    barrier = pltpu.get_barrier_semaphore()
    for device in (
        (solver, up, gz),
        (solver, down, gz),
        (solver, gy, right),
        (solver, gy, left),
        (solver, up, right),
        (solver, up, left),
        (solver, down, right),
        (solver, down, left),
    ):
        pl.semaphore_signal(barrier, inc=1, device_id=device, device_id_type=MESH)

    def greet(tile, carry):
        pl.semaphore_signal(barrier, inc=1, device_id=(other, tile, gz), device_id_type=MESH)
        return carry

    lax.fori_loop(0, N_GY, greet, 0)

    lane = lax.broadcasted_iota(jnp.int32, (CY, CZ), 1)

    def remote(src, dst, send_sem, recv_sem, device):
        return pltpu.make_async_remote_copy(
            src_ref=src,
            dst_ref=dst,
            send_sem=send_sem,
            recv_sem=recv_sem,
            device_id=device,
            device_id_type=MESH,
        )

    def wait_rows(sem, rows):
        part = tally.at[0:rows, :]
        pltpu.make_async_copy(part, part, sem).wait()

    solid_load = pltpu.make_async_copy(solid_in, solid_ref, in_sem.at[2])
    lane_word = lax.shift_right_logical(lane, 2)

    def pack_word(packed, value, word):
        return jnp.where(lane_word == word, pltpu.roll(value, (4 * word + 2) % CZ, 1), packed)

    def pack_first(group, count):
        packed = jnp.zeros((CY, CZ), F32)
        for row in range(count):
            for field in range(5):
                value = fields_0[field, 2 + GROUP * group + row, 8:24, :]
                packed = pack_word(packed, value, 5 * row + field)
        zpack[0, group] = packed

    def outlet_ghost(fields):
        for field in range(5):
            end = fields[field, 1 + FX, 8:24, :]
            fields[field, 2 + FX, 8:24, :] = end
            fields[field, 3 + FX, 8:24, :] = end

    nozzle_loads = [
        pltpu.make_async_copy(
            nozzle_in.at[:, :, rows, :, :], pops_0.at[:, :, rows, 8:24, :], in_sem.at[k]
        )
        for k, rows in ((0, slice(LX - 1, LX)), (3, slice(0, LX - 1)))
    ]
    pipe_loads = [
        pltpu.make_async_copy(
            pipe_in.at[part, rows, :, :],
            fields_0.at[part, slice(rows.start + 2, rows.stop + 2), 8:24, :],
            in_sem.at[k],
        )
        for k, part, rows in (
            (0, slice(1, 5), slice(0, 1)),
            (2, slice(0, 5), slice(1, FX)),
            (3, slice(0, 1), slice(0, 1)),
        )
    ]

    @pl.when(is_nozzle)
    def _():
        for copy in nozzle_loads:
            copy.start()
        solid_load.start()

    @pl.when(jnp.logical_not(is_nozzle))
    def _():
        for copy in pipe_loads:
            copy.start()

    inlet_load.wait()
    source = inlet_ref[...]
    row_ids = lax.broadcasted_iota(jnp.int32, (1, 256), 1)
    tile_rows = lax.broadcasted_iota(jnp.int32, (N_GY, 256), 0)
    source_tile = lax.shift_right_logical(source, 4)
    target_tile = lax.shift_right_logical(row_ids, 4)
    member = (tile_rows == source_tile).astype(jnp.bfloat16)
    first = lax.broadcasted_iota(jnp.int32, (256, 256), 0)
    second = lax.broadcasted_iota(jnp.int32, (256, 256), 1)
    before = (
        (first < second)
        & (lax.shift_right_logical(first, 4) == lax.shift_right_logical(second, 4))
    ).astype(jnp.bfloat16)
    counts = jnp.dot(member, before, preferred_element_type=F32)
    rank = jnp.sum(counts * member.astype(F32), axis=0, keepdims=True)
    far_tile = jnp.where(is_nozzle, target_tile, source_tile)
    local_row = jnp.where(is_nozzle, source, row_ids)
    mine = (local_row == tile_rows + gy * CY).astype(jnp.bfloat16)
    slot_rows = []
    row_slots = []
    for slot in range(2):
        taken = ((far_tile == tile_rows) & (rank == float(slot))).astype(jnp.bfloat16)
        dims = (((1,), (1,)), ((), ()))
        slot_rows.append(lax.dot_general(taken, mine, dims, preferred_element_type=F32))
        row_slots.append(lax.dot_general(mine, taken, dims, preferred_element_type=F32))

    @pl.when(is_nozzle)
    def _():
        nozzle_loads[0].wait()
        red = [pops_0[0, i, LX - 1, 8:24, :] for i in range(19)]
        blue = [pops_0[1, i, LX - 1, 8:24, :] for i in range(19)]
        red_mass = weighted_sum(red)
        blue_mass = weighted_sum(blue)
        inverse = 1.0 / (red_mass + blue_mass)
        mixed = [r + b for r, b in zip(red, blue)]
        for dim in range(3):
            prof[:, dim * CZ : (dim + 1) * CZ] = weighted_momentum(mixed, dim) * inverse
        prof[:, 3 * CZ :] = (red_mass - blue_mass) * inverse

    @pl.when(jnp.logical_not(is_nozzle))
    def _():
        pipe_loads[0].wait()
        for slot, field in enumerate((4, 1, 2, 3)):
            prof[:, slot * CZ : (slot + 1) * CZ] = fields_0[field, 2, 8:24, :]

    rows = prof[...]
    for slot in range(2):
        picked = jnp.dot(
            slot_rows[slot], rows, precision=lax.Precision.HIGHEST, preferred_element_type=F32
        )
        for part in range(4):
            route_out[:, slot * 4 + part, :] = picked[:, part * CZ : (part + 1) * CZ]

    pl.semaphore_wait(barrier, 8 + N_GY)

    def route(tile):
        return remote(
            route_out.at[tile],
            route_in.at[gy],
            send_sem.at[0],
            route_recv.at[0],
            (other, tile, gz),
        )

    def send_route(tile, carry):
        route(tile).start()
        return carry

    lax.fori_loop(0, N_GY, send_route, 0)

    def take_inflow():
        wait_rows(route_recv.at[0], ROUTE_ROWS)
        total = None
        for slot in range(2):
            arrived = jnp.concatenate(
                [route_in[:, slot * 4 + part, :] for part in range(4)], axis=1
            )
            term = jnp.dot(
                row_slots[slot],
                arrived,
                precision=lax.Precision.HIGHEST,
                preferred_element_type=F32,
            )
            total = term if total is None else total + term
        return [total[:, part * CZ : (part + 1) * CZ] for part in range(4)]

    @pl.when(jnp.logical_not(is_nozzle))
    def _():
        from_left = (lane & 3) < 2

        def group_copies(step, fields, group, count, kinds=range(4)):
            first_row = 2 + GROUP * group
            span = pl.ds(first_row, count)
            arrived = recv_sem.at[4 * step + (N_GROUPS - 1 - group) // 2]
            ends = [
                (fields.at[:, span, 22:24, :], fields.at[:, span, 6:8, :], (solver, up, gz)),
                (fields.at[:, span, 8:10, :], fields.at[:, span, 24:26, :], (solver, down, gz)),
                (zpack.at[step, group], zleft.at[step, group], (solver, gy, right)),
                (zpack.at[step, group], zright.at[step, group], (solver, gy, left)),
            ]
            return [
                remote(ends[k][0], ends[k][1], send_sem.at[0], arrived, ends[k][2]) for k in kinds
            ]

        def send_rows(group, count):
            for copy in group_copies(0, fields_0, group, count, (0, 1)):
                copy.start()

        def send_lanes(group, count):
            pack_first(group, count)
            for copy in group_copies(0, fields_0, group, count, (2, 3)):
                copy.start()

        out_fields = out_ref.reshape(5, FX, CY, CZ)

        def copy_out(groups):
            first_row = GROUP * groups[-1][0]
            span = pl.ds(first_row, sum(count for _, count in groups))
            return pltpu.make_async_copy(
                stage_pipe.at[:, span, :, :],
                out_fields.at[:, span, :, :],
                out_sem.at[0],
            )

        def split(value):
            high = value.astype(jnp.bfloat16)
            return [high, (value - high.astype(F32)).astype(jnp.bfloat16)]

        def moved_row(fields, along_z, place):
            centre, grad, smooth = [], [], []
            for field in range(5):
                low_x = fields[field, place - 1, 8:24, :]
                high_x = fields[field, place + 1, 8:24, :]
                d_x = (fields[field, place - 2, 8:24, :] - fields[field, place + 2, 8:24, :]) + (
                    8.0 * (high_x - low_x)
                )
                low_y = fields[field, place, 7:23, :]
                high_y = fields[field, place, 9:25, :]
                d_y = (fields[field, place, 6:22, :] - fields[field, place, 10:26, :]) + (
                    8.0 * (high_y - low_y)
                )
                d_z = along_z[field][:, 0:CZ]
                centre.append(fields[field, place, 8:24, :])
                grad.append((d_x, d_y, d_z))
                smooth.append(low_x + high_x + low_y + high_y + along_z[field][:, CZ:])
            scale = TIME_STEP / 12.0
            speed = [scale * centre[k] for k in (1, 2, 3)]
            lift = scale * jnp.exp((1.0 - centre[0]) * DENSITY_LOG)
            spread = TIME_STEP * DIFFUSION
            out = []
            for field in range(4):
                rate = (
                    speed[0] * grad[field][0]
                    + speed[1] * grad[field][1]
                    + speed[2] * grad[field][2]
                )
                if field > 0:
                    rate = rate + lift * grad[4][field - 1]
                out.append((1.0 - 6.0 * spread) * centre[field] + spread * smooth[field] - rate)
            rate = scale * (grad[1][0] + grad[2][1] + grad[3][2])
            out.append((1.0 - 6.0 * spread) * centre[4] + spread * smooth[4] - rate)
            return out

        def run_chunk(step, fields, groups):
            wait_rows(
                recv_sem.at[4 * step + (N_GROUPS - 1 - groups[0][0]) // 2],
                sum(2 * 2 * 5 * count + 2 * CY for _, count in groups),
            )
            lanes_in = []
            for group, count in groups:
                halo = jnp.where(from_left, zleft[step, group], zright[step, group])
                for row in range(count):
                    for field in range(5):
                        here = fields[field, 2 + GROUP * group + row, 8:24, :]
                        edge = pltpu.roll(halo, (-(4 * (5 * row + field) + 2)) % CZ, 1)
                        lanes_in.append(jnp.concatenate(split(here) + split(edge), axis=1))
            lanes_out = jnp.dot(
                jnp.concatenate(lanes_in, axis=0), band[...], preferred_element_type=F32
            )
            done = 0
            for group, count in groups:
                packed = jnp.zeros((CY, CZ), F32)
                for row in range(count):
                    along_z = [lanes_out[(done + k) * CY : (done + k + 1) * CY] for k in range(5)]
                    done += 5
                    place = GROUP * group + row
                    values = moved_row(fields, along_z, 2 + place)
                    for field in range(5):
                        if step == 0:
                            fields_1[field, 2 + place, 8:24, :] = values[field]
                            packed = pack_word(packed, values[field], 5 * row + field)
                        else:
                            stage_pipe[field, place] = 0.5 * (
                                fields_0[field, 2 + place, 8:24, :] + values[field]
                            )
                if step == 0:
                    zpack[1, group] = packed
                    for copy in group_copies(1, fields_1, group, count):
                        copy.start()
            if step == 1:
                copy_out(groups).start()

        for copy in pipe_loads[1:]:
            copy.wait()
        send_rows(N_GROUPS - 1, LAST_ROWS)

        def send_step(k, carry):
            send_rows(N_GROUPS - 2 - k, GROUP)
            return carry

        lax.fori_loop(0, N_GROUPS - 1, send_step, 0)
        send_lanes(N_GROUPS - 1, LAST_ROWS)

        def pack_step(k, carry):
            send_lanes(N_GROUPS - 2 - k, GROUP)
            return carry

        lax.fori_loop(0, N_GROUPS - 1, pack_step, 0)
        outlet_ghost(fields_0)
        lane_in = lax.broadcasted_iota(jnp.int32, (CZ, CZ), 0)
        lane_out = lax.broadcasted_iota(jnp.int32, (CZ, CZ), 1)
        ahead = lane_in - lane_out
        wrapped = jnp.where(
            ahead > 64, ahead - CZ, jnp.where(ahead < -64, ahead + CZ, jnp.zeros_like(ahead))
        )
        for part, apart in enumerate((ahead, wrapped)):
            near = (jnp.abs(apart) == 1).astype(F32)
            far = (jnp.abs(apart) == 2).astype(F32)
            slope = jnp.where(apart > 0, 8.0 * near - far, far - 8.0 * near)
            for copy in range(2):
                rows = slice((2 * part + copy) * CZ, (2 * part + copy + 1) * CZ)
                band[rows, 0:CZ] = slope.astype(jnp.bfloat16)
                band[rows, CZ:] = near.astype(jnp.bfloat16)

        run_chunk(0, fields_0, ((6, LAST_ROWS), (5, GROUP)))
        outlet_ghost(fields_1)

        def first_step(k, carry):
            run_chunk(0, fields_0, ((4 - 2 * k, GROUP), (3 - 2 * k, GROUP)))
            return carry

        lax.fori_loop(0, 2, first_step, 0)
        inflow = take_inflow()
        ghost = [0.5 * (1.0 + inflow[3]), inflow[0], inflow[1], inflow[2]]
        for place in range(2):
            for field in range(4):
                fields_0[field, place, 8:24, :] = ghost[field]
                fields_1[field, place, 8:24, :] = ghost[field]
            fields_0[4, place, 8:24, :] = fields_0[4, 2, 8:24, :]
        run_chunk(0, fields_0, ((0, GROUP),))
        for place in range(2):
            fields_1[4, place, 8:24, :] = fields_1[4, 2, 8:24, :]
        run_chunk(1, fields_1, ((6, LAST_ROWS), (5, GROUP)))

        def second_step(k, carry):
            run_chunk(1, fields_1, ((4 - 2 * k, GROUP), (3 - 2 * k, GROUP)))
            return carry

        lax.fori_loop(0, 2, second_step, 0)
        run_chunk(1, fields_1, ((0, GROUP),))

        pltpu.make_async_copy(stage_pipe, out_fields, out_sem.at[0]).wait()
        wait_rows(send_sem.at[0], ROUTE_ROWS + PIPE_ROWS)

    @pl.when(is_nozzle)
    def _():
        def face_copies(step, pops, rows):
            copies = []

            def add(src, dst, device):
                copies.append(remote(src, dst, send_sem.at[0], recv_sem.at[step], device))

            low, high = slice(0, 8), slice(8, 16)
            for k, column, edges in ((0, right, nz_left), (1, left, nz_right)):
                for side, row, part, place in ((0, up, high, 0), (1, down, low, 24)):
                    add(
                        nz_out.at[step, :, part, :],
                        edges.at[step, :, place : place + 8, :],
                        (solver, row, column),
                    )
                    add(
                        row_sums.at[step, side, 1 + k],
                        row_corners_in.at[step, side, k],
                        (solver, row, column),
                    )
            for i in PLUS_Y:
                add(pops.at[:, i, rows, 23:24, :], pops.at[:, i, rows, 7:8, :], (solver, up, gz))
            for i in MINUS_Y:
                add(pops.at[:, i, rows, 8:9, :], pops.at[:, i, rows, 24:25, :], (solver, down, gz))
            add(row_sums.at[step, 0], row_sums_in.at[step, 0], (solver, up, gz))
            add(row_sums.at[step, 1], row_sums_in.at[step, 1], (solver, down, gz))
            for k, column, edges in ((0, right, nz_left), (1, left, nz_right)):
                add(nz_out.at[step], edges.at[step, :, 8:24, :], (solver, gy, column))
                add(own_sums.at[step, 1 + k], own_sums_in.at[step, k], (solver, gy, column))
            return copies

        def lane_of(directions, i, colour, row):
            return 2 * ((directions.index(i) * 2 + colour) * 6 + row) + (directions is MINUS_Z)

        def ghost_row(pops, phase_last):
            for i in range(19):
                pops[0, i, LX, 8:24, :] = (1.0 + phase_last) * ghost_eq[i]
                pops[1, i, LX, 8:24, :] = (1.0 - phase_last) * ghost_eq[i]

        def pack_faces(pops, rows, packed):
            lane_pair = lax.shift_right_logical(lane, 1)
            for row in rows:
                for colour in range(2):
                    for k in range(5):
                        pair = (k * 2 + colour) * 6 + row
                        value = jnp.where(
                            lane < CZ // 2,
                            pops[colour, MINUS_Z[k], row, 8:24, :],
                            pops[colour, PLUS_Z[k], row, 8:24, :],
                        )
                        value = pltpu.roll(value, 2 * pair + 1, 1)
                        packed = jnp.where(lane_pair == pair, value, packed)
            return packed

        def pack_classes(pops, cells, packed):
            for x in cells:
                for colour in range(2):
                    sums = []
                    for k, directions in enumerate(CLASSES):
                        value = part_sum(
                            directions,
                            lambda i: pops[
                                colour, i, min(max(x - VELOCITY_TABLE[i][0], 0), LX), 8:24, :
                            ],
                        )
                        class_sums[k, colour, x] = value
                        sums.append(value)
                    for k in range(3):
                        word = 10 * k + 5 * colour + x
                        value = jnp.where(
                            lane == 126,
                            sums[3 * k + 1],
                            jnp.where(lane == 1, sums[3 * k + 2], sums[3 * k]),
                        )
                        value = pltpu.roll(value, 4 * word + 2, 1)
                        packed = jnp.where(lane_word == word, value, packed)
            return packed

        def edge_rows(step):
            for colour in range(2):
                span = slice(8 * colour, 8 * colour + 8)
                for k in range(3):
                    row_sums[step, 0, k, span, :] = (
                        class_sums[k, colour, :, 15, :] + class_sums[3 + k, colour, :, 14, :]
                    )
                    row_sums[step, 1, k, span, :] = (
                        class_sums[k, colour, :, 0, :] + class_sums[6 + k, colour, :, 1, :]
                    )
                    own_sums[step, k, 0, span, :] = class_sums[6 + k, colour, :, 0, :]
                    own_sums[step, k, 1, span, :] = class_sums[3 + k, colour, :, 15, :]

        def pack(step, pops, rows, cells, packed):
            nz_out[step, 0] = pack_faces(pops, rows, packed[0])
            nz_out[step, 1] = pack_classes(pops, cells, packed[1])

        def send_faces(step, pops, rows):
            edge_rows(step)
            copies = face_copies(step, pops, rows)
            for copy in copies:
                copy.start()

        def arrive(step, rows):
            wait_rows(recv_sem.at[step], FACE_ROWS + POP_ROWS * rows)

        def stream(step, pops, rows):
            for colour in range(2):
                for i in range(19):
                    shift_y, shift_z = VELOCITY_TABLE[i][1:]
                    span = slice(8 - shift_y, 24 - shift_y)
                    for row in rows:
                        value = pops[colour, i, row, span, :]
                        if shift_z == 1:
                            place = lane_of(PLUS_Z, i, colour, row)
                            edge = nz_left[step, 0, span, :]
                            if place:
                                edge = pltpu.roll(edge, CZ - place, 1)
                            value = jnp.where(lane == 0, edge, pltpu.roll(value, 1, 1))
                        elif shift_z == -1:
                            place = lane_of(MINUS_Z, i, colour, row)
                            edge = pltpu.roll(nz_right[step, 0, span, :], CZ - 1 - place, 1)
                            value = jnp.where(lane == CZ - 1, edge, pltpu.roll(value, CZ - 1, 1))
                        moved[colour, i, row] = value


        def read(colour, i, x):
            shift_x = VELOCITY_TABLE[i][0]
            return moved[colour, i, clip_row(x - shift_x)]

        def mass_step(k, carry):
            red = weighted_sum([read(0, i, k - 1) for i in range(19)])
            blue = weighted_sum([read(1, i, k - 1) for i in range(19)])
            masses[0, k] = red
            masses[1, k] = blue
            phase_buf[k, 8:24, :] = (red - blue) / (red + blue)
            return carry

        def phase_rows(step):
            for side, place in ((0, 7), (1, 24)):
                part = [row_sums_in[step, side, k] + own_sums[step, k, side] for k in range(3)]
                corner = [
                    row_corners_in[step, side, k] + own_sums_in[step, k, side] for k in range(2)
                ]
                edge_lane = lax.broadcasted_iota(jnp.int32, (16, CZ), 1)
                total = (
                    part[0]
                    + pltpu.roll(jnp.where(edge_lane == CZ - 1, corner[0], part[1]), 1, 1)
                    + pltpu.roll(jnp.where(edge_lane == 0, corner[1], part[2]), CZ - 1, 1)
                )
                red = total[0:8]
                blue = total[8:16]
                phase_buf[1 : 1 + LX, place, :] = ((red - blue) / (red + blue))[0:LX]
        def collide(step, pops, first, last):
            beside = None
            for k, span in enumerate((slice(8, 24), slice(7, 23), slice(9, 25))):
                both = jnp.where(
                    (lane & 3) < 2, nz_left[step, 1, span, :], nz_right[step, 1, span, :]
                )
                beside = both if k == 0 else beside + pltpu.roll(both, CZ - 40 * k, 1)
            beside = beside + jnp.where(
                (lane & 3) < 2, pltpu.roll(beside, 1, 1), pltpu.roll(beside, CZ - 1, 1)
            )

            def side_mass(colour, x):
                def shifted(i):
                    shift_x, shift_y = VELOCITY_TABLE[i][0:2]
                    row = clip_row(x - shift_x)
                    return pops[colour, i, row, 8 - shift_y : 24 - shift_y, :]

                low = pltpu.roll(part_sum(MINUS_Z, shifted), CZ - 1, 1)
                high = pltpu.roll(part_sum(PLUS_Z, shifted), 1, 1)
                far = pltpu.roll(beside, CZ - 2 - 4 * (5 * colour + x), 1)
                return far + jnp.where(lane == CZ - 1, low, high)

            def slope_step(x):
                here = phase_buf[x + 1, 8:24, :]
                side_red = side_mass(0, x)
                side_blue = side_mass(1, x)
                side = (side_red - side_blue) / (side_red + side_blue)
                low_z = pltpu.roll(jnp.where(lane == CZ - 1, side, here), 1, 1)
                high_z = pltpu.roll(jnp.where(lane == 0, side, here), CZ - 1, 1)
                grad = [
                    0.5 * (phase_buf[x + 2, 8:24, :] - phase_buf[x, 8:24, :]),
                    0.5 * (phase_buf[x + 1, 9:25, :] - phase_buf[x + 1, 7:23, :]),
                    0.5 * (high_z - low_z),
                ]
                for dim in range(3):
                    slopes[dim, x] = grad[dim]

            def collide_step(x, carry):
                red = masses[0, x + 1]
                blue = masses[1, x + 1]
                total = red + blue
                inverse = 1.0 / total
                mixed = [read(0, i, x) + read(1, i, x) for i in range(19)]
                vec = [weighted_momentum(mixed, dim) * inverse for dim in range(3)]
                balance = equilibrium_list(total, vec)
                grad = [slopes[dim, x] for dim in range(3)]
                grad_sq = grad[0] * grad[0] + grad[1] * grad[1] + grad[2] * grad[2]
                inverse_norm = 1.0 / jnp.sqrt(grad_sq + GRAD_FLOOR * GRAD_FLOOR)
                red_part = red * inverse
                tension = SURF_TENSION * inverse_norm
                level = tension * grad_sq * (1.0 / 3.0)
                split = SEGREGATION_BETA * (red_part * blue) * inverse_norm
                solid = solid_ref[x] != 0
                for i in range(19):
                    value = mixed[i] - (mixed[i] - balance[i]) * (1.0 / RELAX_TIME) - level
                    if i:
                        slope = along(i, grad)
                        value = value + tension * (slope * slope)
                        red_value = red_part * value + split * slope
                    else:
                        red_value = red_part * value
                    back = OPPOSITE_TABLE[i]
                    red_new = jnp.where(solid, read(0, back, x), red_value)
                    blue_new = jnp.where(solid, read(1, back, x), value - red_value)
                    if step < 2:
                        pops_1[0, i, x, 8:24, :] = red_new
                        pops_1[1, i, x, 8:24, :] = blue_new
                    else:
                        stage_nozzle[i, x] = red_new
                        stage_nozzle[19 + i, x] = blue_new
                if step >= 2:
                    copy_out(x).start()
                return carry

            for x in range(first, last):
                slope_step(x)
            for x in range(first, last):
                collide_step(x, 0)

        out_pops = out_ref.reshape(2 * 19, LX, CY, CZ)

        def copy_out(x):
            return pltpu.make_async_copy(
                stage_nozzle.at[:, pl.ds(x, 1), :, :],
                out_pops.at[:, pl.ds(x, 1), :, :],
                out_sem.at[0],
            )

        empty = (jnp.zeros((CY, CZ), F32), jnp.zeros((CY, CZ), F32))
        nozzle_loads[1].wait()
        solid_load.wait()
        pack(0, pops_0, range(LX), range(LX - 1), empty)
        send_faces(0, pops_0, slice(0, LX))
        inflow = take_inflow()
        outflow = equilibrium_list(jnp.exp(inflow[0]), inflow[1:])
        for i in range(19):
            ghost_eq[i] = 0.5 * outflow[i]
        ghost_row(pops_0, prof[:, 3 * CZ :])
        pack(1, pops_0, (LX,), (LX - 1,), nz_out[0])
        send_faces(1, pops_0, slice(LX, LX + 1))
        arrive(0, LX)
        stream(0, pops_0, range(LX))
        lax.fori_loop(0, LX, mass_step, 0)
        phase_rows(0)
        collide(0, pops_0, 0, LX - 2)
        pack(2, pops_1, range(LX - 2), range(LX - 3), empty)
        send_faces(2, pops_1, slice(0, LX - 2))
        arrive(1, 1)
        stream(1, pops_0, (LX,))
        for k in range(LX, LX + 2):
            mass_step(k, 0)
        phase_rows(1)
        collide(1, pops_0, LX - 2, LX)
        red_last = weighted_sum([pops_1[0, i, LX - 1, 8:24, :] for i in range(19)])
        blue_last = weighted_sum([pops_1[1, i, LX - 1, 8:24, :] for i in range(19)])
        ghost_row(pops_1, (red_last - blue_last) / (red_last + blue_last))
        pack(3, pops_1, range(LX - 2, LX + 1), range(LX - 3, LX), nz_out[2])
        send_faces(3, pops_1, slice(LX - 2, LX + 1))
        arrive(2, LX - 2)
        stream(2, pops_1, range(LX - 2))
        lax.fori_loop(0, LX - 2, mass_step, 0)
        phase_rows(2)
        collide(2, pops_1, 0, LX - 4)
        arrive(3, 3)
        stream(3, pops_1, range(LX - 2, LX + 1))
        for k in range(LX - 2, LX + 2):
            mass_step(k, 0)
        phase_rows(3)
        collide(3, pops_1, LX - 4, LX)
        pltpu.make_async_copy(stage_nozzle, out_pops, out_sem.at[0]).wait()
        wait_rows(send_sem.at[0], ROUTE_ROWS + NOZZLE_ROWS)


def on_device(coupled_state, solid_mask, inlet_source):
    words = coupled_state.shape[1]
    vmem = lambda *shape: pltpu.VMEM(shape, F32)
    in_hbm = lambda array: pltpu.with_memory_space_constraint(array, pltpu.HBM)
    dma = lambda *shape: pltpu.SemaphoreType.DMA(shape)
    out = pl.pallas_call(
        kernel,
        out_shape=pltpu.VMEM((words, CY, CZ), F32),
        in_specs=[
            pl.BlockSpec(memory_space=pltpu.HBM),
            pl.BlockSpec(memory_space=pltpu.HBM),
            pl.BlockSpec(memory_space=pltpu.HBM),
            pl.BlockSpec(memory_space=pltpu.HBM),
        ],
        out_specs=pl.BlockSpec(memory_space=pl.ANY),
        scratch_shapes=[
            vmem(5, FX, CY, CZ),
            vmem(2 * 19, LX, CY, CZ),
            pltpu.VMEM((LX, CY, CZ), jnp.int32),
            pltpu.VMEM((1, 256), jnp.int32),
            pltpu.VMEM((512, 256), jnp.bfloat16),
            vmem(CY, 4 * CZ),
            vmem(N_GY, 8, CZ),
            vmem(N_GY, 8, CZ),
            vmem(5, FX + 4, 32, CZ),
            vmem(5, FX + 4, 32, CZ),
            vmem(2, N_GROUPS, CY, CZ),
            vmem(2, N_GROUPS, CY, CZ),
            vmem(2, N_GROUPS, CY, CZ),
            vmem(2, 19, LX + 1, 32, CZ),
            vmem(2, 19, LX + 1, 32, CZ),
            vmem(2, 19, LX + 1, CY, CZ),
            vmem(2, LX + 2, CY, CZ),
            vmem(LX + 2, 32, CZ),
            vmem(19, CY, CZ),
            vmem(3, LX, CY, CZ),
            vmem(9, 2, 8, CY, CZ),
            vmem(4, 2, CY, CZ),
            vmem(4, 2, 32, CZ),
            vmem(4, 2, 32, CZ),
            vmem(4, 2, 3, 16, CZ),
            vmem(4, 3, 2, 16, CZ),
            vmem(4, 2, 3, 16, CZ),
            vmem(4, 2, 2, 16, CZ),
            vmem(4, 2, 2, 16, CZ),
            vmem(MOST_ROWS, CZ),
            dma(4),
            dma(1),
            dma(1),
            dma(1),
            dma(8),
        ],
        compiler_params=pltpu.CompilerParams(
            collective_id=0, has_side_effects=True, vmem_limit_bytes=40 << 20
        ),
    )(
        in_hbm(coupled_state.reshape(5, FX, CY, CZ)),
        in_hbm(coupled_state.reshape(2, 19, LX, CY, CZ)),
        in_hbm(solid_mask.reshape(LX, CY, CZ)),
        in_hbm(inlet_source),
    )
    return out.reshape(coupled_state.shape)


def solution(mesh):
    return jax.shard_map(
        on_device,
        mesh=mesh,
        in_specs=(P("solver", None, "gy", "gz", None), P(None, "gy", "gz", None), P("gz", None)),
        out_specs=P("solver", None, "gy", "gz", None),
        check_vma=False,
    )
```

```python
import math

import jax
import jax.numpy as jnp
from jax import lax
from jax.experimental import pallas as pl
from jax.experimental.pallas import tpu as pltpu
from jax.sharding import PartitionSpec as P

CY = 16
CZ = 128
LX = 5
FX = 38
N_GY = 16
N_GZ = 8
MESH = pl.DeviceIdType.MESH
F32 = jnp.float32

VELOCITY_TABLE = [
    (0, 0, 0),
    (1, 0, 0),
    (-1, 0, 0),
    (0, 1, 0),
    (0, -1, 0),
    (0, 0, 1),
    (0, 0, -1),
    (1, 1, 0),
    (-1, -1, 0),
    (1, -1, 0),
    (-1, 1, 0),
    (1, 0, 1),
    (-1, 0, -1),
    (1, 0, -1),
    (-1, 0, 1),
    (0, 1, 1),
    (0, -1, -1),
    (0, 1, -1),
    (0, -1, 1),
]
OPPOSITE_TABLE = [0, 2, 1, 4, 3, 6, 5, 8, 7, 10, 9, 12, 11, 14, 13, 16, 15, 18, 17]
RELAX_TIME = 0.8
SURF_TENSION = 0.02
SEGREGATION_BETA = 0.7
GRAD_FLOOR = 0.1
TIME_STEP = 0.2
VISCOSITY = 0.05
DIFFUSION = 0.05
DENSITY_LOG = math.log(2.0)

PLUS_Z = [i for i in range(19) if VELOCITY_TABLE[i][2] == 1]
MINUS_Z = [i for i in range(19) if VELOCITY_TABLE[i][2] == -1]
PLUS_Y = [i for i in range(19) if VELOCITY_TABLE[i][1] == 1]
SIGNS = (0, 1, -1)
CLASSES = [
    [i for i in range(19) if VELOCITY_TABLE[i][1:] == (sy, sz)] for sy in SIGNS for sz in SIGNS
]
MINUS_Y = [i for i in range(19) if VELOCITY_TABLE[i][1] == -1]

GROUP = 6
N_GROUPS = 7
LAST_ROWS = FX - GROUP * (N_GROUPS - 1)
CHUNKS = (
    ((6, LAST_ROWS), (5, GROUP)),
    ((4, GROUP), (3, GROUP)),
    ((2, GROUP), (1, GROUP)),
    ((0, GROUP),),
)


ROUTE_ROWS = 8 * N_GY
PIPE_ROWS = 2 * (2 * 2 * 5 * FX + 2 * CY * N_GROUPS)
FACE_ROWS = 2 * 2 * CY + 4 * 2 * 8 + 2 * 3 * 16 + 4 * 16 + 2 * 2 * 16
POP_ROWS = 2 * 5 * 2
NOZZLE_ROWS = 4 * FACE_ROWS + POP_ROWS * 2 * (LX + 1)
MOST_ROWS = ROUTE_ROWS + max(PIPE_ROWS, NOZZLE_ROWS)


def weighted_sum(values):
    faces = values[1]
    for i in range(2, 7):
        faces = faces + values[i]
    edges = values[7]
    for i in range(8, 19):
        edges = edges + values[i]
    return values[0] * (1.0 / 3.0) + faces * (1.0 / 18.0) + edges * (1.0 / 36.0)


def clip_row(row):
    return min(max(row, 0), LX) if isinstance(row, int) else jnp.clip(row, 0, LX)


def weight_of(i):
    return 1.0 / 3.0 if i == 0 else (1.0 / 18.0 if i < 7 else 1.0 / 36.0)


def part_sum(directions, read):
    total = None
    for weight in (1.0 / 3.0, 1.0 / 18.0, 1.0 / 36.0):
        values = [read(i) for i in directions if weight_of(i) == weight]
        if values:
            group = values[0]
            for value in values[1:]:
                group = group + value
            total = weight * group if total is None else total + weight * group
    return total


def weighted_momentum(values, dim):
    faces = None
    edges = None
    for i in range(1, 19):
        sign = VELOCITY_TABLE[i][dim]
        if sign == 0:
            continue
        if i < 7:
            faces = (
                values[i]
                if faces is None
                else (faces + values[i] if sign > 0 else faces - values[i])
            )
        else:
            edges = (
                values[i]
                if edges is None
                else (edges + values[i] if sign > 0 else edges - values[i])
            )
    return faces * (1.0 / 18.0) + edges * (1.0 / 36.0)


def along(direction, vec):
    total = None
    for sign, part in zip(VELOCITY_TABLE[direction], vec):
        if sign == 0:
            continue
        if total is None:
            total = part if sign > 0 else -part
        else:
            total = total + part if sign > 0 else total - part
    return total


def equilibrium_list(density, vec):
    speed_sq = vec[0] * vec[0] + vec[1] * vec[1] + vec[2] * vec[2]
    rest = density * (1.0 - 1.5 * speed_sq)
    out = [rest]
    for i in range(1, 19, 2):
        proj = along(i, vec)
        even = rest + (4.5 * density) * (proj * proj)
        odd = (3.0 * density) * proj
        out += [even + odd, even - odd]
    return out


def read_moved(moved, colour, i, x):
    return moved[colour, i, clip_row(x - VELOCITY_TABLE[i][0])]


def collide_cells(x, moved, masses, slopes, solid_ref, write):
    def read(colour, i):
        return read_moved(moved, colour, i, x)

    red = masses[0, x + 1]
    blue = masses[1, x + 1]
    total = red + blue
    inverse = 1.0 / total
    mixed = [read(0, i) + read(1, i) for i in range(19)]
    vec = [weighted_momentum(mixed, dim) * inverse for dim in range(3)]
    balance = equilibrium_list(total, vec)
    grad = [slopes[dim, x] for dim in range(3)]
    grad_sq = grad[0] * grad[0] + grad[1] * grad[1] + grad[2] * grad[2]
    inverse_norm = 1.0 / jnp.sqrt(grad_sq + GRAD_FLOOR * GRAD_FLOOR)
    red_part = red * inverse
    tension = SURF_TENSION * inverse_norm
    level = tension * grad_sq * (1.0 / 3.0)
    split = SEGREGATION_BETA * (red_part * blue) * inverse_norm
    solid = solid_ref[x] != 0
    for i in range(19):
        value = mixed[i] - (mixed[i] - balance[i]) * (1.0 / RELAX_TIME) - level
        if i:
            slope = along(i, grad)
            value = value + tension * (slope * slope)
            red_value = red_part * value + split * slope
        else:
            red_value = red_part * value
        back = OPPOSITE_TABLE[i]
        red_new = jnp.where(solid, read(0, back), red_value)
        blue_new = jnp.where(solid, read(1, back), value - red_value)
        write(0, i, red_new)
        write(1, i, blue_new)


def kernel(
    pipe_in,
    nozzle_in,
    solid_in,
    inlet_in,
    out_ref,
    moved,
    masses,
    slopes,
    solid_ref,
    inlet_ref,
    band,
    prof,
    route_out,
    route_in,
    fields_0,
    fields_1,
    zpack,
    zleft,
    zright,
    pops_0,
    pops_1,
    phase_buf,
    ghost_eq,
    class_sums,
    nz_out,
    nz_left,
    nz_right,
    row_sums,
    own_sums,
    row_sums_in,
    row_corners_in,
    own_sums_in,
    tally,
    in_sem,
    send_sem,
    route_recv,
    recv_sem,
):
    solver = lax.axis_index("solver")
    gy = lax.axis_index("gy")
    gz = lax.axis_index("gz")
    other = 1 - solver
    up = lax.rem(gy + 1, N_GY)
    down = lax.rem(gy + N_GY - 1, N_GY)
    right = lax.rem(gz + 1, N_GZ)
    left = lax.rem(gz + N_GZ - 1, N_GZ)
    is_nozzle = solver == 0
    inlet_load = pltpu.make_async_copy(inlet_in, inlet_ref, in_sem.at[1])
    inlet_load.start()
    barrier = pltpu.get_barrier_semaphore()
    for device in (
        (solver, up, gz),
        (solver, down, gz),
        (solver, gy, right),
        (solver, gy, left),
        (solver, up, right),
        (solver, up, left),
        (solver, down, right),
        (solver, down, left),
    ):
        pl.semaphore_signal(barrier, inc=1, device_id=device, device_id_type=MESH)

    def greet(tile, carry):
        pl.semaphore_signal(barrier, inc=1, device_id=(other, tile, gz), device_id_type=MESH)
        return carry

    lax.fori_loop(0, N_GY, greet, 0)

    lane = lax.broadcasted_iota(jnp.int32, (CY, CZ), 1)

    def remote(src, dst, send_sem, recv_sem, device):
        return pltpu.make_async_remote_copy(
            src_ref=src,
            dst_ref=dst,
            send_sem=send_sem,
            recv_sem=recv_sem,
            device_id=device,
            device_id_type=MESH,
        )

    def wait_rows(sem, rows):
        part = tally.at[0:rows, :]
        pltpu.make_async_copy(part, part, sem).wait()

    solid_load = pltpu.make_async_copy(solid_in, solid_ref, in_sem.at[2])
    lane_word = lax.shift_right_logical(lane, 2)

    def pack_word(packed, value, word):
        return jnp.where(lane_word == word, pltpu.roll(value, (4 * word + 2) % CZ, 1), packed)

    def pack_first(group, count):
        packed = jnp.zeros((CY, CZ), F32)
        for row in range(count):
            for field in range(5):
                value = fields_0[field, 2 + GROUP * group + row, 8:24, :]
                packed = pack_word(packed, value, 5 * row + field)
        zpack[0, group] = packed

    def outlet_ghost(fields):
        for field in range(5):
            end = fields[field, 1 + FX, 8:24, :]
            fields[field, 2 + FX, 8:24, :] = end
            fields[field, 3 + FX, 8:24, :] = end

    nozzle_loads = [
        pltpu.make_async_copy(
            nozzle_in.at[:, :, rows, :, :], pops_0.at[:, :, rows, 8:24, :], in_sem.at[k]
        )
        for k, rows in ((0, slice(LX - 1, LX)), (3, slice(0, LX - 1)))
    ]
    pipe_loads = [
        pltpu.make_async_copy(
            pipe_in.at[part, rows, :, :],
            fields_0.at[part, slice(rows.start + 2, rows.stop + 2), 8:24, :],
            in_sem.at[k],
        )
        for k, part, rows in (
            (0, slice(1, 5), slice(0, 1)),
            (2, slice(0, 5), slice(1, FX)),
            (3, slice(0, 1), slice(0, 1)),
        )
    ]

    @pl.when(is_nozzle)
    def _():
        for copy in nozzle_loads:
            copy.start()
        solid_load.start()

    @pl.when(jnp.logical_not(is_nozzle))
    def _():
        for copy in pipe_loads:
            copy.start()

    inlet_load.wait()
    source = inlet_ref[...]
    row_ids = lax.broadcasted_iota(jnp.int32, (1, 256), 1)
    tile_rows = lax.broadcasted_iota(jnp.int32, (N_GY, 256), 0)
    source_tile = lax.shift_right_logical(source, 4)
    target_tile = lax.shift_right_logical(row_ids, 4)
    member = (tile_rows == source_tile).astype(jnp.bfloat16)
    first = lax.broadcasted_iota(jnp.int32, (256, 256), 0)
    second = lax.broadcasted_iota(jnp.int32, (256, 256), 1)
    before = (
        (first < second)
        & (lax.shift_right_logical(first, 4) == lax.shift_right_logical(second, 4))
    ).astype(jnp.bfloat16)
    counts = jnp.dot(member, before, preferred_element_type=F32)
    rank = jnp.sum(counts * member.astype(F32), axis=0, keepdims=True)
    far_tile = jnp.where(is_nozzle, target_tile, source_tile)
    local_row = jnp.where(is_nozzle, source, row_ids)
    mine = (local_row == tile_rows + gy * CY).astype(jnp.bfloat16)
    slot_rows = []
    row_slots = []
    for slot in range(2):
        taken = ((far_tile == tile_rows) & (rank == float(slot))).astype(jnp.bfloat16)
        dims = (((1,), (1,)), ((), ()))
        slot_rows.append(lax.dot_general(taken, mine, dims, preferred_element_type=F32))
        row_slots.append(lax.dot_general(mine, taken, dims, preferred_element_type=F32))

    @pl.when(is_nozzle)
    def _():
        nozzle_loads[0].wait()
        red = [pops_0[0, i, LX - 1, 8:24, :] for i in range(19)]
        blue = [pops_0[1, i, LX - 1, 8:24, :] for i in range(19)]
        red_mass = weighted_sum(red)
        blue_mass = weighted_sum(blue)
        inverse = 1.0 / (red_mass + blue_mass)
        mixed = [r + b for r, b in zip(red, blue)]
        for dim in range(3):
            prof[:, dim * CZ : (dim + 1) * CZ] = weighted_momentum(mixed, dim) * inverse
        prof[:, 3 * CZ :] = (red_mass - blue_mass) * inverse

    @pl.when(jnp.logical_not(is_nozzle))
    def _():
        pipe_loads[0].wait()
        for slot, field in enumerate((4, 1, 2, 3)):
            prof[:, slot * CZ : (slot + 1) * CZ] = fields_0[field, 2, 8:24, :]

    rows = prof[...]
    for slot in range(2):
        picked = jnp.dot(
            slot_rows[slot], rows, precision=lax.Precision.HIGHEST, preferred_element_type=F32
        )
        for part in range(4):
            route_out[:, slot * 4 + part, :] = picked[:, part * CZ : (part + 1) * CZ]

    pl.semaphore_wait(barrier, 8 + N_GY)

    def route(tile):
        return remote(
            route_out.at[tile],
            route_in.at[gy],
            send_sem.at[0],
            route_recv.at[0],
            (other, tile, gz),
        )

    def send_route(tile, carry):
        route(tile).start()
        return carry

    lax.fori_loop(0, N_GY, send_route, 0)

    def take_inflow():
        wait_rows(route_recv.at[0], ROUTE_ROWS)
        total = None
        for slot in range(2):
            arrived = jnp.concatenate(
                [route_in[:, slot * 4 + part, :] for part in range(4)], axis=1
            )
            term = jnp.dot(
                row_slots[slot],
                arrived,
                precision=lax.Precision.HIGHEST,
                preferred_element_type=F32,
            )
            total = term if total is None else total + term
        return [total[:, part * CZ : (part + 1) * CZ] for part in range(4)]

    @pl.when(jnp.logical_not(is_nozzle))
    def _():
        from_left = (lane & 3) < 2

        def group_copies(step, fields, group, count, kinds=range(4)):
            first_row = 2 + GROUP * group
            span = pl.ds(first_row, count)
            arrived = recv_sem.at[4 * step + (N_GROUPS - 1 - group) // 2]
            ends = [
                (fields.at[:, span, 22:24, :], fields.at[:, span, 6:8, :], (solver, up, gz)),
                (fields.at[:, span, 8:10, :], fields.at[:, span, 24:26, :], (solver, down, gz)),
                (zpack.at[step, group], zleft.at[step, group], (solver, gy, right)),
                (zpack.at[step, group], zright.at[step, group], (solver, gy, left)),
            ]
            return [
                remote(ends[k][0], ends[k][1], send_sem.at[0], arrived, ends[k][2]) for k in kinds
            ]

        def send_rows(group, count):
            for copy in group_copies(0, fields_0, group, count, (0, 1)):
                copy.start()

        def send_lanes(group, count):
            pack_first(group, count)
            for copy in group_copies(0, fields_0, group, count, (2, 3)):
                copy.start()

        def split(value):
            high = value.astype(jnp.bfloat16)
            return [high, (value - high.astype(F32)).astype(jnp.bfloat16)]

        def moved_row(fields, along_z, place):
            centre, grad, smooth = [], [], []
            for field in range(5):
                low_x = fields[field, place - 1, 8:24, :]
                high_x = fields[field, place + 1, 8:24, :]
                d_x = (fields[field, place - 2, 8:24, :] - fields[field, place + 2, 8:24, :]) + (
                    8.0 * (high_x - low_x)
                )
                low_y = fields[field, place, 7:23, :]
                high_y = fields[field, place, 9:25, :]
                d_y = (fields[field, place, 6:22, :] - fields[field, place, 10:26, :]) + (
                    8.0 * (high_y - low_y)
                )
                d_z = along_z[field][:, 0:CZ]
                centre.append(fields[field, place, 8:24, :])
                grad.append((d_x, d_y, d_z))
                smooth.append(low_x + high_x + low_y + high_y + along_z[field][:, CZ:])
            scale = TIME_STEP / 12.0
            speed = [scale * centre[k] for k in (1, 2, 3)]
            lift = scale * jnp.exp((1.0 - centre[0]) * DENSITY_LOG)
            spread = TIME_STEP * DIFFUSION
            out = []
            for field in range(4):
                rate = (
                    speed[0] * grad[field][0]
                    + speed[1] * grad[field][1]
                    + speed[2] * grad[field][2]
                )
                if field > 0:
                    rate = rate + lift * grad[4][field - 1]
                out.append((1.0 - 6.0 * spread) * centre[field] + spread * smooth[field] - rate)
            rate = scale * (grad[1][0] + grad[2][1] + grad[3][2])
            out.append((1.0 - 6.0 * spread) * centre[4] + spread * smooth[4] - rate)
            return out

        def run_chunk(step, fields, groups):
            wait_rows(
                recv_sem.at[4 * step + (N_GROUPS - 1 - groups[0][0]) // 2],
                sum(2 * 2 * 5 * count + 2 * CY for _, count in groups),
            )
            lanes_in = []
            for group, count in groups:
                halo = jnp.where(from_left, zleft[step, group], zright[step, group])
                for row in range(count):
                    for field in range(5):
                        here = fields[field, 2 + GROUP * group + row, 8:24, :]
                        edge = pltpu.roll(halo, (-(4 * (5 * row + field) + 2)) % CZ, 1)
                        lanes_in.append(jnp.concatenate(split(here) + split(edge), axis=1))
            lanes_out = jnp.dot(
                jnp.concatenate(lanes_in, axis=0), band[...], preferred_element_type=F32
            )
            done = 0
            for group, count in groups:
                packed = jnp.zeros((CY, CZ), F32)
                for row in range(count):
                    along_z = [lanes_out[(done + k) * CY : (done + k + 1) * CY] for k in range(5)]
                    done += 5
                    place = GROUP * group + row
                    values = moved_row(fields, along_z, 2 + place)
                    for field in range(5):
                        if step == 0:
                            fields_1[field, 2 + place, 8:24, :] = values[field]
                            packed = pack_word(packed, values[field], 5 * row + field)
                        else:
                            out_ref[field * FX + place] = 0.5 * (
                                fields_0[field, 2 + place, 8:24, :] + values[field]
                            )
                if step == 0:
                    zpack[1, group] = packed
                    for copy in group_copies(1, fields_1, group, count):
                        copy.start()

        for copy in pipe_loads[1:]:
            copy.wait()
        send_rows(N_GROUPS - 1, LAST_ROWS)

        def send_step(k, carry):
            send_rows(N_GROUPS - 2 - k, GROUP)
            return carry

        lax.fori_loop(0, N_GROUPS - 1, send_step, 0)
        send_lanes(N_GROUPS - 1, LAST_ROWS)

        def pack_step(k, carry):
            send_lanes(N_GROUPS - 2 - k, GROUP)
            return carry

        lax.fori_loop(0, N_GROUPS - 1, pack_step, 0)
        outlet_ghost(fields_0)
        lane_in = lax.broadcasted_iota(jnp.int32, (CZ, CZ), 0)
        lane_out = lax.broadcasted_iota(jnp.int32, (CZ, CZ), 1)
        ahead = lane_in - lane_out
        wrapped = jnp.where(
            ahead > 64, ahead - CZ, jnp.where(ahead < -64, ahead + CZ, jnp.zeros_like(ahead))
        )
        for part, apart in enumerate((ahead, wrapped)):
            near = (jnp.abs(apart) == 1).astype(F32)
            far = (jnp.abs(apart) == 2).astype(F32)
            slope = jnp.where(apart > 0, 8.0 * near - far, far - 8.0 * near)
            for copy in range(2):
                rows = slice((2 * part + copy) * CZ, (2 * part + copy + 1) * CZ)
                band[rows, 0:CZ] = slope.astype(jnp.bfloat16)
                band[rows, CZ:] = near.astype(jnp.bfloat16)

        run_chunk(0, fields_0, ((6, LAST_ROWS), (5, GROUP)))
        outlet_ghost(fields_1)

        def first_step(k, carry):
            run_chunk(0, fields_0, ((4 - 2 * k, GROUP), (3 - 2 * k, GROUP)))
            return carry

        lax.fori_loop(0, 2, first_step, 0)
        inflow = take_inflow()
        ghost = [0.5 * (1.0 + inflow[3]), inflow[0], inflow[1], inflow[2]]
        for place in range(2):
            for field in range(4):
                fields_0[field, place, 8:24, :] = ghost[field]
                fields_1[field, place, 8:24, :] = ghost[field]
            fields_0[4, place, 8:24, :] = fields_0[4, 2, 8:24, :]
        run_chunk(0, fields_0, ((0, GROUP),))
        for place in range(2):
            fields_1[4, place, 8:24, :] = fields_1[4, 2, 8:24, :]
        run_chunk(1, fields_1, ((6, LAST_ROWS), (5, GROUP)))

        def second_step(k, carry):
            run_chunk(1, fields_1, ((4 - 2 * k, GROUP), (3 - 2 * k, GROUP)))
            return carry

        lax.fori_loop(0, 2, second_step, 0)
        run_chunk(1, fields_1, ((0, GROUP),))

        wait_rows(send_sem.at[0], ROUTE_ROWS + PIPE_ROWS)

    @pl.when(is_nozzle)
    def _():
        def face_copies(step, pops, rows):
            copies = []

            def add(src, dst, device):
                copies.append(remote(src, dst, send_sem.at[0], recv_sem.at[step], device))

            low, high = slice(0, 8), slice(8, 16)
            for k, column, edges in ((0, right, nz_left), (1, left, nz_right)):
                for side, row, part, place in ((0, up, high, 0), (1, down, low, 24)):
                    add(
                        nz_out.at[step, :, part, :],
                        edges.at[step, :, place : place + 8, :],
                        (solver, row, column),
                    )
                    add(
                        row_sums.at[step, side, 1 + k],
                        row_corners_in.at[step, side, k],
                        (solver, row, column),
                    )
            for i in PLUS_Y:
                add(pops.at[:, i, rows, 23:24, :], pops.at[:, i, rows, 7:8, :], (solver, up, gz))
            for i in MINUS_Y:
                add(pops.at[:, i, rows, 8:9, :], pops.at[:, i, rows, 24:25, :], (solver, down, gz))
            add(row_sums.at[step, 0], row_sums_in.at[step, 0], (solver, up, gz))
            add(row_sums.at[step, 1], row_sums_in.at[step, 1], (solver, down, gz))
            for k, column, edges in ((0, right, nz_left), (1, left, nz_right)):
                add(nz_out.at[step], edges.at[step, :, 8:24, :], (solver, gy, column))
                add(own_sums.at[step, 1 + k], own_sums_in.at[step, k], (solver, gy, column))
            return copies

        def lane_of(directions, i, colour, row):
            return 2 * ((directions.index(i) * 2 + colour) * 6 + row) + (directions is MINUS_Z)

        def ghost_row(pops, phase_last):
            for i in range(19):
                pops[0, i, LX, 8:24, :] = (1.0 + phase_last) * ghost_eq[i]
                pops[1, i, LX, 8:24, :] = (1.0 - phase_last) * ghost_eq[i]

        def pack_faces(pops, rows, packed):
            lane_pair = lax.shift_right_logical(lane, 1)
            for row in rows:
                for colour in range(2):
                    for k in range(5):
                        pair = (k * 2 + colour) * 6 + row
                        value = jnp.where(
                            lane < CZ // 2,
                            pops[colour, MINUS_Z[k], row, 8:24, :],
                            pops[colour, PLUS_Z[k], row, 8:24, :],
                        )
                        value = pltpu.roll(value, 2 * pair + 1, 1)
                        packed = jnp.where(lane_pair == pair, value, packed)
            return packed

        def pack_classes(pops, cells, packed):
            for x in cells:
                for colour in range(2):
                    sums = []
                    for k, directions in enumerate(CLASSES):
                        value = part_sum(
                            directions,
                            lambda i: pops[
                                colour, i, min(max(x - VELOCITY_TABLE[i][0], 0), LX), 8:24, :
                            ],
                        )
                        class_sums[k, colour, x] = value
                        sums.append(value)
                    for k in range(3):
                        word = 10 * k + 5 * colour + x
                        value = jnp.where(
                            lane == 126,
                            sums[3 * k + 1],
                            jnp.where(lane == 1, sums[3 * k + 2], sums[3 * k]),
                        )
                        value = pltpu.roll(value, 4 * word + 2, 1)
                        packed = jnp.where(lane_word == word, value, packed)
            return packed

        def edge_rows(step):
            for colour in range(2):
                span = slice(8 * colour, 8 * colour + 8)
                for k in range(3):
                    row_sums[step, 0, k, span, :] = (
                        class_sums[k, colour, :, 15, :] + class_sums[3 + k, colour, :, 14, :]
                    )
                    row_sums[step, 1, k, span, :] = (
                        class_sums[k, colour, :, 0, :] + class_sums[6 + k, colour, :, 1, :]
                    )
                    own_sums[step, k, 0, span, :] = class_sums[6 + k, colour, :, 0, :]
                    own_sums[step, k, 1, span, :] = class_sums[3 + k, colour, :, 15, :]

        def pack(step, pops, rows, cells, packed):
            nz_out[step, 0] = pack_faces(pops, rows, packed[0])
            nz_out[step, 1] = pack_classes(pops, cells, packed[1])

        def send_faces(step, pops, rows):
            edge_rows(step)
            copies = face_copies(step, pops, rows)
            for copy in copies:
                copy.start()

        def arrive(step, rows):
            wait_rows(recv_sem.at[step], FACE_ROWS + POP_ROWS * rows)

        def stream(step, pops, rows):
            for colour in range(2):
                for i in range(19):
                    shift_y, shift_z = VELOCITY_TABLE[i][1:]
                    span = slice(8 - shift_y, 24 - shift_y)
                    for row in rows:
                        value = pops[colour, i, row, span, :]
                        if shift_z == 1:
                            place = lane_of(PLUS_Z, i, colour, row)
                            edge = nz_left[step, 0, span, :]
                            if place:
                                edge = pltpu.roll(edge, CZ - place, 1)
                            value = jnp.where(lane == 0, edge, pltpu.roll(value, 1, 1))
                        elif shift_z == -1:
                            place = lane_of(MINUS_Z, i, colour, row)
                            edge = pltpu.roll(nz_right[step, 0, span, :], CZ - 1 - place, 1)
                            value = jnp.where(lane == CZ - 1, edge, pltpu.roll(value, CZ - 1, 1))
                        moved[colour, i, row] = value


        def read(colour, i, x):
            return read_moved(moved, colour, i, x)

        def mass_step(k, carry):
            red = weighted_sum([read(0, i, k - 1) for i in range(19)])
            blue = weighted_sum([read(1, i, k - 1) for i in range(19)])
            masses[0, k] = red
            masses[1, k] = blue
            phase_buf[k, 8:24, :] = (red - blue) / (red + blue)
            return carry

        def phase_rows(step):
            for side, place in ((0, 7), (1, 24)):
                part = [row_sums_in[step, side, k] + own_sums[step, k, side] for k in range(3)]
                corner = [
                    row_corners_in[step, side, k] + own_sums_in[step, k, side] for k in range(2)
                ]
                edge_lane = lax.broadcasted_iota(jnp.int32, (16, CZ), 1)
                total = (
                    part[0]
                    + pltpu.roll(jnp.where(edge_lane == CZ - 1, corner[0], part[1]), 1, 1)
                    + pltpu.roll(jnp.where(edge_lane == 0, corner[1], part[2]), CZ - 1, 1)
                )
                red = total[0:8]
                blue = total[8:16]
                phase_buf[1 : 1 + LX, place, :] = ((red - blue) / (red + blue))[0:LX]
        def collide(step, pops, first, last):
            beside = None
            for k, span in enumerate((slice(8, 24), slice(7, 23), slice(9, 25))):
                both = jnp.where(
                    (lane & 3) < 2, nz_left[step, 1, span, :], nz_right[step, 1, span, :]
                )
                beside = both if k == 0 else beside + pltpu.roll(both, CZ - 40 * k, 1)
            beside = beside + jnp.where(
                (lane & 3) < 2, pltpu.roll(beside, 1, 1), pltpu.roll(beside, CZ - 1, 1)
            )

            def side_mass(colour, x):
                def shifted(i):
                    shift_x, shift_y = VELOCITY_TABLE[i][0:2]
                    row = clip_row(x - shift_x)
                    return pops[colour, i, row, 8 - shift_y : 24 - shift_y, :]

                low = pltpu.roll(part_sum(MINUS_Z, shifted), CZ - 1, 1)
                high = pltpu.roll(part_sum(PLUS_Z, shifted), 1, 1)
                far = pltpu.roll(beside, CZ - 2 - 4 * (5 * colour + x), 1)
                return far + jnp.where(lane == CZ - 1, low, high)

            def slope_step(x):
                here = phase_buf[x + 1, 8:24, :]
                side_red = side_mass(0, x)
                side_blue = side_mass(1, x)
                side = (side_red - side_blue) / (side_red + side_blue)
                low_z = pltpu.roll(jnp.where(lane == CZ - 1, side, here), 1, 1)
                high_z = pltpu.roll(jnp.where(lane == 0, side, here), CZ - 1, 1)
                grad = [
                    0.5 * (phase_buf[x + 2, 8:24, :] - phase_buf[x, 8:24, :]),
                    0.5 * (phase_buf[x + 1, 9:25, :] - phase_buf[x + 1, 7:23, :]),
                    0.5 * (high_z - low_z),
                ]
                for dim in range(3):
                    slopes[dim, x] = grad[dim]

            for x in range(first, last):
                slope_step(x)
            for x in range(first, last if step < 3 else first):

                def write(colour, i, value, x=x):
                    if step < 2:
                        pops_1[colour, i, x, 8:24, :] = value
                    else:
                        out_ref[(19 * colour + i) * LX + x] = value

                collide_cells(x, moved, masses, slopes, solid_ref, write)

        empty = (jnp.zeros((CY, CZ), F32), jnp.zeros((CY, CZ), F32))
        nozzle_loads[1].wait()
        solid_load.wait()
        pack(0, pops_0, range(LX), range(LX - 1), empty)
        send_faces(0, pops_0, slice(0, LX))
        inflow = take_inflow()
        outflow = equilibrium_list(jnp.exp(inflow[0]), inflow[1:])
        for i in range(19):
            ghost_eq[i] = 0.5 * outflow[i]
        ghost_row(pops_0, prof[:, 3 * CZ :])
        pack(1, pops_0, (LX,), (LX - 1,), nz_out[0])
        send_faces(1, pops_0, slice(LX, LX + 1))
        arrive(0, LX)
        stream(0, pops_0, range(LX))
        lax.fori_loop(0, LX, mass_step, 0)
        phase_rows(0)
        collide(0, pops_0, 0, LX - 2)
        pack(2, pops_1, range(LX - 2), range(LX - 3), empty)
        send_faces(2, pops_1, slice(0, LX - 2))
        arrive(1, 1)
        stream(1, pops_0, (LX,))
        for k in range(LX, LX + 2):
            mass_step(k, 0)
        phase_rows(1)
        collide(1, pops_0, LX - 2, LX)
        red_last = weighted_sum([pops_1[0, i, LX - 1, 8:24, :] for i in range(19)])
        blue_last = weighted_sum([pops_1[1, i, LX - 1, 8:24, :] for i in range(19)])
        ghost_row(pops_1, (red_last - blue_last) / (red_last + blue_last))
        pack(3, pops_1, range(LX - 2, LX + 1), range(LX - 3, LX), nz_out[2])
        send_faces(3, pops_1, slice(LX - 2, LX + 1))
        arrive(2, LX - 2)
        stream(2, pops_1, range(LX - 2))
        lax.fori_loop(0, LX - 2, mass_step, 0)
        phase_rows(2)
        collide(2, pops_1, 0, LX - 4)
        arrive(3, 3)
        stream(3, pops_1, range(LX - 2, LX + 1))
        for k in range(LX - 2, LX + 2):
            mass_step(k, 0)
        phase_rows(3)
        collide(3, pops_1, LX - 4, LX)
        wait_rows(send_sem.at[0], ROUTE_ROWS + NOZZLE_ROWS)


def finish(done_ref, moved, masses, slopes, solid_ref, out_ref, stage, sems):
    is_nozzle = lax.axis_index("solver") == 0

    @pl.when(jnp.logical_not(is_nozzle))
    def _():
        copy = pltpu.make_async_copy(done_ref, out_ref, sems.at[0])
        copy.start()
        copy.wait()

    @pl.when(is_nozzle)
    def _():
        done_pops = done_ref.reshape(2 * 19, LX, CY, CZ)
        out_pops = out_ref.reshape(2 * 19, LX, CY, CZ)
        copies = []
        for x in range(LX):
            row = slice(x, x + 1)

            def write(colour, i, value, x=x):
                stage[19 * colour + i, x] = value

            if x >= LX - 4:
                collide_cells(x, moved, masses, slopes, solid_ref, write)
            source = stage if x >= LX - 4 else done_pops
            copies.append(
                pltpu.make_async_copy(
                    source.at[:, row, :, :], out_pops.at[:, row, :, :], sems.at[x]
                )
            )
            copies[-1].start()
        for copy in copies:
            copy.wait()


def on_device(coupled_state, solid_mask, inlet_source):
    words = coupled_state.shape[1]
    vmem = lambda *shape: pltpu.VMEM(shape, F32)
    in_hbm = lambda array: pltpu.with_memory_space_constraint(array, pltpu.HBM)
    dma = lambda *shape: pltpu.SemaphoreType.DMA(shape)
    done = pl.pallas_call(
        kernel,
        out_shape=[
            vmem(words, CY, CZ),
            vmem(2, 19, LX + 1, CY, CZ),
            vmem(2, LX + 2, CY, CZ),
            vmem(3, LX, CY, CZ),
            pltpu.VMEM((LX, CY, CZ), jnp.int32),
        ],
        in_specs=[
            pl.BlockSpec(memory_space=pltpu.HBM),
            pl.BlockSpec(memory_space=pltpu.HBM),
            pl.BlockSpec(memory_space=pltpu.HBM),
            pl.BlockSpec(memory_space=pltpu.HBM),
        ],
        out_specs=[pl.BlockSpec(memory_space=pltpu.VMEM)] * 5,
        scratch_shapes=[
            pltpu.VMEM((1, 256), jnp.int32),
            pltpu.VMEM((512, 256), jnp.bfloat16),
            vmem(CY, 4 * CZ),
            vmem(N_GY, 8, CZ),
            vmem(N_GY, 8, CZ),
            vmem(5, FX + 4, 32, CZ),
            vmem(5, FX + 4, 32, CZ),
            vmem(2, N_GROUPS, CY, CZ),
            vmem(2, N_GROUPS, CY, CZ),
            vmem(2, N_GROUPS, CY, CZ),
            vmem(2, 19, LX + 1, 32, CZ),
            vmem(2, 19, LX + 1, 32, CZ),
            vmem(LX + 2, 32, CZ),
            vmem(19, CY, CZ),
            vmem(9, 2, 8, CY, CZ),
            vmem(4, 2, CY, CZ),
            vmem(4, 2, 32, CZ),
            vmem(4, 2, 32, CZ),
            vmem(4, 2, 3, 16, CZ),
            vmem(4, 3, 2, 16, CZ),
            vmem(4, 2, 3, 16, CZ),
            vmem(4, 2, 2, 16, CZ),
            vmem(4, 2, 2, 16, CZ),
            vmem(MOST_ROWS, CZ),
            dma(4),
            dma(1),
            dma(1),
            dma(8),
        ],
        compiler_params=pltpu.CompilerParams(
            collective_id=0, has_side_effects=True, vmem_limit_bytes=28 << 20
        ),
    )(
        in_hbm(coupled_state.reshape(5, FX, CY, CZ)),
        in_hbm(coupled_state.reshape(2, 19, LX, CY, CZ)),
        in_hbm(solid_mask.reshape(LX, CY, CZ)),
        in_hbm(inlet_source),
    )
    out = pl.pallas_call(
        finish,
        out_shape=pltpu.HBM((words, CY, CZ), F32),
        in_specs=[pl.BlockSpec(memory_space=pltpu.VMEM)] * 5,
        out_specs=pl.BlockSpec(memory_space=pl.ANY),
        scratch_shapes=[vmem(2 * 19, LX, CY, CZ), dma(LX)],
        compiler_params=pltpu.CompilerParams(vmem_limit_bytes=8 << 20),
    )(*(pltpu.with_memory_space_constraint(array, pltpu.VMEM) for array in done))
    return out.reshape(coupled_state.shape)


def solution(mesh):
    return jax.shard_map(
        on_device,
        mesh=mesh,
        in_specs=(P("solver", None, "gy", "gz", None), P(None, "gy", "gz", None), P("gz", None)),
        out_specs=P("solver", None, "gy", "gz", None),
        check_vma=False,
    )
```

```python
import math

import jax
import jax.numpy as jnp
from jax import lax
from jax.experimental import pallas as pl
from jax.experimental.pallas import tpu as pltpu
from jax.sharding import PartitionSpec as P

CY = 16
CZ = 128
LX = 5
FX = 38
N_GY = 16
N_GZ = 8
MESH = pl.DeviceIdType.MESH
F32 = jnp.float32

VELOCITY_TABLE = [
    (0, 0, 0),
    (1, 0, 0),
    (-1, 0, 0),
    (0, 1, 0),
    (0, -1, 0),
    (0, 0, 1),
    (0, 0, -1),
    (1, 1, 0),
    (-1, -1, 0),
    (1, -1, 0),
    (-1, 1, 0),
    (1, 0, 1),
    (-1, 0, -1),
    (1, 0, -1),
    (-1, 0, 1),
    (0, 1, 1),
    (0, -1, -1),
    (0, 1, -1),
    (0, -1, 1),
]
OPPOSITE_TABLE = [0, 2, 1, 4, 3, 6, 5, 8, 7, 10, 9, 12, 11, 14, 13, 16, 15, 18, 17]
RELAX_TIME = 0.8
SURF_TENSION = 0.02
SEGREGATION_BETA = 0.7
GRAD_FLOOR = 0.1
TIME_STEP = 0.2
VISCOSITY = 0.05
DIFFUSION = 0.05
DENSITY_LOG = math.log(2.0)

PLUS_Z = [i for i in range(19) if VELOCITY_TABLE[i][2] == 1]
MINUS_Z = [i for i in range(19) if VELOCITY_TABLE[i][2] == -1]
PLUS_Y = [i for i in range(19) if VELOCITY_TABLE[i][1] == 1]
SIGNS = (0, 1, -1)
CLASSES = [
    [i for i in range(19) if VELOCITY_TABLE[i][1:] == (sy, sz)] for sy in SIGNS for sz in SIGNS
]
MINUS_Y = [i for i in range(19) if VELOCITY_TABLE[i][1] == -1]

GROUP = 6
N_GROUPS = 7
LAST_ROWS = FX - GROUP * (N_GROUPS - 1)
CHUNKS = (
    ((6, LAST_ROWS), (5, GROUP)),
    ((4, GROUP), (3, GROUP)),
    ((2, GROUP), (1, GROUP)),
    ((0, GROUP),),
)


ROUTE_ROWS = 8 * N_GY
PIPE_ROWS = 2 * (2 * 2 * 5 * FX + 2 * CY * N_GROUPS)
FACE_ROWS = 2 * 2 * CY + 2 * 3 * 16 + 2 * 2 * 16
CORNER_ROWS = 4 * 2 * 8 + 4 * 16
POP_ROWS = 2 * 5 * 2
NOZZLE_ROWS = 4 * (FACE_ROWS + CORNER_ROWS) + POP_ROWS * 2 * (LX + 1)
MOST_ROWS = ROUTE_ROWS + max(PIPE_ROWS, NOZZLE_ROWS)


def weighted_sum(values):
    faces = values[1]
    for i in range(2, 7):
        faces = faces + values[i]
    edges = values[7]
    for i in range(8, 19):
        edges = edges + values[i]
    return values[0] * (1.0 / 3.0) + faces * (1.0 / 18.0) + edges * (1.0 / 36.0)


def clip_row(row):
    return min(max(row, 0), LX) if isinstance(row, int) else jnp.clip(row, 0, LX)


def weight_of(i):
    return 1.0 / 3.0 if i == 0 else (1.0 / 18.0 if i < 7 else 1.0 / 36.0)


def part_sum(directions, read):
    total = None
    for weight in (1.0 / 3.0, 1.0 / 18.0, 1.0 / 36.0):
        values = [read(i) for i in directions if weight_of(i) == weight]
        if values:
            group = values[0]
            for value in values[1:]:
                group = group + value
            total = weight * group if total is None else total + weight * group
    return total


def weighted_momentum(values, dim):
    faces = None
    edges = None
    for i in range(1, 19):
        sign = VELOCITY_TABLE[i][dim]
        if sign == 0:
            continue
        if i < 7:
            faces = (
                values[i]
                if faces is None
                else (faces + values[i] if sign > 0 else faces - values[i])
            )
        else:
            edges = (
                values[i]
                if edges is None
                else (edges + values[i] if sign > 0 else edges - values[i])
            )
    return faces * (1.0 / 18.0) + edges * (1.0 / 36.0)


def along(direction, vec):
    total = None
    for sign, part in zip(VELOCITY_TABLE[direction], vec):
        if sign == 0:
            continue
        if total is None:
            total = part if sign > 0 else -part
        else:
            total = total + part if sign > 0 else total - part
    return total


def equilibrium_list(density, vec):
    speed_sq = vec[0] * vec[0] + vec[1] * vec[1] + vec[2] * vec[2]
    rest = density * (1.0 - 1.5 * speed_sq)
    out = [rest]
    for i in range(1, 19, 2):
        proj = along(i, vec)
        even = rest + (4.5 * density) * (proj * proj)
        odd = (3.0 * density) * proj
        out += [even + odd, even - odd]
    return out


def read_moved(moved, colour, i, x):
    return moved[colour, i, clip_row(x - VELOCITY_TABLE[i][0])]


def relax_cells(x, moved, masses, relaxed):
    for i, value in enumerate(relaxed_list(x, moved, masses)):
        relaxed[i] = value


def relaxed_list(x, moved, masses):
    total = masses[0, x + 1] + masses[1, x + 1]
    inverse = 1.0 / total
    mixed = [read_moved(moved, 0, i, x) + read_moved(moved, 1, i, x) for i in range(19)]
    vec = [weighted_momentum(mixed, dim) * inverse for dim in range(3)]
    balance = equilibrium_list(total, vec)
    return [m - (m - b) * (1.0 / RELAX_TIME) for m, b in zip(mixed, balance)]


def collide_cells(x, moved, masses, slopes, solid_ref, write, relaxed=None):
    def read(colour, i):
        return read_moved(moved, colour, i, x)

    red = masses[0, x + 1]
    blue = masses[1, x + 1]
    total = red + blue
    inverse = 1.0 / total
    if relaxed is None:
        settled = relaxed_list(x, moved, masses)
    else:
        settled = [relaxed[i] for i in range(19)]
    grad = [slopes[dim, x] for dim in range(3)]
    grad_sq = grad[0] * grad[0] + grad[1] * grad[1] + grad[2] * grad[2]
    inverse_norm = 1.0 / jnp.sqrt(grad_sq + GRAD_FLOOR * GRAD_FLOOR)
    red_part = red * inverse
    tension = SURF_TENSION * inverse_norm
    level = tension * grad_sq * (1.0 / 3.0)
    split = SEGREGATION_BETA * (red_part * blue) * inverse_norm
    solid = solid_ref[x] != 0
    for i in range(19):
        value = settled[i] - level
        if i:
            slope = along(i, grad)
            value = value + tension * (slope * slope)
            red_value = red_part * value + split * slope
        else:
            red_value = red_part * value
        back = OPPOSITE_TABLE[i]
        red_new = jnp.where(solid, read(0, back), red_value)
        blue_new = jnp.where(solid, read(1, back), value - red_value)
        write(0, i, red_new)
        write(1, i, blue_new)


def kernel(
    pipe_in,
    nozzle_in,
    solid_in,
    inlet_in,
    out_ref,
    moved,
    masses,
    slopes,
    solid_ref,
    inlet_ref,
    band,
    prof,
    route_out,
    route_in,
    fields_0,
    fields_1,
    zpack,
    zleft,
    zright,
    pops_0,
    pops_1,
    phase_buf,
    ghost_eq,
    relaxed,
    own_side,
    class_sums,
    nz_out,
    nz_left,
    nz_right,
    row_sums,
    own_sums,
    row_sums_in,
    row_corners_in,
    own_sums_in,
    tally,
    in_sem,
    send_sem,
    route_recv,
    recv_sem,
):
    solver = lax.axis_index("solver")
    gy = lax.axis_index("gy")
    gz = lax.axis_index("gz")
    other = 1 - solver
    up = lax.rem(gy + 1, N_GY)
    down = lax.rem(gy + N_GY - 1, N_GY)
    right = lax.rem(gz + 1, N_GZ)
    left = lax.rem(gz + N_GZ - 1, N_GZ)
    is_nozzle = solver == 0
    inlet_load = pltpu.make_async_copy(inlet_in, inlet_ref, in_sem.at[1])
    inlet_load.start()
    barrier = pltpu.get_barrier_semaphore()
    for device in (
        (solver, up, gz),
        (solver, down, gz),
        (solver, gy, right),
        (solver, gy, left),
        (solver, up, right),
        (solver, up, left),
        (solver, down, right),
        (solver, down, left),
    ):
        pl.semaphore_signal(barrier, inc=1, device_id=device, device_id_type=MESH)

    def greet(tile, carry):
        pl.semaphore_signal(barrier, inc=1, device_id=(other, tile, gz), device_id_type=MESH)
        return carry

    lax.fori_loop(0, N_GY, greet, 0)

    lane = lax.broadcasted_iota(jnp.int32, (CY, CZ), 1)

    def remote(src, dst, send_sem, recv_sem, device):
        return pltpu.make_async_remote_copy(
            src_ref=src,
            dst_ref=dst,
            send_sem=send_sem,
            recv_sem=recv_sem,
            device_id=device,
            device_id_type=MESH,
        )

    def wait_rows(sem, rows):
        part = tally.at[0:rows, :]
        pltpu.make_async_copy(part, part, sem).wait()

    solid_load = pltpu.make_async_copy(solid_in, solid_ref, in_sem.at[2])
    lane_word = lax.shift_right_logical(lane, 2)

    def pack_word(packed, value, word):
        return jnp.where(lane_word == word, pltpu.roll(value, (4 * word + 2) % CZ, 1), packed)

    def pack_first(group, count):
        packed = jnp.zeros((CY, CZ), F32)
        for row in range(count):
            for field in range(5):
                value = fields_0[field, 2 + GROUP * group + row, 8:24, :]
                packed = pack_word(packed, value, 5 * row + field)
        zpack[0, group] = packed

    def outlet_ghost(fields):
        for field in range(5):
            end = fields[field, 1 + FX, 8:24, :]
            fields[field, 2 + FX, 8:24, :] = end
            fields[field, 3 + FX, 8:24, :] = end

    nozzle_loads = [
        pltpu.make_async_copy(
            nozzle_in.at[:, :, rows, :, :], pops_0.at[:, :, rows, 8:24, :], in_sem.at[k]
        )
        for k, rows in ((0, slice(LX - 1, LX)), (3, slice(0, LX - 1)))
    ]
    pipe_loads = [
        pltpu.make_async_copy(
            pipe_in.at[part, rows, :, :],
            fields_0.at[part, slice(rows.start + 2, rows.stop + 2), 8:24, :],
            in_sem.at[k],
        )
        for k, part, rows in (
            (0, slice(1, 5), slice(0, 1)),
            (2, slice(0, 5), slice(1, FX)),
            (3, slice(0, 1), slice(0, 1)),
        )
    ]

    @pl.when(is_nozzle)
    def _():
        for copy in nozzle_loads:
            copy.start()
        solid_load.start()

    @pl.when(jnp.logical_not(is_nozzle))
    def _():
        for copy in pipe_loads:
            copy.start()

    inlet_load.wait()
    source = inlet_ref[...]
    row_ids = lax.broadcasted_iota(jnp.int32, (1, 256), 1)
    tile_rows = lax.broadcasted_iota(jnp.int32, (N_GY, 256), 0)
    source_tile = lax.shift_right_logical(source, 4)
    target_tile = lax.shift_right_logical(row_ids, 4)
    member = (tile_rows == source_tile).astype(jnp.bfloat16)
    first = lax.broadcasted_iota(jnp.int32, (256, 256), 0)
    second = lax.broadcasted_iota(jnp.int32, (256, 256), 1)
    before = (
        (first < second)
        & (lax.shift_right_logical(first, 4) == lax.shift_right_logical(second, 4))
    ).astype(jnp.bfloat16)
    counts = jnp.dot(member, before, preferred_element_type=F32)
    rank = jnp.sum(counts * member.astype(F32), axis=0, keepdims=True)
    far_tile = jnp.where(is_nozzle, target_tile, source_tile)
    local_row = jnp.where(is_nozzle, source, row_ids)
    mine = (local_row == tile_rows + gy * CY).astype(jnp.bfloat16)
    slot_rows = []
    row_slots = []
    for slot in range(2):
        taken = ((far_tile == tile_rows) & (rank == float(slot))).astype(jnp.bfloat16)
        dims = (((1,), (1,)), ((), ()))
        slot_rows.append(lax.dot_general(taken, mine, dims, preferred_element_type=F32))
        row_slots.append(lax.dot_general(mine, taken, dims, preferred_element_type=F32))

    @pl.when(is_nozzle)
    def _():
        nozzle_loads[0].wait()
        red = [pops_0[0, i, LX - 1, 8:24, :] for i in range(19)]
        blue = [pops_0[1, i, LX - 1, 8:24, :] for i in range(19)]
        red_mass = weighted_sum(red)
        blue_mass = weighted_sum(blue)
        inverse = 1.0 / (red_mass + blue_mass)
        mixed = [r + b for r, b in zip(red, blue)]
        for dim in range(3):
            prof[:, dim * CZ : (dim + 1) * CZ] = weighted_momentum(mixed, dim) * inverse
        prof[:, 3 * CZ :] = (red_mass - blue_mass) * inverse

    @pl.when(jnp.logical_not(is_nozzle))
    def _():
        pipe_loads[0].wait()
        for slot, field in enumerate((4, 1, 2, 3)):
            prof[:, slot * CZ : (slot + 1) * CZ] = fields_0[field, 2, 8:24, :]

    rows = prof[...]
    for slot in range(2):
        picked = jnp.dot(
            slot_rows[slot], rows, precision=lax.Precision.HIGHEST, preferred_element_type=F32
        )
        for part in range(4):
            route_out[:, slot * 4 + part, :] = picked[:, part * CZ : (part + 1) * CZ]

    pl.semaphore_wait(barrier, 8 + N_GY)

    def route(tile):
        return remote(
            route_out.at[tile],
            route_in.at[gy],
            send_sem.at[0],
            route_recv.at[0],
            (other, tile, gz),
        )

    def send_route(tile, carry):
        route(tile).start()
        return carry

    lax.fori_loop(0, N_GY, send_route, 0)

    def take_inflow():
        wait_rows(route_recv.at[0], ROUTE_ROWS)
        total = None
        for slot in range(2):
            arrived = jnp.concatenate(
                [route_in[:, slot * 4 + part, :] for part in range(4)], axis=1
            )
            term = jnp.dot(
                row_slots[slot],
                arrived,
                precision=lax.Precision.HIGHEST,
                preferred_element_type=F32,
            )
            total = term if total is None else total + term
        return [total[:, part * CZ : (part + 1) * CZ] for part in range(4)]

    @pl.when(jnp.logical_not(is_nozzle))
    def _():
        from_left = (lane & 3) < 2

        def group_copies(step, fields, group, count, kinds=range(4)):
            first_row = 2 + GROUP * group
            span = pl.ds(first_row, count)
            arrived = recv_sem.at[4 * step + (N_GROUPS - 1 - group) // 2]
            ends = [
                (fields.at[:, span, 22:24, :], fields.at[:, span, 6:8, :], (solver, up, gz)),
                (fields.at[:, span, 8:10, :], fields.at[:, span, 24:26, :], (solver, down, gz)),
                (zpack.at[step, group], zleft.at[step, group], (solver, gy, right)),
                (zpack.at[step, group], zright.at[step, group], (solver, gy, left)),
            ]
            return [
                remote(ends[k][0], ends[k][1], send_sem.at[0], arrived, ends[k][2]) for k in kinds
            ]

        def send_rows(group, count):
            for copy in group_copies(0, fields_0, group, count, (0, 1)):
                copy.start()

        def send_lanes(group, count):
            pack_first(group, count)
            for copy in group_copies(0, fields_0, group, count, (2, 3)):
                copy.start()

        def split(value):
            high = value.astype(jnp.bfloat16)
            return [high, (value - high.astype(F32)).astype(jnp.bfloat16)]

        def moved_row(fields, along_z, place):
            centre, grad, smooth = [], [], []
            for field in range(5):
                low_x = fields[field, place - 1, 8:24, :]
                high_x = fields[field, place + 1, 8:24, :]
                d_x = (fields[field, place - 2, 8:24, :] - fields[field, place + 2, 8:24, :]) + (
                    8.0 * (high_x - low_x)
                )
                low_y = fields[field, place, 7:23, :]
                high_y = fields[field, place, 9:25, :]
                d_y = (fields[field, place, 6:22, :] - fields[field, place, 10:26, :]) + (
                    8.0 * (high_y - low_y)
                )
                d_z = along_z[field][:, 0:CZ]
                centre.append(fields[field, place, 8:24, :])
                grad.append((d_x, d_y, d_z))
                smooth.append(low_x + high_x + low_y + high_y + along_z[field][:, CZ:])
            scale = TIME_STEP / 12.0
            speed = [scale * centre[k] for k in (1, 2, 3)]
            lift = scale * jnp.exp((1.0 - centre[0]) * DENSITY_LOG)
            spread = TIME_STEP * DIFFUSION
            out = []
            for field in range(4):
                rate = (
                    speed[0] * grad[field][0]
                    + speed[1] * grad[field][1]
                    + speed[2] * grad[field][2]
                )
                if field > 0:
                    rate = rate + lift * grad[4][field - 1]
                out.append((1.0 - 6.0 * spread) * centre[field] + spread * smooth[field] - rate)
            rate = scale * (grad[1][0] + grad[2][1] + grad[3][2])
            out.append((1.0 - 6.0 * spread) * centre[4] + spread * smooth[4] - rate)
            return out

        def run_chunk(step, fields, groups):
            wait_rows(
                recv_sem.at[4 * step + (N_GROUPS - 1 - groups[0][0]) // 2],
                sum(2 * 2 * 5 * count + 2 * CY for _, count in groups),
            )
            lanes_in = []
            for group, count in groups:
                halo = jnp.where(from_left, zleft[step, group], zright[step, group])
                for row in range(count):
                    for field in range(5):
                        here = fields[field, 2 + GROUP * group + row, 8:24, :]
                        edge = pltpu.roll(halo, (-(4 * (5 * row + field) + 2)) % CZ, 1)
                        lanes_in.append(jnp.concatenate(split(here) + split(edge), axis=1))
            lanes_out = jnp.dot(
                jnp.concatenate(lanes_in, axis=0), band[...], preferred_element_type=F32
            )
            done = 0
            for group, count in groups:
                packed = jnp.zeros((CY, CZ), F32)
                for row in range(count):
                    along_z = [lanes_out[(done + k) * CY : (done + k + 1) * CY] for k in range(5)]
                    done += 5
                    place = GROUP * group + row
                    values = moved_row(fields, along_z, 2 + place)
                    for field in range(5):
                        if step == 0:
                            fields_1[field, 2 + place, 8:24, :] = values[field]
                            packed = pack_word(packed, values[field], 5 * row + field)
                        else:
                            out_ref[field * FX + place] = 0.5 * (
                                fields_0[field, 2 + place, 8:24, :] + values[field]
                            )
                if step == 0:
                    zpack[1, group] = packed
                    for copy in group_copies(1, fields_1, group, count):
                        copy.start()

        for copy in pipe_loads[1:]:
            copy.wait()
        send_rows(N_GROUPS - 1, LAST_ROWS)

        def send_step(k, carry):
            send_rows(N_GROUPS - 2 - k, GROUP)
            return carry

        lax.fori_loop(0, N_GROUPS - 1, send_step, 0)
        send_lanes(N_GROUPS - 1, LAST_ROWS)

        def pack_step(k, carry):
            send_lanes(N_GROUPS - 2 - k, GROUP)
            return carry

        lax.fori_loop(0, N_GROUPS - 1, pack_step, 0)
        outlet_ghost(fields_0)
        lane_in = lax.broadcasted_iota(jnp.int32, (CZ, CZ), 0)
        lane_out = lax.broadcasted_iota(jnp.int32, (CZ, CZ), 1)
        ahead = lane_in - lane_out
        wrapped = jnp.where(
            ahead > 64, ahead - CZ, jnp.where(ahead < -64, ahead + CZ, jnp.zeros_like(ahead))
        )
        for part, apart in enumerate((ahead, wrapped)):
            near = (jnp.abs(apart) == 1).astype(F32)
            far = (jnp.abs(apart) == 2).astype(F32)
            slope = jnp.where(apart > 0, 8.0 * near - far, far - 8.0 * near)
            for copy in range(2):
                rows = slice((2 * part + copy) * CZ, (2 * part + copy + 1) * CZ)
                band[rows, 0:CZ] = slope.astype(jnp.bfloat16)
                band[rows, CZ:] = near.astype(jnp.bfloat16)

        run_chunk(0, fields_0, ((6, LAST_ROWS), (5, GROUP)))
        outlet_ghost(fields_1)

        def first_step(k, carry):
            run_chunk(0, fields_0, ((4 - 2 * k, GROUP), (3 - 2 * k, GROUP)))
            return carry

        lax.fori_loop(0, 2, first_step, 0)
        inflow = take_inflow()
        ghost = [0.5 * (1.0 + inflow[3]), inflow[0], inflow[1], inflow[2]]
        for place in range(2):
            for field in range(4):
                fields_0[field, place, 8:24, :] = ghost[field]
                fields_1[field, place, 8:24, :] = ghost[field]
            fields_0[4, place, 8:24, :] = fields_0[4, 2, 8:24, :]
        run_chunk(0, fields_0, ((0, GROUP),))
        for place in range(2):
            fields_1[4, place, 8:24, :] = fields_1[4, 2, 8:24, :]
        run_chunk(1, fields_1, ((6, LAST_ROWS), (5, GROUP)))

        def second_step(k, carry):
            run_chunk(1, fields_1, ((4 - 2 * k, GROUP), (3 - 2 * k, GROUP)))
            return carry

        lax.fori_loop(0, 2, second_step, 0)
        run_chunk(1, fields_1, ((0, GROUP),))

        wait_rows(send_sem.at[0], ROUTE_ROWS + PIPE_ROWS)

    @pl.when(is_nozzle)
    def _():
        def face_copies(step, pops, rows):
            copies = []

            def add(src, dst, device, kind=0):
                arrived = recv_sem.at[2 * step + kind]
                copies.append(remote(src, dst, send_sem.at[0], arrived, device))

            low, high = slice(0, 8), slice(8, 16)
            for k, column, edges in ((0, right, nz_left), (1, left, nz_right)):
                for side, row, part, place in ((0, up, high, 0), (1, down, low, 24)):
                    add(
                        nz_out.at[step, :, part, :],
                        edges.at[step, :, place : place + 8, :],
                        (solver, row, column),
                        1,
                    )
                    add(
                        row_sums.at[step, side, 1 + k],
                        row_corners_in.at[step, side, k],
                        (solver, row, column),
                        1,
                    )
            for i in PLUS_Y:
                add(pops.at[:, i, rows, 23:24, :], pops.at[:, i, rows, 7:8, :], (solver, up, gz))
            for i in MINUS_Y:
                add(pops.at[:, i, rows, 8:9, :], pops.at[:, i, rows, 24:25, :], (solver, down, gz))
            add(row_sums.at[step, 0], row_sums_in.at[step, 0], (solver, up, gz))
            add(row_sums.at[step, 1], row_sums_in.at[step, 1], (solver, down, gz))
            for k, column, edges in ((0, right, nz_left), (1, left, nz_right)):
                add(nz_out.at[step], edges.at[step, :, 8:24, :], (solver, gy, column))
                add(own_sums.at[step, 1 + k], own_sums_in.at[step, k], (solver, gy, column))
            return copies

        def lane_of(directions, i, colour, row):
            return 2 * ((directions.index(i) * 2 + colour) * 6 + row) + (directions is MINUS_Z)

        def ghost_row(pops, phase_last):
            for i in range(19):
                pops[0, i, LX, 8:24, :] = (1.0 + phase_last) * ghost_eq[i]
                pops[1, i, LX, 8:24, :] = (1.0 - phase_last) * ghost_eq[i]

        def pack_faces(pops, rows, packed):
            lane_pair = lax.shift_right_logical(lane, 1)
            for row in rows:
                for colour in range(2):
                    for k in range(5):
                        pair = (k * 2 + colour) * 6 + row
                        value = jnp.where(
                            lane < CZ // 2,
                            pops[colour, MINUS_Z[k], row, 8:24, :],
                            pops[colour, PLUS_Z[k], row, 8:24, :],
                        )
                        value = pltpu.roll(value, 2 * pair + 1, 1)
                        packed = jnp.where(lane_pair == pair, value, packed)
            return packed

        def pack_classes(pops, cells, packed):
            for x in cells:
                for colour in range(2):
                    sums = []
                    for k, directions in enumerate(CLASSES):
                        value = part_sum(
                            directions,
                            lambda i: pops[
                                colour, i, min(max(x - VELOCITY_TABLE[i][0], 0), LX), 8:24, :
                            ],
                        )
                        class_sums[k, colour, x] = value
                        sums.append(value)
                    for k in range(3):
                        word = 10 * k + 5 * colour + x
                        value = jnp.where(
                            lane == 126,
                            sums[3 * k + 1],
                            jnp.where(lane == 1, sums[3 * k + 2], sums[3 * k]),
                        )
                        value = pltpu.roll(value, 4 * word + 2, 1)
                        packed = jnp.where(lane_word == word, value, packed)
            return packed

        def edge_rows(step):
            for colour in range(2):
                span = slice(8 * colour, 8 * colour + 8)
                for k in range(3):
                    row_sums[step, 0, k, span, :] = (
                        class_sums[k, colour, :, 15, :] + class_sums[3 + k, colour, :, 14, :]
                    )
                    row_sums[step, 1, k, span, :] = (
                        class_sums[k, colour, :, 0, :] + class_sums[6 + k, colour, :, 1, :]
                    )
                    own_sums[step, k, 0, span, :] = class_sums[6 + k, colour, :, 0, :]
                    own_sums[step, k, 1, span, :] = class_sums[3 + k, colour, :, 15, :]

        def pack(step, pops, rows, cells, packed):
            nz_out[step, 0] = pack_faces(pops, rows, packed[0])
            nz_out[step, 1] = pack_classes(pops, cells, packed[1])

        def send_faces(step, pops, rows):
            edge_rows(step)
            copies = face_copies(step, pops, rows)
            for copy in copies:
                copy.start()

        def stream_in(step, pops, rows, mass_rows, cells):
            wait_rows(recv_sem.at[2 * step], FACE_ROWS + POP_ROWS * len(rows))
            stream(step, pops, rows, range(15))
            for k in mass_rows:
                mass_part(k)
            for x in cells:
                side_part(pops, x)
            wait_rows(recv_sem.at[2 * step + 1], CORNER_ROWS)
            stream(step, pops, rows, range(15, 19))
            for k in mass_rows:
                mass_rest(k)
            phase_rows(step)

        def stream(step, pops, rows, directions):
            for colour in range(2):
                for i in directions:
                    shift_y, shift_z = VELOCITY_TABLE[i][1:]
                    span = slice(8 - shift_y, 24 - shift_y)
                    for row in rows:
                        value = pops[colour, i, row, span, :]
                        if shift_z == 1:
                            place = lane_of(PLUS_Z, i, colour, row)
                            edge = nz_left[step, 0, span, :]
                            if place:
                                edge = pltpu.roll(edge, CZ - place, 1)
                            value = jnp.where(lane == 0, edge, pltpu.roll(value, 1, 1))
                        elif shift_z == -1:
                            place = lane_of(MINUS_Z, i, colour, row)
                            edge = pltpu.roll(nz_right[step, 0, span, :], CZ - 1 - place, 1)
                            value = jnp.where(lane == CZ - 1, edge, pltpu.roll(value, CZ - 1, 1))
                        moved[colour, i, row] = value


        def read(colour, i, x):
            return read_moved(moved, colour, i, x)

        def mass_part(k):
            for colour in range(2):
                masses[colour, k] = part_sum(range(15), lambda i: read(colour, i, k - 1))

        def mass_rest(k):
            red, blue = (
                masses[colour, k]
                + part_sum(range(15, 19), lambda i: read(colour, i, k - 1))
                for colour in range(2)
            )
            masses[0, k] = red
            masses[1, k] = blue
            phase_buf[k, 8:24, :] = (red - blue) / (red + blue)

        def side_part(pops, x):
            for colour in range(2):

                def shifted(i):
                    shift_x, shift_y = VELOCITY_TABLE[i][0:2]
                    row = clip_row(x - shift_x)
                    return pops[colour, i, row, 8 - shift_y : 24 - shift_y, :]

                low = pltpu.roll(part_sum(MINUS_Z, shifted), CZ - 1, 1)
                high = pltpu.roll(part_sum(PLUS_Z, shifted), 1, 1)
                own_side[colour, x] = jnp.where(lane == CZ - 1, low, high)

        def phase_rows(step):
            for side, place in ((0, 7), (1, 24)):
                part = [row_sums_in[step, side, k] + own_sums[step, k, side] for k in range(3)]
                corner = [
                    row_corners_in[step, side, k] + own_sums_in[step, k, side] for k in range(2)
                ]
                edge_lane = lax.broadcasted_iota(jnp.int32, (16, CZ), 1)
                total = (
                    part[0]
                    + pltpu.roll(jnp.where(edge_lane == CZ - 1, corner[0], part[1]), 1, 1)
                    + pltpu.roll(jnp.where(edge_lane == 0, corner[1], part[2]), CZ - 1, 1)
                )
                red = total[0:8]
                blue = total[8:16]
                phase_buf[1 : 1 + LX, place, :] = ((red - blue) / (red + blue))[0:LX]
        def collide(step, pops, first, last):
            beside = None
            for k, span in enumerate((slice(8, 24), slice(7, 23), slice(9, 25))):
                both = jnp.where(
                    (lane & 3) < 2, nz_left[step, 1, span, :], nz_right[step, 1, span, :]
                )
                beside = both if k == 0 else beside + pltpu.roll(both, CZ - 40 * k, 1)
            beside = beside + jnp.where(
                (lane & 3) < 2, pltpu.roll(beside, 1, 1), pltpu.roll(beside, CZ - 1, 1)
            )

            def side_mass(colour, x):
                far = pltpu.roll(beside, CZ - 2 - 4 * (5 * colour + x), 1)
                return far + own_side[colour, x]

            def slope_step(x):
                here = phase_buf[x + 1, 8:24, :]
                side_red = side_mass(0, x)
                side_blue = side_mass(1, x)
                side = (side_red - side_blue) / (side_red + side_blue)
                low_z = pltpu.roll(jnp.where(lane == CZ - 1, side, here), 1, 1)
                high_z = pltpu.roll(jnp.where(lane == 0, side, here), CZ - 1, 1)
                grad = [
                    0.5 * (phase_buf[x + 2, 8:24, :] - phase_buf[x, 8:24, :]),
                    0.5 * (phase_buf[x + 1, 9:25, :] - phase_buf[x + 1, 7:23, :]),
                    0.5 * (high_z - low_z),
                ]
                for dim in range(3):
                    slopes[dim, x] = grad[dim]

            for x in range(first, last):
                slope_step(x)
            for x in range(first, last if step < 3 else first):

                def write(colour, i, value, x=x):
                    if step < 2:
                        pops_1[colour, i, x, 8:24, :] = value
                    else:
                        out_ref[(19 * colour + i) * LX + x] = value

                ready = relaxed if step == 1 and x == LX - 2 else None
                collide_cells(x, moved, masses, slopes, solid_ref, write, ready)

        empty = (jnp.zeros((CY, CZ), F32), jnp.zeros((CY, CZ), F32))
        nozzle_loads[1].wait()
        solid_load.wait()
        pack(0, pops_0, range(LX), range(LX - 1), empty)
        send_faces(0, pops_0, slice(0, LX))
        inflow = take_inflow()
        outflow = equilibrium_list(jnp.exp(inflow[0]), inflow[1:])
        for i in range(19):
            ghost_eq[i] = 0.5 * outflow[i]
        ghost_row(pops_0, prof[:, 3 * CZ :])
        pack(1, pops_0, (LX,), (LX - 1,), nz_out[0])
        send_faces(1, pops_0, slice(LX, LX + 1))
        stream_in(0, pops_0, range(LX), range(LX), range(LX - 2))
        collide(0, pops_0, 0, LX - 2)
        pack(2, pops_1, range(LX - 2), range(LX - 3), empty)
        send_faces(2, pops_1, slice(0, LX - 2))
        relax_cells(LX - 2, moved, masses, relaxed)
        stream_in(1, pops_0, (LX,), range(LX, LX + 2), range(LX - 2, LX))
        collide(1, pops_0, LX - 2, LX)
        red_last = weighted_sum([pops_1[0, i, LX - 1, 8:24, :] for i in range(19)])
        blue_last = weighted_sum([pops_1[1, i, LX - 1, 8:24, :] for i in range(19)])
        ghost_row(pops_1, (red_last - blue_last) / (red_last + blue_last))
        pack(3, pops_1, range(LX - 2, LX + 1), range(LX - 3, LX), nz_out[2])
        send_faces(3, pops_1, slice(LX - 2, LX + 1))
        stream_in(2, pops_1, range(LX - 2), range(LX - 2), range(LX - 4))
        collide(2, pops_1, 0, LX - 4)
        stream_in(3, pops_1, range(LX - 2, LX + 1), range(LX - 2, LX + 2), range(LX - 4, LX))
        collide(3, pops_1, LX - 4, LX)
        wait_rows(send_sem.at[0], ROUTE_ROWS + NOZZLE_ROWS)


def finish(done_ref, moved, masses, slopes, solid_ref, out_ref, stage, sems):
    is_nozzle = lax.axis_index("solver") == 0

    @pl.when(jnp.logical_not(is_nozzle))
    def _():
        copy = pltpu.make_async_copy(done_ref, out_ref, sems.at[0])
        copy.start()
        copy.wait()

    @pl.when(is_nozzle)
    def _():
        done_pops = done_ref.reshape(2 * 19, LX, CY, CZ)
        out_pops = out_ref.reshape(2 * 19, LX, CY, CZ)
        copies = []
        for x in range(LX):
            row = slice(x, x + 1)

            def write(colour, i, value, x=x):
                stage[19 * colour + i, x] = value

            if x >= LX - 4:
                collide_cells(x, moved, masses, slopes, solid_ref, write)
            source = stage if x >= LX - 4 else done_pops
            copies.append(
                pltpu.make_async_copy(
                    source.at[:, row, :, :], out_pops.at[:, row, :, :], sems.at[x]
                )
            )
            copies[-1].start()
        for copy in copies:
            copy.wait()


def on_device(coupled_state, solid_mask, inlet_source):
    words = coupled_state.shape[1]
    vmem = lambda *shape: pltpu.VMEM(shape, F32)
    in_hbm = lambda array: pltpu.with_memory_space_constraint(array, pltpu.HBM)
    dma = lambda *shape: pltpu.SemaphoreType.DMA(shape)
    done = pl.pallas_call(
        kernel,
        out_shape=[
            vmem(words, CY, CZ),
            vmem(2, 19, LX + 1, CY, CZ),
            vmem(2, LX + 2, CY, CZ),
            vmem(3, LX, CY, CZ),
            pltpu.VMEM((LX, CY, CZ), jnp.int32),
        ],
        in_specs=[
            pl.BlockSpec(memory_space=pltpu.HBM),
            pl.BlockSpec(memory_space=pltpu.HBM),
            pl.BlockSpec(memory_space=pltpu.HBM),
            pl.BlockSpec(memory_space=pltpu.HBM),
        ],
        out_specs=[pl.BlockSpec(memory_space=pltpu.VMEM)] * 5,
        scratch_shapes=[
            pltpu.VMEM((1, 256), jnp.int32),
            pltpu.VMEM((512, 256), jnp.bfloat16),
            vmem(CY, 4 * CZ),
            vmem(N_GY, 8, CZ),
            vmem(N_GY, 8, CZ),
            vmem(5, FX + 4, 32, CZ),
            vmem(5, FX + 4, 32, CZ),
            vmem(2, N_GROUPS, CY, CZ),
            vmem(2, N_GROUPS, CY, CZ),
            vmem(2, N_GROUPS, CY, CZ),
            vmem(2, 19, LX + 1, 32, CZ),
            vmem(2, 19, LX + 1, 32, CZ),
            vmem(LX + 2, 32, CZ),
            vmem(19, CY, CZ),
            vmem(19, CY, CZ),
            vmem(2, LX, CY, CZ),
            vmem(9, 2, 8, CY, CZ),
            vmem(4, 2, CY, CZ),
            vmem(4, 2, 32, CZ),
            vmem(4, 2, 32, CZ),
            vmem(4, 2, 3, 16, CZ),
            vmem(4, 3, 2, 16, CZ),
            vmem(4, 2, 3, 16, CZ),
            vmem(4, 2, 2, 16, CZ),
            vmem(4, 2, 2, 16, CZ),
            vmem(MOST_ROWS, CZ),
            dma(4),
            dma(1),
            dma(1),
            dma(8),
        ],
        compiler_params=pltpu.CompilerParams(
            collective_id=0, has_side_effects=True, vmem_limit_bytes=28 << 20
        ),
    )(
        in_hbm(coupled_state.reshape(5, FX, CY, CZ)),
        in_hbm(coupled_state.reshape(2, 19, LX, CY, CZ)),
        in_hbm(solid_mask.reshape(LX, CY, CZ)),
        in_hbm(inlet_source),
    )
    out = pl.pallas_call(
        finish,
        out_shape=pltpu.HBM((words, CY, CZ), F32),
        in_specs=[pl.BlockSpec(memory_space=pltpu.VMEM)] * 5,
        out_specs=pl.BlockSpec(memory_space=pl.ANY),
        scratch_shapes=[vmem(2 * 19, LX, CY, CZ), dma(LX)],
        compiler_params=pltpu.CompilerParams(vmem_limit_bytes=8 << 20),
    )(*(pltpu.with_memory_space_constraint(array, pltpu.VMEM) for array in done))
    return out.reshape(coupled_state.shape)


def solution(mesh):
    return jax.shard_map(
        on_device,
        mesh=mesh,
        in_specs=(P("solver", None, "gy", "gz", None), P(None, "gy", "gz", None), P("gz", None)),
        out_specs=P("solver", None, "gy", "gz", None),
        check_vma=False,
    )
```

```python
import math

import jax
import jax.numpy as jnp
from jax import lax
from jax.experimental import pallas as pl
from jax.experimental.pallas import tpu as pltpu
from jax.sharding import PartitionSpec as P

CY = 16
CZ = 128
LX = 5
FX = 38
N_GY = 16
N_GZ = 8
MESH = pl.DeviceIdType.MESH
F32 = jnp.float32

VELOCITY_TABLE = [
    (0, 0, 0),
    (1, 0, 0),
    (-1, 0, 0),
    (0, 1, 0),
    (0, -1, 0),
    (0, 0, 1),
    (0, 0, -1),
    (1, 1, 0),
    (-1, -1, 0),
    (1, -1, 0),
    (-1, 1, 0),
    (1, 0, 1),
    (-1, 0, -1),
    (1, 0, -1),
    (-1, 0, 1),
    (0, 1, 1),
    (0, -1, -1),
    (0, 1, -1),
    (0, -1, 1),
]
OPPOSITE_TABLE = [0, 2, 1, 4, 3, 6, 5, 8, 7, 10, 9, 12, 11, 14, 13, 16, 15, 18, 17]
RELAX_TIME = 0.8
SURF_TENSION = 0.02
SEGREGATION_BETA = 0.7
GRAD_FLOOR = 0.1
TIME_STEP = 0.2
VISCOSITY = 0.05
DIFFUSION = 0.05
DENSITY_LOG = math.log(2.0)

PLUS_Z = [i for i in range(19) if VELOCITY_TABLE[i][2] == 1]
MINUS_Z = [i for i in range(19) if VELOCITY_TABLE[i][2] == -1]
PLUS_Y = [i for i in range(19) if VELOCITY_TABLE[i][1] == 1]
SIGNS = (0, 1, -1)
CLASSES = [
    [i for i in range(19) if VELOCITY_TABLE[i][1:] == (sy, sz)] for sy in SIGNS for sz in SIGNS
]
MINUS_Y = [i for i in range(19) if VELOCITY_TABLE[i][1] == -1]

GROUP = 6
N_GROUPS = 7
LAST_ROWS = FX - GROUP * (N_GROUPS - 1)
CHUNKS = (
    ((6, LAST_ROWS), (5, GROUP)),
    ((4, GROUP), (3, GROUP)),
    ((2, GROUP), (1, GROUP)),
    ((0, GROUP),),
)


ROUTE_ROWS = 8 * N_GY
PIPE_ROWS = 2 * (2 * 2 * 5 * FX + 2 * CY * N_GROUPS)
FACE_ROWS = 2 * 2 * CY + 2 * 3 * 16 + 2 * 2 * 16
CORNER_ROWS = 4 * 2 * 8 + 4 * 16
POP_ROWS = 2 * 5 * 2
NOZZLE_ROWS = 4 * (FACE_ROWS + CORNER_ROWS) + POP_ROWS * 2 * (LX + 1)
MOST_ROWS = ROUTE_ROWS + max(PIPE_ROWS, NOZZLE_ROWS)


def weighted_sum(values):
    faces = values[1]
    for i in range(2, 7):
        faces = faces + values[i]
    edges = values[7]
    for i in range(8, 19):
        edges = edges + values[i]
    return values[0] * (1.0 / 3.0) + faces * (1.0 / 18.0) + edges * (1.0 / 36.0)


def clip_row(row):
    return min(max(row, 0), LX) if isinstance(row, int) else jnp.clip(row, 0, LX)


def weight_of(i):
    return 1.0 / 3.0 if i == 0 else (1.0 / 18.0 if i < 7 else 1.0 / 36.0)


def part_sum(directions, read):
    total = None
    for weight in (1.0 / 3.0, 1.0 / 18.0, 1.0 / 36.0):
        values = [read(i) for i in directions if weight_of(i) == weight]
        if values:
            group = values[0]
            for value in values[1:]:
                group = group + value
            total = weight * group if total is None else total + weight * group
    return total


def weighted_momentum(values, dim):
    faces = None
    edges = None
    for i in range(1, 19):
        sign = VELOCITY_TABLE[i][dim]
        if sign == 0:
            continue
        if i < 7:
            faces = (
                values[i]
                if faces is None
                else (faces + values[i] if sign > 0 else faces - values[i])
            )
        else:
            edges = (
                values[i]
                if edges is None
                else (edges + values[i] if sign > 0 else edges - values[i])
            )
    return faces * (1.0 / 18.0) + edges * (1.0 / 36.0)


def along(direction, vec):
    total = None
    for sign, part in zip(VELOCITY_TABLE[direction], vec):
        if sign == 0:
            continue
        if total is None:
            total = part if sign > 0 else -part
        else:
            total = total + part if sign > 0 else total - part
    return total


def equilibrium_list(density, vec):
    speed_sq = vec[0] * vec[0] + vec[1] * vec[1] + vec[2] * vec[2]
    rest = density * (1.0 - 1.5 * speed_sq)
    out = [rest]
    for i in range(1, 19, 2):
        proj = along(i, vec)
        even = rest + (4.5 * density) * (proj * proj)
        odd = (3.0 * density) * proj
        out += [even + odd, even - odd]
    return out


def read_moved(moved, colour, i, x):
    return moved[colour, i, clip_row(x - VELOCITY_TABLE[i][0])]


def relax_cells(x, moved, masses, relaxed):
    for i, value in enumerate(relaxed_list(x, moved, masses)):
        relaxed[i] = value


def relaxed_list(x, moved, masses):
    total = masses[0, x + 1] + masses[1, x + 1]
    inverse = 1.0 / total
    mixed = [read_moved(moved, 0, i, x) + read_moved(moved, 1, i, x) for i in range(19)]
    vec = [weighted_momentum(mixed, dim) * inverse for dim in range(3)]
    balance = equilibrium_list(total, vec)
    return [m - (m - b) * (1.0 / RELAX_TIME) for m, b in zip(mixed, balance)]


def collide_cells(x, moved, masses, slopes, solid_ref, write, relaxed=None):
    def read(colour, i):
        return read_moved(moved, colour, i, x)

    red = masses[0, x + 1]
    blue = masses[1, x + 1]
    total = red + blue
    inverse = 1.0 / total
    if relaxed is None:
        settled = relaxed_list(x, moved, masses)
    else:
        settled = [relaxed[i] for i in range(19)]
    grad = [slopes[dim, x] for dim in range(3)]
    grad_sq = grad[0] * grad[0] + grad[1] * grad[1] + grad[2] * grad[2]
    inverse_norm = 1.0 / jnp.sqrt(grad_sq + GRAD_FLOOR * GRAD_FLOOR)
    red_part = red * inverse
    tension = SURF_TENSION * inverse_norm
    level = tension * grad_sq * (1.0 / 3.0)
    split = SEGREGATION_BETA * (red_part * blue) * inverse_norm
    solid = solid_ref[x] != 0
    for i in range(19):
        value = settled[i] - level
        if i:
            slope = along(i, grad)
            value = value + tension * (slope * slope)
            red_value = red_part * value + split * slope
        else:
            red_value = red_part * value
        back = OPPOSITE_TABLE[i]
        red_new = jnp.where(solid, read(0, back), red_value)
        blue_new = jnp.where(solid, read(1, back), value - red_value)
        write(0, i, red_new)
        write(1, i, blue_new)


def kernel(
    pipe_in,
    nozzle_in,
    solid_in,
    inlet_in,
    out_ref,
    moved,
    masses,
    slopes,
    relaxed,
    solid_ref,
    inlet_ref,
    band,
    prof,
    route_out,
    route_in,
    fields_0,
    fields_1,
    zpack,
    zleft,
    zright,
    pops_0,
    pops_1,
    phase_buf,
    ghost_eq,
    own_side,
    class_sums,
    nz_out,
    nz_left,
    nz_right,
    row_sums,
    own_sums,
    row_sums_in,
    row_corners_in,
    own_sums_in,
    tally,
    in_sem,
    send_sem,
    route_recv,
    recv_sem,
):
    solver = lax.axis_index("solver")
    gy = lax.axis_index("gy")
    gz = lax.axis_index("gz")
    other = 1 - solver
    up = lax.rem(gy + 1, N_GY)
    down = lax.rem(gy + N_GY - 1, N_GY)
    right = lax.rem(gz + 1, N_GZ)
    left = lax.rem(gz + N_GZ - 1, N_GZ)
    is_nozzle = solver == 0
    inlet_load = pltpu.make_async_copy(inlet_in, inlet_ref, in_sem.at[1])
    inlet_load.start()
    barrier = pltpu.get_barrier_semaphore()
    for device in (
        (solver, up, gz),
        (solver, down, gz),
        (solver, gy, right),
        (solver, gy, left),
        (solver, up, right),
        (solver, up, left),
        (solver, down, right),
        (solver, down, left),
    ):
        pl.semaphore_signal(barrier, inc=1, device_id=device, device_id_type=MESH)

    def greet(tile, carry):
        pl.semaphore_signal(barrier, inc=1, device_id=(other, tile, gz), device_id_type=MESH)
        return carry

    lax.fori_loop(0, N_GY, greet, 0)

    lane = lax.broadcasted_iota(jnp.int32, (CY, CZ), 1)

    def remote(src, dst, send_sem, recv_sem, device):
        return pltpu.make_async_remote_copy(
            src_ref=src,
            dst_ref=dst,
            send_sem=send_sem,
            recv_sem=recv_sem,
            device_id=device,
            device_id_type=MESH,
        )

    def wait_rows(sem, rows):
        part = tally.at[0:rows, :]
        pltpu.make_async_copy(part, part, sem).wait()

    solid_load = pltpu.make_async_copy(solid_in, solid_ref, in_sem.at[2])
    lane_word = lax.shift_right_logical(lane, 2)

    def pack_word(packed, value, word):
        return jnp.where(lane_word == word, pltpu.roll(value, (4 * word + 2) % CZ, 1), packed)

    def pack_first(group, count):
        packed = jnp.zeros((CY, CZ), F32)
        for row in range(count):
            for field in range(5):
                value = fields_0[field, 2 + GROUP * group + row, 8:24, :]
                packed = pack_word(packed, value, 5 * row + field)
        zpack[0, group] = packed

    def outlet_ghost(fields):
        for field in range(5):
            end = fields[field, 1 + FX, 8:24, :]
            fields[field, 2 + FX, 8:24, :] = end
            fields[field, 3 + FX, 8:24, :] = end

    nozzle_loads = [
        pltpu.make_async_copy(
            nozzle_in.at[:, :, rows, :, :], pops_0.at[:, :, rows, 8:24, :], in_sem.at[k]
        )
        for k, rows in ((0, slice(LX - 1, LX)), (3, slice(0, LX - 1)))
    ]
    pipe_loads = [
        pltpu.make_async_copy(
            pipe_in.at[part, rows, :, :],
            fields_0.at[part, slice(rows.start + 2, rows.stop + 2), 8:24, :],
            in_sem.at[k],
        )
        for k, part, rows in (
            (0, slice(1, 5), slice(0, 1)),
            (2, slice(0, 5), slice(1, FX)),
            (3, slice(0, 1), slice(0, 1)),
        )
    ]

    @pl.when(is_nozzle)
    def _():
        for copy in nozzle_loads:
            copy.start()
        solid_load.start()

    @pl.when(jnp.logical_not(is_nozzle))
    def _():
        for copy in pipe_loads:
            copy.start()

    inlet_load.wait()
    source = inlet_ref[...]
    row_ids = lax.broadcasted_iota(jnp.int32, (1, 256), 1)
    tile_rows = lax.broadcasted_iota(jnp.int32, (N_GY, 256), 0)
    source_tile = lax.shift_right_logical(source, 4)
    target_tile = lax.shift_right_logical(row_ids, 4)
    member = (tile_rows == source_tile).astype(jnp.bfloat16)
    first = lax.broadcasted_iota(jnp.int32, (256, 256), 0)
    second = lax.broadcasted_iota(jnp.int32, (256, 256), 1)
    before = (
        (first < second)
        & (lax.shift_right_logical(first, 4) == lax.shift_right_logical(second, 4))
    ).astype(jnp.bfloat16)
    counts = jnp.dot(member, before, preferred_element_type=F32)
    rank = jnp.sum(counts * member.astype(F32), axis=0, keepdims=True)
    far_tile = jnp.where(is_nozzle, target_tile, source_tile)
    local_row = jnp.where(is_nozzle, source, row_ids)
    mine = (local_row == tile_rows + gy * CY).astype(jnp.bfloat16)
    slot_rows = []
    row_slots = []
    for slot in range(2):
        taken = ((far_tile == tile_rows) & (rank == float(slot))).astype(jnp.bfloat16)
        dims = (((1,), (1,)), ((), ()))
        slot_rows.append(lax.dot_general(taken, mine, dims, preferred_element_type=F32))
        row_slots.append(lax.dot_general(mine, taken, dims, preferred_element_type=F32))

    @pl.when(is_nozzle)
    def _():
        nozzle_loads[0].wait()
        red = [pops_0[0, i, LX - 1, 8:24, :] for i in range(19)]
        blue = [pops_0[1, i, LX - 1, 8:24, :] for i in range(19)]
        red_mass = weighted_sum(red)
        blue_mass = weighted_sum(blue)
        inverse = 1.0 / (red_mass + blue_mass)
        mixed = [r + b for r, b in zip(red, blue)]
        for dim in range(3):
            prof[:, dim * CZ : (dim + 1) * CZ] = weighted_momentum(mixed, dim) * inverse
        prof[:, 3 * CZ :] = (red_mass - blue_mass) * inverse

    @pl.when(jnp.logical_not(is_nozzle))
    def _():
        pipe_loads[0].wait()
        for slot, field in enumerate((4, 1, 2, 3)):
            prof[:, slot * CZ : (slot + 1) * CZ] = fields_0[field, 2, 8:24, :]

    rows = prof[...]
    for slot in range(2):
        picked = jnp.dot(
            slot_rows[slot], rows, precision=lax.Precision.HIGHEST, preferred_element_type=F32
        )
        for part in range(4):
            route_out[:, slot * 4 + part, :] = picked[:, part * CZ : (part + 1) * CZ]

    pl.semaphore_wait(barrier, 8 + N_GY)

    def route(tile):
        return remote(
            route_out.at[tile],
            route_in.at[gy],
            send_sem.at[0],
            route_recv.at[0],
            (other, tile, gz),
        )

    def send_route(tile, carry):
        route(tile).start()
        return carry

    lax.fori_loop(0, N_GY, send_route, 0)

    def take_inflow():
        wait_rows(route_recv.at[0], ROUTE_ROWS)
        total = None
        for slot in range(2):
            arrived = jnp.concatenate(
                [route_in[:, slot * 4 + part, :] for part in range(4)], axis=1
            )
            term = jnp.dot(
                row_slots[slot],
                arrived,
                precision=lax.Precision.HIGHEST,
                preferred_element_type=F32,
            )
            total = term if total is None else total + term
        return [total[:, part * CZ : (part + 1) * CZ] for part in range(4)]

    @pl.when(jnp.logical_not(is_nozzle))
    def _():
        from_left = (lane & 3) < 2

        def group_copies(step, fields, group, count, kinds=range(4)):
            first_row = 2 + GROUP * group
            span = pl.ds(first_row, count)
            arrived = recv_sem.at[4 * step + (N_GROUPS - 1 - group) // 2]
            ends = [
                (fields.at[:, span, 22:24, :], fields.at[:, span, 6:8, :], (solver, up, gz)),
                (fields.at[:, span, 8:10, :], fields.at[:, span, 24:26, :], (solver, down, gz)),
                (zpack.at[step, group], zleft.at[step, group], (solver, gy, right)),
                (zpack.at[step, group], zright.at[step, group], (solver, gy, left)),
            ]
            return [
                remote(ends[k][0], ends[k][1], send_sem.at[0], arrived, ends[k][2]) for k in kinds
            ]

        def send_rows(group, count):
            for copy in group_copies(0, fields_0, group, count, (0, 1)):
                copy.start()

        def send_lanes(group, count):
            pack_first(group, count)
            for copy in group_copies(0, fields_0, group, count, (2, 3)):
                copy.start()

        def split(value):
            high = value.astype(jnp.bfloat16)
            return [high, (value - high.astype(F32)).astype(jnp.bfloat16)]

        def moved_row(fields, along_z, place):
            centre, grad, smooth = [], [], []
            for field in range(5):
                low_x = fields[field, place - 1, 8:24, :]
                high_x = fields[field, place + 1, 8:24, :]
                d_x = (fields[field, place - 2, 8:24, :] - fields[field, place + 2, 8:24, :]) + (
                    8.0 * (high_x - low_x)
                )
                low_y = fields[field, place, 7:23, :]
                high_y = fields[field, place, 9:25, :]
                d_y = (fields[field, place, 6:22, :] - fields[field, place, 10:26, :]) + (
                    8.0 * (high_y - low_y)
                )
                d_z = along_z[field][:, 0:CZ]
                centre.append(fields[field, place, 8:24, :])
                grad.append((d_x, d_y, d_z))
                smooth.append(low_x + high_x + low_y + high_y + along_z[field][:, CZ:])
            scale = TIME_STEP / 12.0
            speed = [scale * centre[k] for k in (1, 2, 3)]
            lift = scale * jnp.exp((1.0 - centre[0]) * DENSITY_LOG)
            spread = TIME_STEP * DIFFUSION
            out = []
            for field in range(4):
                rate = (
                    speed[0] * grad[field][0]
                    + speed[1] * grad[field][1]
                    + speed[2] * grad[field][2]
                )
                if field > 0:
                    rate = rate + lift * grad[4][field - 1]
                out.append((1.0 - 6.0 * spread) * centre[field] + spread * smooth[field] - rate)
            rate = scale * (grad[1][0] + grad[2][1] + grad[3][2])
            out.append((1.0 - 6.0 * spread) * centre[4] + spread * smooth[4] - rate)
            return out

        def run_chunk(step, fields, groups):
            wait_rows(
                recv_sem.at[4 * step + (N_GROUPS - 1 - groups[0][0]) // 2],
                sum(2 * 2 * 5 * count + 2 * CY for _, count in groups),
            )
            lanes_in = []
            for group, count in groups:
                halo = jnp.where(from_left, zleft[step, group], zright[step, group])
                for row in range(count):
                    for field in range(5):
                        here = fields[field, 2 + GROUP * group + row, 8:24, :]
                        edge = pltpu.roll(halo, (-(4 * (5 * row + field) + 2)) % CZ, 1)
                        lanes_in.append(jnp.concatenate(split(here) + split(edge), axis=1))
            lanes_out = jnp.dot(
                jnp.concatenate(lanes_in, axis=0), band[...], preferred_element_type=F32
            )
            done = 0
            for group, count in groups:
                packed = jnp.zeros((CY, CZ), F32)
                for row in range(count):
                    along_z = [lanes_out[(done + k) * CY : (done + k + 1) * CY] for k in range(5)]
                    done += 5
                    place = GROUP * group + row
                    values = moved_row(fields, along_z, 2 + place)
                    for field in range(5):
                        if step == 0:
                            fields_1[field, 2 + place, 8:24, :] = values[field]
                            packed = pack_word(packed, values[field], 5 * row + field)
                        else:
                            out_ref[field * FX + place] = 0.5 * (
                                fields_0[field, 2 + place, 8:24, :] + values[field]
                            )
                if step == 0:
                    zpack[1, group] = packed
                    for copy in group_copies(1, fields_1, group, count):
                        copy.start()

        for copy in pipe_loads[1:]:
            copy.wait()
        send_rows(N_GROUPS - 1, LAST_ROWS)

        def send_step(k, carry):
            send_rows(N_GROUPS - 2 - k, GROUP)
            return carry

        lax.fori_loop(0, N_GROUPS - 1, send_step, 0)
        send_lanes(N_GROUPS - 1, LAST_ROWS)

        def pack_step(k, carry):
            send_lanes(N_GROUPS - 2 - k, GROUP)
            return carry

        lax.fori_loop(0, N_GROUPS - 1, pack_step, 0)
        outlet_ghost(fields_0)
        lane_in = lax.broadcasted_iota(jnp.int32, (CZ, CZ), 0)
        lane_out = lax.broadcasted_iota(jnp.int32, (CZ, CZ), 1)
        ahead = lane_in - lane_out
        wrapped = jnp.where(
            ahead > 64, ahead - CZ, jnp.where(ahead < -64, ahead + CZ, jnp.zeros_like(ahead))
        )
        for part, apart in enumerate((ahead, wrapped)):
            near = (jnp.abs(apart) == 1).astype(F32)
            far = (jnp.abs(apart) == 2).astype(F32)
            slope = jnp.where(apart > 0, 8.0 * near - far, far - 8.0 * near)
            for copy in range(2):
                rows = slice((2 * part + copy) * CZ, (2 * part + copy + 1) * CZ)
                band[rows, 0:CZ] = slope.astype(jnp.bfloat16)
                band[rows, CZ:] = near.astype(jnp.bfloat16)

        run_chunk(0, fields_0, ((6, LAST_ROWS), (5, GROUP)))
        outlet_ghost(fields_1)

        def first_step(k, carry):
            run_chunk(0, fields_0, ((4 - 2 * k, GROUP), (3 - 2 * k, GROUP)))
            return carry

        lax.fori_loop(0, 2, first_step, 0)
        inflow = take_inflow()
        ghost = [0.5 * (1.0 + inflow[3]), inflow[0], inflow[1], inflow[2]]
        for place in range(2):
            for field in range(4):
                fields_0[field, place, 8:24, :] = ghost[field]
                fields_1[field, place, 8:24, :] = ghost[field]
            fields_0[4, place, 8:24, :] = fields_0[4, 2, 8:24, :]
        run_chunk(0, fields_0, ((0, GROUP),))
        for place in range(2):
            fields_1[4, place, 8:24, :] = fields_1[4, 2, 8:24, :]
        run_chunk(1, fields_1, ((6, LAST_ROWS), (5, GROUP)))

        def second_step(k, carry):
            run_chunk(1, fields_1, ((4 - 2 * k, GROUP), (3 - 2 * k, GROUP)))
            return carry

        lax.fori_loop(0, 2, second_step, 0)
        run_chunk(1, fields_1, ((0, GROUP),))

        wait_rows(send_sem.at[0], ROUTE_ROWS + PIPE_ROWS)

    @pl.when(is_nozzle)
    def _():
        def face_copies(step, pops, rows):
            copies = []

            def add(src, dst, device, kind=0):
                arrived = recv_sem.at[2 * step + kind]
                copies.append(remote(src, dst, send_sem.at[0], arrived, device))

            low, high = slice(0, 8), slice(8, 16)
            for k, column, edges in ((0, right, nz_left), (1, left, nz_right)):
                for side, row, part, place in ((0, up, high, 0), (1, down, low, 24)):
                    add(
                        nz_out.at[step, :, part, :],
                        edges.at[step, :, place : place + 8, :],
                        (solver, row, column),
                        1,
                    )
                    add(
                        row_sums.at[step, side, 1 + k],
                        row_corners_in.at[step, side, k],
                        (solver, row, column),
                        1,
                    )
            for i in PLUS_Y:
                add(pops.at[:, i, rows, 23:24, :], pops.at[:, i, rows, 7:8, :], (solver, up, gz))
            for i in MINUS_Y:
                add(pops.at[:, i, rows, 8:9, :], pops.at[:, i, rows, 24:25, :], (solver, down, gz))
            add(row_sums.at[step, 0], row_sums_in.at[step, 0], (solver, up, gz))
            add(row_sums.at[step, 1], row_sums_in.at[step, 1], (solver, down, gz))
            for k, column, edges in ((0, right, nz_left), (1, left, nz_right)):
                add(nz_out.at[step], edges.at[step, :, 8:24, :], (solver, gy, column))
                add(own_sums.at[step, 1 + k], own_sums_in.at[step, k], (solver, gy, column))
            return copies

        def lane_of(directions, i, colour, row):
            return 2 * ((directions.index(i) * 2 + colour) * 6 + row) + (directions is MINUS_Z)

        def ghost_row(pops, phase_last):
            for i in range(19):
                pops[0, i, LX, 8:24, :] = (1.0 + phase_last) * ghost_eq[i]
                pops[1, i, LX, 8:24, :] = (1.0 - phase_last) * ghost_eq[i]

        def pack_faces(pops, rows, packed):
            lane_pair = lax.shift_right_logical(lane, 1)
            for row in rows:
                for colour in range(2):
                    for k in range(5):
                        pair = (k * 2 + colour) * 6 + row
                        value = jnp.where(
                            lane < CZ // 2,
                            pops[colour, MINUS_Z[k], row, 8:24, :],
                            pops[colour, PLUS_Z[k], row, 8:24, :],
                        )
                        value = pltpu.roll(value, 2 * pair + 1, 1)
                        packed = jnp.where(lane_pair == pair, value, packed)
            return packed

        def pack_classes(pops, cells, packed):
            for x in cells:
                for colour in range(2):
                    sums = []
                    for k, directions in enumerate(CLASSES):
                        value = part_sum(
                            directions,
                            lambda i: pops[
                                colour, i, min(max(x - VELOCITY_TABLE[i][0], 0), LX), 8:24, :
                            ],
                        )
                        class_sums[k, colour, x] = value
                        sums.append(value)
                    for k in range(3):
                        word = 10 * k + 5 * colour + x
                        value = jnp.where(
                            lane == 126,
                            sums[3 * k + 1],
                            jnp.where(lane == 1, sums[3 * k + 2], sums[3 * k]),
                        )
                        value = pltpu.roll(value, 4 * word + 2, 1)
                        packed = jnp.where(lane_word == word, value, packed)
            return packed

        def edge_rows(step):
            for colour in range(2):
                span = slice(8 * colour, 8 * colour + 8)
                for k in range(3):
                    row_sums[step, 0, k, span, :] = (
                        class_sums[k, colour, :, 15, :] + class_sums[3 + k, colour, :, 14, :]
                    )
                    row_sums[step, 1, k, span, :] = (
                        class_sums[k, colour, :, 0, :] + class_sums[6 + k, colour, :, 1, :]
                    )
                    own_sums[step, k, 0, span, :] = class_sums[6 + k, colour, :, 0, :]
                    own_sums[step, k, 1, span, :] = class_sums[3 + k, colour, :, 15, :]

        def pack(step, pops, rows, cells, packed):
            nz_out[step, 0] = pack_faces(pops, rows, packed[0])
            nz_out[step, 1] = pack_classes(pops, cells, packed[1])

        def send_faces(step, pops, rows):
            edge_rows(step)
            copies = face_copies(step, pops, rows)
            for copy in copies:
                copy.start()

        def stream_in(step, pops, rows, mass_rows, cells):
            wait_rows(recv_sem.at[2 * step], FACE_ROWS + POP_ROWS * len(rows))
            stream(step, pops, rows, range(15))
            for k in mass_rows:
                mass_part(k)
            for x in cells:
                side_part(pops, x)
            wait_rows(recv_sem.at[2 * step + 1], CORNER_ROWS)
            stream(step, pops, rows, range(15, 19))
            for k in mass_rows:
                mass_rest(k)
            phase_rows(step)

        def stream(step, pops, rows, directions):
            for colour in range(2):
                for i in directions:
                    shift_y, shift_z = VELOCITY_TABLE[i][1:]
                    span = slice(8 - shift_y, 24 - shift_y)
                    for row in rows:
                        value = pops[colour, i, row, span, :]
                        if shift_z == 1:
                            place = lane_of(PLUS_Z, i, colour, row)
                            edge = nz_left[step, 0, span, :]
                            if place:
                                edge = pltpu.roll(edge, CZ - place, 1)
                            value = jnp.where(lane == 0, edge, pltpu.roll(value, 1, 1))
                        elif shift_z == -1:
                            place = lane_of(MINUS_Z, i, colour, row)
                            edge = pltpu.roll(nz_right[step, 0, span, :], CZ - 1 - place, 1)
                            value = jnp.where(lane == CZ - 1, edge, pltpu.roll(value, CZ - 1, 1))
                        moved[colour, i, row] = value


        def read(colour, i, x):
            return read_moved(moved, colour, i, x)

        def mass_part(k):
            for colour in range(2):
                masses[colour, k] = part_sum(range(15), lambda i: read(colour, i, k - 1))

        def mass_rest(k):
            red, blue = (
                masses[colour, k]
                + part_sum(range(15, 19), lambda i: read(colour, i, k - 1))
                for colour in range(2)
            )
            masses[0, k] = red
            masses[1, k] = blue
            phase_buf[k, 8:24, :] = (red - blue) / (red + blue)

        def side_part(pops, x):
            for colour in range(2):

                def shifted(i):
                    shift_x, shift_y = VELOCITY_TABLE[i][0:2]
                    row = clip_row(x - shift_x)
                    return pops[colour, i, row, 8 - shift_y : 24 - shift_y, :]

                low = pltpu.roll(part_sum(MINUS_Z, shifted), CZ - 1, 1)
                high = pltpu.roll(part_sum(PLUS_Z, shifted), 1, 1)
                own_side[colour, x] = jnp.where(lane == CZ - 1, low, high)

        def phase_rows(step):
            for side, place in ((0, 7), (1, 24)):
                part = [row_sums_in[step, side, k] + own_sums[step, k, side] for k in range(3)]
                corner = [
                    row_corners_in[step, side, k] + own_sums_in[step, k, side] for k in range(2)
                ]
                edge_lane = lax.broadcasted_iota(jnp.int32, (16, CZ), 1)
                total = (
                    part[0]
                    + pltpu.roll(jnp.where(edge_lane == CZ - 1, corner[0], part[1]), 1, 1)
                    + pltpu.roll(jnp.where(edge_lane == 0, corner[1], part[2]), CZ - 1, 1)
                )
                red = total[0:8]
                blue = total[8:16]
                phase_buf[1 : 1 + LX, place, :] = ((red - blue) / (red + blue))[0:LX]
        def collide(step, pops, first, last):
            beside = None
            for k, span in enumerate((slice(8, 24), slice(7, 23), slice(9, 25))):
                both = jnp.where(
                    (lane & 3) < 2, nz_left[step, 1, span, :], nz_right[step, 1, span, :]
                )
                beside = both if k == 0 else beside + pltpu.roll(both, CZ - 40 * k, 1)
            beside = beside + jnp.where(
                (lane & 3) < 2, pltpu.roll(beside, 1, 1), pltpu.roll(beside, CZ - 1, 1)
            )

            def side_mass(colour, x):
                far = pltpu.roll(beside, CZ - 2 - 4 * (5 * colour + x), 1)
                return far + own_side[colour, x]

            def slope_step(x):
                here = phase_buf[x + 1, 8:24, :]
                side_red = side_mass(0, x)
                side_blue = side_mass(1, x)
                side = (side_red - side_blue) / (side_red + side_blue)
                low_z = pltpu.roll(jnp.where(lane == CZ - 1, side, here), 1, 1)
                high_z = pltpu.roll(jnp.where(lane == 0, side, here), CZ - 1, 1)
                grad = [
                    0.5 * (phase_buf[x + 2, 8:24, :] - phase_buf[x, 8:24, :]),
                    0.5 * (phase_buf[x + 1, 9:25, :] - phase_buf[x + 1, 7:23, :]),
                    0.5 * (high_z - low_z),
                ]
                for dim in range(3):
                    slopes[dim, x] = grad[dim]

            for x in range(first, last):
                slope_step(x)
            for x in range(first, last if step < 3 else first):

                def write(colour, i, value, x=x):
                    if step < 2:
                        pops_1[colour, i, x, 8:24, :] = value
                    else:
                        out_ref[(19 * colour + i) * LX + x] = value

                ready = relaxed if step == 1 and x == LX - 2 else None
                collide_cells(x, moved, masses, slopes, solid_ref, write, ready)

        empty = (jnp.zeros((CY, CZ), F32), jnp.zeros((CY, CZ), F32))
        nozzle_loads[1].wait()
        solid_load.wait()
        pack(0, pops_0, range(LX), range(LX - 1), empty)
        send_faces(0, pops_0, slice(0, LX))
        inflow = take_inflow()
        outflow = equilibrium_list(jnp.exp(inflow[0]), inflow[1:])
        for i in range(19):
            ghost_eq[i] = 0.5 * outflow[i]
        ghost_row(pops_0, prof[:, 3 * CZ :])
        pack(1, pops_0, (LX,), (LX - 1,), nz_out[0])
        send_faces(1, pops_0, slice(LX, LX + 1))
        stream_in(0, pops_0, range(LX), range(LX), range(LX - 2))
        collide(0, pops_0, 0, LX - 2)
        pack(2, pops_1, range(LX - 2), range(LX - 3), empty)
        send_faces(2, pops_1, slice(0, LX - 2))
        relax_cells(LX - 2, moved, masses, relaxed)
        stream_in(1, pops_0, (LX,), range(LX, LX + 2), range(LX - 2, LX))
        collide(1, pops_0, LX - 2, LX)
        red_last = weighted_sum([pops_1[0, i, LX - 1, 8:24, :] for i in range(19)])
        blue_last = weighted_sum([pops_1[1, i, LX - 1, 8:24, :] for i in range(19)])
        ghost_row(pops_1, (red_last - blue_last) / (red_last + blue_last))
        pack(3, pops_1, range(LX - 2, LX + 1), range(LX - 3, LX), nz_out[2])
        send_faces(3, pops_1, slice(LX - 2, LX + 1))
        stream_in(2, pops_1, range(LX - 2), range(LX - 2), range(LX - 4))
        collide(2, pops_1, 0, LX - 4)
        relax_cells(LX - 4, moved, masses, relaxed)
        stream_in(3, pops_1, range(LX - 2, LX + 1), range(LX - 2, LX + 2), range(LX - 4, LX))
        collide(3, pops_1, LX - 4, LX)
        wait_rows(send_sem.at[0], ROUTE_ROWS + NOZZLE_ROWS)


def finish(done_ref, moved, masses, slopes, relaxed, solid_ref, out_ref, stage, sems):
    is_nozzle = lax.axis_index("solver") == 0

    @pl.when(jnp.logical_not(is_nozzle))
    def _():
        copy = pltpu.make_async_copy(done_ref, out_ref, sems.at[0])
        copy.start()
        copy.wait()

    @pl.when(is_nozzle)
    def _():
        done_pops = done_ref.reshape(2 * 19, LX, CY, CZ)
        out_pops = out_ref.reshape(2 * 19, LX, CY, CZ)
        copies = []
        for x in range(LX):
            row = slice(x, x + 1)

            def write(colour, i, value, x=x):
                stage[19 * colour + i, x] = value

            if x >= LX - 4:
                ready = relaxed if x == LX - 4 else None
                collide_cells(x, moved, masses, slopes, solid_ref, write, ready)
            source = stage if x >= LX - 4 else done_pops
            copies.append(
                pltpu.make_async_copy(
                    source.at[:, row, :, :], out_pops.at[:, row, :, :], sems.at[x]
                )
            )
            copies[-1].start()
        for copy in copies:
            copy.wait()


def on_device(coupled_state, solid_mask, inlet_source):
    words = coupled_state.shape[1]
    vmem = lambda *shape: pltpu.VMEM(shape, F32)
    in_hbm = lambda array: pltpu.with_memory_space_constraint(array, pltpu.HBM)
    dma = lambda *shape: pltpu.SemaphoreType.DMA(shape)
    done = pl.pallas_call(
        kernel,
        out_shape=[
            vmem(words, CY, CZ),
            vmem(2, 19, LX + 1, CY, CZ),
            vmem(2, LX + 2, CY, CZ),
            vmem(3, LX, CY, CZ),
            vmem(19, CY, CZ),
            pltpu.VMEM((LX, CY, CZ), jnp.int32),
        ],
        in_specs=[
            pl.BlockSpec(memory_space=pltpu.HBM),
            pl.BlockSpec(memory_space=pltpu.HBM),
            pl.BlockSpec(memory_space=pltpu.HBM),
            pl.BlockSpec(memory_space=pltpu.HBM),
        ],
        out_specs=[pl.BlockSpec(memory_space=pltpu.VMEM)] * 6,
        scratch_shapes=[
            pltpu.VMEM((1, 256), jnp.int32),
            pltpu.VMEM((512, 256), jnp.bfloat16),
            vmem(CY, 4 * CZ),
            vmem(N_GY, 8, CZ),
            vmem(N_GY, 8, CZ),
            vmem(5, FX + 4, 32, CZ),
            vmem(5, FX + 4, 32, CZ),
            vmem(2, N_GROUPS, CY, CZ),
            vmem(2, N_GROUPS, CY, CZ),
            vmem(2, N_GROUPS, CY, CZ),
            vmem(2, 19, LX + 1, 32, CZ),
            vmem(2, 19, LX + 1, 32, CZ),
            vmem(LX + 2, 32, CZ),
            vmem(19, CY, CZ),
            vmem(2, LX, CY, CZ),
            vmem(9, 2, 8, CY, CZ),
            vmem(4, 2, CY, CZ),
            vmem(4, 2, 32, CZ),
            vmem(4, 2, 32, CZ),
            vmem(4, 2, 3, 16, CZ),
            vmem(4, 3, 2, 16, CZ),
            vmem(4, 2, 3, 16, CZ),
            vmem(4, 2, 2, 16, CZ),
            vmem(4, 2, 2, 16, CZ),
            vmem(MOST_ROWS, CZ),
            dma(4),
            dma(1),
            dma(1),
            dma(8),
        ],
        compiler_params=pltpu.CompilerParams(
            collective_id=0, has_side_effects=True, vmem_limit_bytes=28 << 20
        ),
    )(
        in_hbm(coupled_state.reshape(5, FX, CY, CZ)),
        in_hbm(coupled_state.reshape(2, 19, LX, CY, CZ)),
        in_hbm(solid_mask.reshape(LX, CY, CZ)),
        in_hbm(inlet_source),
    )
    out = pl.pallas_call(
        finish,
        out_shape=pltpu.HBM((words, CY, CZ), F32),
        in_specs=[pl.BlockSpec(memory_space=pltpu.VMEM)] * 6,
        out_specs=pl.BlockSpec(memory_space=pl.ANY),
        scratch_shapes=[vmem(2 * 19, LX, CY, CZ), dma(LX)],
        compiler_params=pltpu.CompilerParams(vmem_limit_bytes=8 << 20),
    )(*(pltpu.with_memory_space_constraint(array, pltpu.VMEM) for array in done))
    return out.reshape(coupled_state.shape)


def solution(mesh):
    return jax.shard_map(
        on_device,
        mesh=mesh,
        in_specs=(P("solver", None, "gy", "gz", None), P(None, "gy", "gz", None), P("gz", None)),
        out_specs=P("solver", None, "gy", "gz", None),
        check_vma=False,
    )
```

```python
import math

import jax
import jax.numpy as jnp
from jax import lax
from jax.experimental import pallas as pl
from jax.experimental.pallas import tpu as pltpu
from jax.sharding import PartitionSpec as P

CY = 16
CZ = 128
LX = 5
FX = 38
N_GY = 16
N_GZ = 8
MESH = pl.DeviceIdType.MESH
F32 = jnp.float32

VELOCITY_TABLE = [
    (0, 0, 0),
    (1, 0, 0),
    (-1, 0, 0),
    (0, 1, 0),
    (0, -1, 0),
    (0, 0, 1),
    (0, 0, -1),
    (1, 1, 0),
    (-1, -1, 0),
    (1, -1, 0),
    (-1, 1, 0),
    (1, 0, 1),
    (-1, 0, -1),
    (1, 0, -1),
    (-1, 0, 1),
    (0, 1, 1),
    (0, -1, -1),
    (0, 1, -1),
    (0, -1, 1),
]
OPPOSITE_TABLE = [0, 2, 1, 4, 3, 6, 5, 8, 7, 10, 9, 12, 11, 14, 13, 16, 15, 18, 17]
RELAX_TIME = 0.8
SURF_TENSION = 0.02
SEGREGATION_BETA = 0.7
GRAD_FLOOR = 0.1
TIME_STEP = 0.2
VISCOSITY = 0.05
DIFFUSION = 0.05
DENSITY_LOG = math.log(2.0)

PLUS_Z = [i for i in range(19) if VELOCITY_TABLE[i][2] == 1]
MINUS_Z = [i for i in range(19) if VELOCITY_TABLE[i][2] == -1]
PLUS_Y = [i for i in range(19) if VELOCITY_TABLE[i][1] == 1]
SIGNS = (0, 1, -1)
CLASSES = [
    [i for i in range(19) if VELOCITY_TABLE[i][1:] == (sy, sz)] for sy in SIGNS for sz in SIGNS
]
MINUS_Y = [i for i in range(19) if VELOCITY_TABLE[i][1] == -1]

GROUP = 6
N_GROUPS = 7
LAST_ROWS = FX - GROUP * (N_GROUPS - 1)
CHUNKS = (
    ((6, LAST_ROWS), (5, GROUP)),
    ((4, GROUP), (3, GROUP)),
    ((2, GROUP), (1, GROUP)),
    ((0, GROUP),),
)


ROUTE_ROWS = 8 * N_GY
PIPE_ROWS = 2 * (2 * 2 * 5 * FX + 2 * CY * N_GROUPS)
FACE_ROWS = 2 * 2 * CY + 2 * 3 * 16 + 2 * 2 * 16
CORNER_ROWS = 4 * 2 * 8 + 4 * 16
POP_ROWS = 2 * 5 * 2
NOZZLE_ROWS = 4 * (FACE_ROWS + CORNER_ROWS) + POP_ROWS * 2 * (LX + 1)
MOST_ROWS = ROUTE_ROWS + max(PIPE_ROWS, NOZZLE_ROWS)


def weighted_sum(values):
    faces = values[1]
    for i in range(2, 7):
        faces = faces + values[i]
    edges = values[7]
    for i in range(8, 19):
        edges = edges + values[i]
    return values[0] * (1.0 / 3.0) + faces * (1.0 / 18.0) + edges * (1.0 / 36.0)


def clip_row(row):
    return min(max(row, 0), LX) if isinstance(row, int) else jnp.clip(row, 0, LX)


def weight_of(i):
    return 1.0 / 3.0 if i == 0 else (1.0 / 18.0 if i < 7 else 1.0 / 36.0)


def part_sum(directions, read):
    total = None
    for weight in (1.0 / 3.0, 1.0 / 18.0, 1.0 / 36.0):
        values = [read(i) for i in directions if weight_of(i) == weight]
        if values:
            group = values[0]
            for value in values[1:]:
                group = group + value
            total = weight * group if total is None else total + weight * group
    return total


def weighted_momentum(values, dim):
    faces = None
    edges = None
    for i in range(1, 19):
        sign = VELOCITY_TABLE[i][dim]
        if sign == 0:
            continue
        if i < 7:
            faces = (
                values[i]
                if faces is None
                else (faces + values[i] if sign > 0 else faces - values[i])
            )
        else:
            edges = (
                values[i]
                if edges is None
                else (edges + values[i] if sign > 0 else edges - values[i])
            )
    return faces * (1.0 / 18.0) + edges * (1.0 / 36.0)


def along(direction, vec):
    total = None
    for sign, part in zip(VELOCITY_TABLE[direction], vec):
        if sign == 0:
            continue
        if total is None:
            total = part if sign > 0 else -part
        else:
            total = total + part if sign > 0 else total - part
    return total


def equilibrium_list(density, vec):
    speed_sq = vec[0] * vec[0] + vec[1] * vec[1] + vec[2] * vec[2]
    rest = density * (1.0 - 1.5 * speed_sq)
    out = [rest]
    for i in range(1, 19, 2):
        proj = along(i, vec)
        even = rest + (4.5 * density) * (proj * proj)
        odd = (3.0 * density) * proj
        out += [even + odd, even - odd]
    return out


def read_moved(moved, colour, i, x):
    return moved[colour, i, clip_row(x - VELOCITY_TABLE[i][0])]


def relax_cells(x, moved, masses, relaxed):
    for i, value in enumerate(relaxed_list(x, moved, masses)):
        relaxed[i] = value


def relaxed_list(x, moved, masses):
    total = masses[0, x + 1] + masses[1, x + 1]
    inverse = 1.0 / total
    mixed = [read_moved(moved, 0, i, x) + read_moved(moved, 1, i, x) for i in range(19)]
    vec = [weighted_momentum(mixed, dim) * inverse for dim in range(3)]
    balance = equilibrium_list(total, vec)
    return [m - (m - b) * (1.0 / RELAX_TIME) for m, b in zip(mixed, balance)]


def collide_cells(x, moved, masses, slopes, solid_ref, write, relaxed=None):
    def read(colour, i):
        return read_moved(moved, colour, i, x)

    red = masses[0, x + 1]
    blue = masses[1, x + 1]
    total = red + blue
    inverse = 1.0 / total
    if relaxed is None:
        settled = relaxed_list(x, moved, masses)
    else:
        settled = [relaxed[i] for i in range(19)]
    grad = [slopes[dim, x] for dim in range(3)]
    grad_sq = grad[0] * grad[0] + grad[1] * grad[1] + grad[2] * grad[2]
    inverse_norm = lax.rsqrt(grad_sq + GRAD_FLOOR * GRAD_FLOOR)
    red_part = red * inverse
    tension = SURF_TENSION * inverse_norm
    level = tension * grad_sq * (1.0 / 3.0)
    split = SEGREGATION_BETA * (red_part * blue) * inverse_norm
    solid = solid_ref[x] != 0
    for i in range(19):
        value = settled[i] - level
        if i:
            slope = along(i, grad)
            value = value + tension * (slope * slope)
            red_value = red_part * value + split * slope
        else:
            red_value = red_part * value
        back = OPPOSITE_TABLE[i]
        red_new = jnp.where(solid, read(0, back), red_value)
        blue_new = jnp.where(solid, read(1, back), value - red_value)
        write(0, i, red_new)
        write(1, i, blue_new)


def kernel(
    pipe_in,
    nozzle_in,
    solid_in,
    inlet_in,
    out_ref,
    moved,
    masses,
    slopes,
    relaxed,
    solid_ref,
    inlet_ref,
    band,
    prof,
    route_out,
    route_in,
    fields_0,
    fields_1,
    zpack,
    zleft,
    zright,
    pops_0,
    pops_1,
    phase_buf,
    ghost_eq,
    own_side,
    class_sums,
    nz_out,
    nz_left,
    nz_right,
    row_sums,
    own_sums,
    row_sums_in,
    row_corners_in,
    own_sums_in,
    tally,
    in_sem,
    send_sem,
    route_recv,
    recv_sem,
):
    solver = lax.axis_index("solver")
    gy = lax.axis_index("gy")
    gz = lax.axis_index("gz")
    other = 1 - solver
    up = lax.rem(gy + 1, N_GY)
    down = lax.rem(gy + N_GY - 1, N_GY)
    right = lax.rem(gz + 1, N_GZ)
    left = lax.rem(gz + N_GZ - 1, N_GZ)
    is_nozzle = solver == 0
    inlet_load = pltpu.make_async_copy(inlet_in, inlet_ref, in_sem.at[1])
    inlet_load.start()
    barrier = pltpu.get_barrier_semaphore()
    for device in (
        (solver, up, gz),
        (solver, down, gz),
        (solver, gy, right),
        (solver, gy, left),
        (solver, up, right),
        (solver, up, left),
        (solver, down, right),
        (solver, down, left),
    ):
        pl.semaphore_signal(barrier, inc=1, device_id=device, device_id_type=MESH)

    def greet(tile, carry):
        pl.semaphore_signal(barrier, inc=1, device_id=(other, tile, gz), device_id_type=MESH)
        return carry

    lax.fori_loop(0, N_GY, greet, 0)

    lane = lax.broadcasted_iota(jnp.int32, (CY, CZ), 1)

    def remote(src, dst, send_sem, recv_sem, device):
        return pltpu.make_async_remote_copy(
            src_ref=src,
            dst_ref=dst,
            send_sem=send_sem,
            recv_sem=recv_sem,
            device_id=device,
            device_id_type=MESH,
        )

    def wait_rows(sem, rows):
        part = tally.at[0:rows, :]
        pltpu.make_async_copy(part, part, sem).wait()

    solid_load = pltpu.make_async_copy(solid_in, solid_ref, in_sem.at[2])
    lane_word = lax.shift_right_logical(lane, 2)

    def pack_word(packed, value, word):
        return jnp.where(lane_word == word, pltpu.roll(value, (4 * word + 2) % CZ, 1), packed)

    def pack_first(group, count):
        packed = jnp.zeros((CY, CZ), F32)
        for row in range(count):
            for field in range(5):
                value = fields_0[field, 2 + GROUP * group + row, 8:24, :]
                packed = pack_word(packed, value, 5 * row + field)
        zpack[0, group] = packed

    def outlet_ghost(fields):
        for field in range(5):
            end = fields[field, 1 + FX, 8:24, :]
            fields[field, 2 + FX, 8:24, :] = end
            fields[field, 3 + FX, 8:24, :] = end

    nozzle_loads = [
        pltpu.make_async_copy(
            nozzle_in.at[:, :, rows, :, :], pops_0.at[:, :, rows, 8:24, :], in_sem.at[k]
        )
        for k, rows in ((0, slice(LX - 1, LX)), (3, slice(0, LX - 1)))
    ]
    pipe_loads = [
        pltpu.make_async_copy(
            pipe_in.at[part, rows, :, :],
            fields_0.at[part, slice(rows.start + 2, rows.stop + 2), 8:24, :],
            in_sem.at[k],
        )
        for k, part, rows in (
            (0, slice(1, 5), slice(0, 1)),
            (2, slice(0, 5), slice(1, FX)),
            (3, slice(0, 1), slice(0, 1)),
        )
    ]

    @pl.when(is_nozzle)
    def _():
        for copy in nozzle_loads:
            copy.start()
        solid_load.start()

    @pl.when(jnp.logical_not(is_nozzle))
    def _():
        for copy in pipe_loads:
            copy.start()

    inlet_load.wait()
    source = inlet_ref[...]
    row_ids = lax.broadcasted_iota(jnp.int32, (1, 256), 1)
    tile_rows = lax.broadcasted_iota(jnp.int32, (N_GY, 256), 0)
    source_tile = lax.shift_right_logical(source, 4)
    target_tile = lax.shift_right_logical(row_ids, 4)
    member = (tile_rows == source_tile).astype(jnp.bfloat16)
    first = lax.broadcasted_iota(jnp.int32, (256, 256), 0)
    second = lax.broadcasted_iota(jnp.int32, (256, 256), 1)
    before = (
        (first < second)
        & (lax.shift_right_logical(first, 4) == lax.shift_right_logical(second, 4))
    ).astype(jnp.bfloat16)
    counts = jnp.dot(member, before, preferred_element_type=F32)
    rank = jnp.sum(counts * member.astype(F32), axis=0, keepdims=True)
    far_tile = jnp.where(is_nozzle, target_tile, source_tile)
    local_row = jnp.where(is_nozzle, source, row_ids)
    mine = (local_row == tile_rows + gy * CY).astype(jnp.bfloat16)
    slot_rows = []
    row_slots = []
    for slot in range(2):
        taken = ((far_tile == tile_rows) & (rank == float(slot))).astype(jnp.bfloat16)
        dims = (((1,), (1,)), ((), ()))
        slot_rows.append(lax.dot_general(taken, mine, dims, preferred_element_type=F32))
        row_slots.append(lax.dot_general(mine, taken, dims, preferred_element_type=F32))

    @pl.when(is_nozzle)
    def _():
        nozzle_loads[0].wait()
        red = [pops_0[0, i, LX - 1, 8:24, :] for i in range(19)]
        blue = [pops_0[1, i, LX - 1, 8:24, :] for i in range(19)]
        red_mass = weighted_sum(red)
        blue_mass = weighted_sum(blue)
        inverse = 1.0 / (red_mass + blue_mass)
        mixed = [r + b for r, b in zip(red, blue)]
        for dim in range(3):
            prof[:, dim * CZ : (dim + 1) * CZ] = weighted_momentum(mixed, dim) * inverse
        prof[:, 3 * CZ :] = (red_mass - blue_mass) * inverse

    @pl.when(jnp.logical_not(is_nozzle))
    def _():
        pipe_loads[0].wait()
        for slot, field in enumerate((4, 1, 2, 3)):
            prof[:, slot * CZ : (slot + 1) * CZ] = fields_0[field, 2, 8:24, :]

    rows = prof[...]
    for slot in range(2):
        picked = jnp.dot(
            slot_rows[slot], rows, precision=lax.Precision.HIGHEST, preferred_element_type=F32
        )
        for part in range(4):
            route_out[:, slot * 4 + part, :] = picked[:, part * CZ : (part + 1) * CZ]

    pl.semaphore_wait(barrier, 8 + N_GY)

    def route(tile):
        return remote(
            route_out.at[tile],
            route_in.at[gy],
            send_sem.at[0],
            route_recv.at[0],
            (other, tile, gz),
        )

    def send_route(tile, carry):
        route(tile).start()
        return carry

    lax.fori_loop(0, N_GY, send_route, 0)

    def take_inflow():
        wait_rows(route_recv.at[0], ROUTE_ROWS)
        total = None
        for slot in range(2):
            arrived = jnp.concatenate(
                [route_in[:, slot * 4 + part, :] for part in range(4)], axis=1
            )
            term = jnp.dot(
                row_slots[slot],
                arrived,
                precision=lax.Precision.HIGHEST,
                preferred_element_type=F32,
            )
            total = term if total is None else total + term
        return [total[:, part * CZ : (part + 1) * CZ] for part in range(4)]

    @pl.when(jnp.logical_not(is_nozzle))
    def _():
        from_left = (lane & 3) < 2

        def group_copies(step, fields, group, count, kinds=range(4)):
            first_row = 2 + GROUP * group
            span = pl.ds(first_row, count)
            arrived = recv_sem.at[4 * step + (N_GROUPS - 1 - group) // 2]
            ends = [
                (fields.at[:, span, 22:24, :], fields.at[:, span, 6:8, :], (solver, up, gz)),
                (fields.at[:, span, 8:10, :], fields.at[:, span, 24:26, :], (solver, down, gz)),
                (zpack.at[step, group], zleft.at[step, group], (solver, gy, right)),
                (zpack.at[step, group], zright.at[step, group], (solver, gy, left)),
            ]
            return [
                remote(ends[k][0], ends[k][1], send_sem.at[0], arrived, ends[k][2]) for k in kinds
            ]

        def send_rows(group, count):
            for copy in group_copies(0, fields_0, group, count, (0, 1)):
                copy.start()

        def send_lanes(group, count):
            pack_first(group, count)
            for copy in group_copies(0, fields_0, group, count, (2, 3)):
                copy.start()

        def split(value):
            high = value.astype(jnp.bfloat16)
            return [high, (value - high.astype(F32)).astype(jnp.bfloat16)]

        def moved_row(fields, along_z, place):
            centre, grad, smooth = [], [], []
            for field in range(5):
                low_x = fields[field, place - 1, 8:24, :]
                high_x = fields[field, place + 1, 8:24, :]
                d_x = (fields[field, place - 2, 8:24, :] - fields[field, place + 2, 8:24, :]) + (
                    8.0 * (high_x - low_x)
                )
                low_y = fields[field, place, 7:23, :]
                high_y = fields[field, place, 9:25, :]
                d_y = (fields[field, place, 6:22, :] - fields[field, place, 10:26, :]) + (
                    8.0 * (high_y - low_y)
                )
                d_z = along_z[field][:, 0:CZ]
                centre.append(fields[field, place, 8:24, :])
                grad.append((d_x, d_y, d_z))
                smooth.append(low_x + high_x + low_y + high_y + along_z[field][:, CZ:])
            scale = TIME_STEP / 12.0
            speed = [scale * centre[k] for k in (1, 2, 3)]
            lift = scale * jnp.exp((1.0 - centre[0]) * DENSITY_LOG)
            spread = TIME_STEP * DIFFUSION
            out = []
            for field in range(4):
                rate = (
                    speed[0] * grad[field][0]
                    + speed[1] * grad[field][1]
                    + speed[2] * grad[field][2]
                )
                if field > 0:
                    rate = rate + lift * grad[4][field - 1]
                out.append((1.0 - 6.0 * spread) * centre[field] + spread * smooth[field] - rate)
            rate = scale * (grad[1][0] + grad[2][1] + grad[3][2])
            out.append((1.0 - 6.0 * spread) * centre[4] + spread * smooth[4] - rate)
            return out

        def run_chunk(step, fields, groups):
            wait_rows(
                recv_sem.at[4 * step + (N_GROUPS - 1 - groups[0][0]) // 2],
                sum(2 * 2 * 5 * count + 2 * CY for _, count in groups),
            )
            lanes_in = []
            for group, count in groups:
                halo = jnp.where(from_left, zleft[step, group], zright[step, group])
                for row in range(count):
                    for field in range(5):
                        here = fields[field, 2 + GROUP * group + row, 8:24, :]
                        edge = pltpu.roll(halo, (-(4 * (5 * row + field) + 2)) % CZ, 1)
                        lanes_in.append(jnp.concatenate(split(here) + split(edge), axis=1))
            lanes_out = jnp.dot(
                jnp.concatenate(lanes_in, axis=0), band[...], preferred_element_type=F32
            )
            done = 0
            for group, count in groups:
                packed = jnp.zeros((CY, CZ), F32)
                for row in range(count):
                    along_z = [lanes_out[(done + k) * CY : (done + k + 1) * CY] for k in range(5)]
                    done += 5
                    place = GROUP * group + row
                    values = moved_row(fields, along_z, 2 + place)
                    for field in range(5):
                        if step == 0:
                            fields_1[field, 2 + place, 8:24, :] = values[field]
                            packed = pack_word(packed, values[field], 5 * row + field)
                        else:
                            out_ref[field * FX + place] = 0.5 * (
                                fields_0[field, 2 + place, 8:24, :] + values[field]
                            )
                if step == 0:
                    zpack[1, group] = packed
                    for copy in group_copies(1, fields_1, group, count):
                        copy.start()

        for copy in pipe_loads[1:]:
            copy.wait()
        send_rows(N_GROUPS - 1, LAST_ROWS)

        def send_step(k, carry):
            send_rows(N_GROUPS - 2 - k, GROUP)
            return carry

        lax.fori_loop(0, N_GROUPS - 1, send_step, 0)
        send_lanes(N_GROUPS - 1, LAST_ROWS)

        def pack_step(k, carry):
            send_lanes(N_GROUPS - 2 - k, GROUP)
            return carry

        lax.fori_loop(0, N_GROUPS - 1, pack_step, 0)
        outlet_ghost(fields_0)
        lane_in = lax.broadcasted_iota(jnp.int32, (CZ, CZ), 0)
        lane_out = lax.broadcasted_iota(jnp.int32, (CZ, CZ), 1)
        ahead = lane_in - lane_out
        wrapped = jnp.where(
            ahead > 64, ahead - CZ, jnp.where(ahead < -64, ahead + CZ, jnp.zeros_like(ahead))
        )
        for part, apart in enumerate((ahead, wrapped)):
            near = (jnp.abs(apart) == 1).astype(F32)
            far = (jnp.abs(apart) == 2).astype(F32)
            slope = jnp.where(apart > 0, 8.0 * near - far, far - 8.0 * near)
            for copy in range(2):
                rows = slice((2 * part + copy) * CZ, (2 * part + copy + 1) * CZ)
                band[rows, 0:CZ] = slope.astype(jnp.bfloat16)
                band[rows, CZ:] = near.astype(jnp.bfloat16)

        run_chunk(0, fields_0, ((6, LAST_ROWS), (5, GROUP)))
        outlet_ghost(fields_1)

        def first_step(k, carry):
            run_chunk(0, fields_0, ((4 - 2 * k, GROUP), (3 - 2 * k, GROUP)))
            return carry

        lax.fori_loop(0, 2, first_step, 0)
        inflow = take_inflow()
        ghost = [0.5 * (1.0 + inflow[3]), inflow[0], inflow[1], inflow[2]]
        for place in range(2):
            for field in range(4):
                fields_0[field, place, 8:24, :] = ghost[field]
                fields_1[field, place, 8:24, :] = ghost[field]
            fields_0[4, place, 8:24, :] = fields_0[4, 2, 8:24, :]
        run_chunk(0, fields_0, ((0, GROUP),))
        for place in range(2):
            fields_1[4, place, 8:24, :] = fields_1[4, 2, 8:24, :]
        run_chunk(1, fields_1, ((6, LAST_ROWS), (5, GROUP)))

        def second_step(k, carry):
            run_chunk(1, fields_1, ((4 - 2 * k, GROUP), (3 - 2 * k, GROUP)))
            return carry

        lax.fori_loop(0, 2, second_step, 0)
        run_chunk(1, fields_1, ((0, GROUP),))

        wait_rows(send_sem.at[0], ROUTE_ROWS + PIPE_ROWS)

    @pl.when(is_nozzle)
    def _():
        def face_copies(step, pops, rows):
            copies = []

            def add(src, dst, device, kind=0):
                arrived = recv_sem.at[2 * step + kind]
                copies.append(remote(src, dst, send_sem.at[0], arrived, device))

            low, high = slice(0, 8), slice(8, 16)
            for k, column, edges in ((0, right, nz_left), (1, left, nz_right)):
                for side, row, part, place in ((0, up, high, 0), (1, down, low, 24)):
                    add(
                        nz_out.at[step, :, part, :],
                        edges.at[step, :, place : place + 8, :],
                        (solver, row, column),
                        1,
                    )
                    add(
                        row_sums.at[step, side, 1 + k],
                        row_corners_in.at[step, side, k],
                        (solver, row, column),
                        1,
                    )
            for i in PLUS_Y:
                add(pops.at[:, i, rows, 23:24, :], pops.at[:, i, rows, 7:8, :], (solver, up, gz))
            for i in MINUS_Y:
                add(pops.at[:, i, rows, 8:9, :], pops.at[:, i, rows, 24:25, :], (solver, down, gz))
            add(row_sums.at[step, 0], row_sums_in.at[step, 0], (solver, up, gz))
            add(row_sums.at[step, 1], row_sums_in.at[step, 1], (solver, down, gz))
            for k, column, edges in ((0, right, nz_left), (1, left, nz_right)):
                add(nz_out.at[step], edges.at[step, :, 8:24, :], (solver, gy, column))
                add(own_sums.at[step, 1 + k], own_sums_in.at[step, k], (solver, gy, column))
            return copies

        def lane_of(directions, i, colour, row):
            return 2 * ((directions.index(i) * 2 + colour) * 6 + row) + (directions is MINUS_Z)

        def ghost_row(pops, phase_last):
            for i in range(19):
                pops[0, i, LX, 8:24, :] = (1.0 + phase_last) * ghost_eq[i]
                pops[1, i, LX, 8:24, :] = (1.0 - phase_last) * ghost_eq[i]

        def pack_faces(pops, rows, packed):
            lane_pair = lax.shift_right_logical(lane, 1)
            for row in rows:
                for colour in range(2):
                    for k in range(5):
                        pair = (k * 2 + colour) * 6 + row
                        value = jnp.where(
                            lane < CZ // 2,
                            pops[colour, MINUS_Z[k], row, 8:24, :],
                            pops[colour, PLUS_Z[k], row, 8:24, :],
                        )
                        value = pltpu.roll(value, 2 * pair + 1, 1)
                        packed = jnp.where(lane_pair == pair, value, packed)
            return packed

        def pack_classes(pops, cells, packed):
            for x in cells:
                for colour in range(2):
                    sums = []
                    for k, directions in enumerate(CLASSES):
                        value = part_sum(
                            directions,
                            lambda i: pops[
                                colour, i, min(max(x - VELOCITY_TABLE[i][0], 0), LX), 8:24, :
                            ],
                        )
                        class_sums[k, colour, x] = value
                        sums.append(value)
                    for k in range(3):
                        word = 10 * k + 5 * colour + x
                        value = jnp.where(
                            lane == 126,
                            sums[3 * k + 1],
                            jnp.where(lane == 1, sums[3 * k + 2], sums[3 * k]),
                        )
                        value = pltpu.roll(value, 4 * word + 2, 1)
                        packed = jnp.where(lane_word == word, value, packed)
            return packed

        def edge_rows(step):
            for colour in range(2):
                span = slice(8 * colour, 8 * colour + 8)
                for k in range(3):
                    row_sums[step, 0, k, span, :] = (
                        class_sums[k, colour, :, 15, :] + class_sums[3 + k, colour, :, 14, :]
                    )
                    row_sums[step, 1, k, span, :] = (
                        class_sums[k, colour, :, 0, :] + class_sums[6 + k, colour, :, 1, :]
                    )
                    own_sums[step, k, 0, span, :] = class_sums[6 + k, colour, :, 0, :]
                    own_sums[step, k, 1, span, :] = class_sums[3 + k, colour, :, 15, :]

        def pack(step, pops, rows, cells, packed):
            nz_out[step, 0] = pack_faces(pops, rows, packed[0])
            nz_out[step, 1] = pack_classes(pops, cells, packed[1])

        def send_faces(step, pops, rows):
            edge_rows(step)
            copies = face_copies(step, pops, rows)
            for copy in copies:
                copy.start()

        def stream_in(step, pops, rows, mass_rows, cells):
            wait_rows(recv_sem.at[2 * step], FACE_ROWS + POP_ROWS * len(rows))
            stream(step, pops, rows, range(15))
            for k in mass_rows:
                mass_part(k)
            for x in cells:
                side_part(pops, x)
            wait_rows(recv_sem.at[2 * step + 1], CORNER_ROWS)
            stream(step, pops, rows, range(15, 19))
            for k in mass_rows:
                mass_rest(k)
            phase_rows(step)

        def stream(step, pops, rows, directions):
            for colour in range(2):
                for i in directions:
                    shift_y, shift_z = VELOCITY_TABLE[i][1:]
                    span = slice(8 - shift_y, 24 - shift_y)
                    for row in rows:
                        value = pops[colour, i, row, span, :]
                        if shift_z == 1:
                            place = lane_of(PLUS_Z, i, colour, row)
                            edge = nz_left[step, 0, span, :]
                            if place:
                                edge = pltpu.roll(edge, CZ - place, 1)
                            value = jnp.where(lane == 0, edge, pltpu.roll(value, 1, 1))
                        elif shift_z == -1:
                            place = lane_of(MINUS_Z, i, colour, row)
                            edge = pltpu.roll(nz_right[step, 0, span, :], CZ - 1 - place, 1)
                            value = jnp.where(lane == CZ - 1, edge, pltpu.roll(value, CZ - 1, 1))
                        moved[colour, i, row] = value


        def read(colour, i, x):
            return read_moved(moved, colour, i, x)

        def mass_part(k):
            for colour in range(2):
                masses[colour, k] = part_sum(range(15), lambda i: read(colour, i, k - 1))

        def mass_rest(k):
            red, blue = (
                masses[colour, k]
                + part_sum(range(15, 19), lambda i: read(colour, i, k - 1))
                for colour in range(2)
            )
            masses[0, k] = red
            masses[1, k] = blue
            phase_buf[k, 8:24, :] = (red - blue) / (red + blue)

        def side_part(pops, x):
            for colour in range(2):

                def shifted(i):
                    shift_x, shift_y = VELOCITY_TABLE[i][0:2]
                    row = clip_row(x - shift_x)
                    return pops[colour, i, row, 8 - shift_y : 24 - shift_y, :]

                low = pltpu.roll(part_sum(MINUS_Z, shifted), CZ - 1, 1)
                high = pltpu.roll(part_sum(PLUS_Z, shifted), 1, 1)
                own_side[colour, x] = jnp.where(lane == CZ - 1, low, high)

        def phase_rows(step):
            for side, place in ((0, 7), (1, 24)):
                part = [row_sums_in[step, side, k] + own_sums[step, k, side] for k in range(3)]
                corner = [
                    row_corners_in[step, side, k] + own_sums_in[step, k, side] for k in range(2)
                ]
                edge_lane = lax.broadcasted_iota(jnp.int32, (16, CZ), 1)
                total = (
                    part[0]
                    + pltpu.roll(jnp.where(edge_lane == CZ - 1, corner[0], part[1]), 1, 1)
                    + pltpu.roll(jnp.where(edge_lane == 0, corner[1], part[2]), CZ - 1, 1)
                )
                red = total[0:8]
                blue = total[8:16]
                phase_buf[1 : 1 + LX, place, :] = ((red - blue) / (red + blue))[0:LX]
        def collide(step, pops, first, last):
            beside = None
            for k, span in enumerate((slice(8, 24), slice(7, 23), slice(9, 25))):
                both = jnp.where(
                    (lane & 3) < 2, nz_left[step, 1, span, :], nz_right[step, 1, span, :]
                )
                beside = both if k == 0 else beside + pltpu.roll(both, CZ - 40 * k, 1)
            beside = beside + jnp.where(
                (lane & 3) < 2, pltpu.roll(beside, 1, 1), pltpu.roll(beside, CZ - 1, 1)
            )

            def side_mass(colour, x):
                far = pltpu.roll(beside, CZ - 2 - 4 * (5 * colour + x), 1)
                return far + own_side[colour, x]

            def slope_step(x):
                here = phase_buf[x + 1, 8:24, :]
                side_red = side_mass(0, x)
                side_blue = side_mass(1, x)
                side = (side_red - side_blue) / (side_red + side_blue)
                low_z = pltpu.roll(jnp.where(lane == CZ - 1, side, here), 1, 1)
                high_z = pltpu.roll(jnp.where(lane == 0, side, here), CZ - 1, 1)
                grad = [
                    0.5 * (phase_buf[x + 2, 8:24, :] - phase_buf[x, 8:24, :]),
                    0.5 * (phase_buf[x + 1, 9:25, :] - phase_buf[x + 1, 7:23, :]),
                    0.5 * (high_z - low_z),
                ]
                for dim in range(3):
                    slopes[dim, x] = grad[dim]

            for x in range(first, last):
                slope_step(x)
            for x in range(first, last if step < 3 else first):

                def write(colour, i, value, x=x):
                    if step < 2:
                        pops_1[colour, i, x, 8:24, :] = value
                    else:
                        out_ref[(19 * colour + i) * LX + x] = value

                ready = relaxed if step == 1 and x == LX - 2 else None
                collide_cells(x, moved, masses, slopes, solid_ref, write, ready)

        empty = (jnp.zeros((CY, CZ), F32), jnp.zeros((CY, CZ), F32))
        nozzle_loads[1].wait()
        solid_load.wait()
        pack(0, pops_0, range(LX), range(LX - 1), empty)
        send_faces(0, pops_0, slice(0, LX))
        inflow = take_inflow()
        outflow = equilibrium_list(jnp.exp(inflow[0]), inflow[1:])
        for i in range(19):
            ghost_eq[i] = 0.5 * outflow[i]
        ghost_row(pops_0, prof[:, 3 * CZ :])
        pack(1, pops_0, (LX,), (LX - 1,), nz_out[0])
        send_faces(1, pops_0, slice(LX, LX + 1))
        stream_in(0, pops_0, range(LX), range(LX), range(LX - 2))
        collide(0, pops_0, 0, LX - 2)
        pack(2, pops_1, range(LX - 2), range(LX - 3), empty)
        send_faces(2, pops_1, slice(0, LX - 2))
        relax_cells(LX - 2, moved, masses, relaxed)
        stream_in(1, pops_0, (LX,), range(LX, LX + 2), range(LX - 2, LX))
        collide(1, pops_0, LX - 2, LX)
        red_last = weighted_sum([pops_1[0, i, LX - 1, 8:24, :] for i in range(19)])
        blue_last = weighted_sum([pops_1[1, i, LX - 1, 8:24, :] for i in range(19)])
        ghost_row(pops_1, (red_last - blue_last) / (red_last + blue_last))
        pack(3, pops_1, range(LX - 2, LX + 1), range(LX - 3, LX), nz_out[2])
        send_faces(3, pops_1, slice(LX - 2, LX + 1))
        stream_in(2, pops_1, range(LX - 2), range(LX - 2), range(LX - 4))
        collide(2, pops_1, 0, LX - 4)
        relax_cells(LX - 4, moved, masses, relaxed)
        stream_in(3, pops_1, range(LX - 2, LX + 1), range(LX - 2, LX + 2), range(LX - 4, LX))
        collide(3, pops_1, LX - 4, LX)
        wait_rows(send_sem.at[0], ROUTE_ROWS + NOZZLE_ROWS)


def finish(done_ref, moved, masses, slopes, relaxed, solid_ref, out_ref, stage, sems):
    is_nozzle = lax.axis_index("solver") == 0

    @pl.when(jnp.logical_not(is_nozzle))
    def _():
        copy = pltpu.make_async_copy(done_ref, out_ref, sems.at[0])
        copy.start()
        copy.wait()

    @pl.when(is_nozzle)
    def _():
        done_pops = done_ref.reshape(2 * 19, LX, CY, CZ)
        out_pops = out_ref.reshape(2 * 19, LX, CY, CZ)
        copies = []
        for x in range(LX):
            row = slice(x, x + 1)

            def write(colour, i, value, x=x):
                stage[19 * colour + i, x] = value

            if x >= LX - 4:
                ready = relaxed if x == LX - 4 else None
                collide_cells(x, moved, masses, slopes, solid_ref, write, ready)
            source = stage if x >= LX - 4 else done_pops
            copies.append(
                pltpu.make_async_copy(
                    source.at[:, row, :, :], out_pops.at[:, row, :, :], sems.at[x]
                )
            )
            copies[-1].start()
        for copy in copies:
            copy.wait()


def on_device(coupled_state, solid_mask, inlet_source):
    words = coupled_state.shape[1]
    vmem = lambda *shape: pltpu.VMEM(shape, F32)
    in_hbm = lambda array: pltpu.with_memory_space_constraint(array, pltpu.HBM)
    dma = lambda *shape: pltpu.SemaphoreType.DMA(shape)
    done = pl.pallas_call(
        kernel,
        out_shape=[
            vmem(words, CY, CZ),
            vmem(2, 19, LX + 1, CY, CZ),
            vmem(2, LX + 2, CY, CZ),
            vmem(3, LX, CY, CZ),
            vmem(19, CY, CZ),
            pltpu.VMEM((LX, CY, CZ), jnp.int32),
        ],
        in_specs=[
            pl.BlockSpec(memory_space=pltpu.HBM),
            pl.BlockSpec(memory_space=pltpu.HBM),
            pl.BlockSpec(memory_space=pltpu.HBM),
            pl.BlockSpec(memory_space=pltpu.HBM),
        ],
        out_specs=[pl.BlockSpec(memory_space=pltpu.VMEM)] * 6,
        scratch_shapes=[
            pltpu.VMEM((1, 256), jnp.int32),
            pltpu.VMEM((512, 256), jnp.bfloat16),
            vmem(CY, 4 * CZ),
            vmem(N_GY, 8, CZ),
            vmem(N_GY, 8, CZ),
            vmem(5, FX + 4, 32, CZ),
            vmem(5, FX + 4, 32, CZ),
            vmem(2, N_GROUPS, CY, CZ),
            vmem(2, N_GROUPS, CY, CZ),
            vmem(2, N_GROUPS, CY, CZ),
            vmem(2, 19, LX + 1, 32, CZ),
            vmem(2, 19, LX + 1, 32, CZ),
            vmem(LX + 2, 32, CZ),
            vmem(19, CY, CZ),
            vmem(2, LX, CY, CZ),
            vmem(9, 2, 8, CY, CZ),
            vmem(4, 2, CY, CZ),
            vmem(4, 2, 32, CZ),
            vmem(4, 2, 32, CZ),
            vmem(4, 2, 3, 16, CZ),
            vmem(4, 3, 2, 16, CZ),
            vmem(4, 2, 3, 16, CZ),
            vmem(4, 2, 2, 16, CZ),
            vmem(4, 2, 2, 16, CZ),
            vmem(MOST_ROWS, CZ),
            dma(4),
            dma(1),
            dma(1),
            dma(8),
        ],
        compiler_params=pltpu.CompilerParams(
            collective_id=0, has_side_effects=True, vmem_limit_bytes=28 << 20
        ),
    )(
        in_hbm(coupled_state.reshape(5, FX, CY, CZ)),
        in_hbm(coupled_state.reshape(2, 19, LX, CY, CZ)),
        in_hbm(solid_mask.reshape(LX, CY, CZ)),
        in_hbm(inlet_source),
    )
    out = pl.pallas_call(
        finish,
        out_shape=pltpu.HBM((words, CY, CZ), F32),
        in_specs=[pl.BlockSpec(memory_space=pltpu.VMEM)] * 6,
        out_specs=pl.BlockSpec(memory_space=pl.ANY),
        scratch_shapes=[vmem(2 * 19, LX, CY, CZ), dma(LX)],
        compiler_params=pltpu.CompilerParams(vmem_limit_bytes=8 << 20),
    )(*(pltpu.with_memory_space_constraint(array, pltpu.VMEM) for array in done))
    return out.reshape(coupled_state.shape)


def solution(mesh):
    return jax.shard_map(
        on_device,
        mesh=mesh,
        in_specs=(P("solver", None, "gy", "gz", None), P(None, "gy", "gz", None), P("gz", None)),
        out_specs=P("solver", None, "gy", "gz", None),
        check_vma=False,
    )
```
